32 devices in a mesh: seq: 4 (over y, core), fsdp: 8 (over z, x).
Axes of the slice: x: 2, y: 2, z: 4, core: 2. Of those that a mesh axis runs over, the one named last changes fastest.
Arguments:
- hidden_in: bfloat16 [8, 1024, 1024], P('fsdp', 'seq'), may hold values from -6 to 6
- memory: bfloat16 [8, 1024, 1024], P('fsdp', 'seq'), may hold values from -6 to 6
- lengths: int32 [8], P('fsdp'), may hold values from 256 to 1024, as said below
- out_grad: bfloat16 [8, 1024, 1024], P('fsdp', 'seq'), may hold values from -6 to 6
- self_in_weight: bfloat16 [1024, 3072], P('fsdp'), may hold values from -0.21875 to 0.21875
- self_query_bias: bfloat16 [1024], P('fsdp'), may hold values from -3 to 3
- self_value_bias: bfloat16 [1024], P('fsdp'), may hold values from -0.29882812 to 0.29882812
- self_out_weight: bfloat16 [1024, 1024], P('fsdp'), may hold values from -3 to 3
- self_out_bias: bfloat16 [1024], P('fsdp'), may hold values from -3 to 3
- cross_query_weight: bfloat16 [1024, 1024], P('fsdp'), may hold values from -0.21875 to 0.21875
- cross_query_bias: bfloat16 [1024], P('fsdp'), may hold values from -3 to 3
- memory_weight: bfloat16 [1024, 2048], P('fsdp'), may hold values from -0.21875 to 0.21875
- memory_value_bias: bfloat16 [1024], P('fsdp'), may hold values from -0.29882812 to 0.29882812
- cross_out_weight: bfloat16 [1024, 1024], P('fsdp'), may hold values from -3 to 3
- cross_out_bias: bfloat16 [1024], P('fsdp'), may hold values from -3 to 3
- ffn_in_weight: bfloat16 [1024, 4096], P('fsdp'), may hold values from -0.1875 to 0.1875
- ffn_in_bias: bfloat16 [4096], P('fsdp'), may hold values from -3 to 3
- ffn_out_weight: bfloat16 [4096, 1024], P('fsdp'), may hold values from -0.5 to 0.5
- ffn_out_bias: bfloat16 [1024], P('fsdp'), may hold values from -3 to 3
- norm_gain: bfloat16 [3, 1024], P(None, 'fsdp'), may hold values from 0.25 to 1.75
- norm_bias: bfloat16 [3, 1024], P(None, 'fsdp'), may hold values from -2 to 2
Outputs:
- layer_out: bfloat16 [8, 1024, 1024], P('fsdp', 'seq')
- input_grad: bfloat16 [8, 1024, 1024], P('fsdp', 'seq')
- memory_grad: bfloat16 [8, 1024, 1024], P('fsdp', 'seq')
- grad_self_in: float32 [1024, 3072], P('fsdp')
- grad_self_query_bias: float32 [1024], P('fsdp')
- grad_self_value_bias: float32 [1024], P('fsdp')
- grad_self_out: float32 [1024, 1024], P('fsdp')
- grad_self_out_bias: float32 [1024], P('fsdp')
- grad_cross_query: float32 [1024, 1024], P('fsdp')
- grad_cross_query_bias: float32 [1024], P('fsdp')
- grad_memory_weight: float32 [1024, 2048], P('fsdp')
- grad_memory_value_bias: float32 [1024], P('fsdp')
- grad_cross_out: float32 [1024, 1024], P('fsdp')
- grad_cross_out_bias: float32 [1024], P('fsdp')
- grad_ffn_in: float32 [1024, 4096], P('fsdp')
- grad_ffn_in_bias: float32 [4096], P('fsdp')
- grad_ffn_out: float32 [4096, 1024], P('fsdp')
- grad_ffn_out_bias: float32 [1024], P('fsdp')
- grad_norm_gain: float32 [3, 1024], P(None, 'fsdp')
- grad_norm_bias: float32 [3, 1024], P(None, 'fsdp')
The draws below stay inside these ranges and needn't reach their ends.
Inputs may be any that keep to these rules, and one draw needn't show every extreme that they name: `lengths`: keys at positions at or beyond a sequence's length are masked; some sequence is full.
All inputs are finite; a program needn't handle non-finite values.
Results may differ from the reference program's by a relative error of at most 0.03.
Values may be sent and summed in bfloat16 or wider, within the bound.
No kernel may reach another device: no remote copies, remote signals or barrier semaphores. Data moves between devices by JAX's collectives and lax.ppermute only.
A program may use at most 192 MiB of HBM per device.

```python
import jax
import jax.numpy as jnp
from jax import lax

D = 1024
HD = 64
FF = 4096
BLK = 256
LEN = 1024
MEM = 1024
BATCH = 8


def draw_lengths(key, part):
    values = jax.random.randint(key, (BATCH,), LEN // 4, LEN + 1)
    return values.at[0].set(LEN).astype(jnp.int32)


def shard_levels(own_key, dims, pieces, smallest, top_value):
    def one(dim, shards_of):
        draws = jax.random.uniform(jax.random.fold_in(jax.random.fold_in(own_key, 6), dim), (shards_of,), jnp.float32, smallest / len(pieces), top_value / len(pieces))
        return jnp.repeat(jnp.exp(draws), dims[dim] // shards_of).reshape((-1,) + (1,) * (len(dims) - dim - 1))

    loudness = one(*pieces[0])
    for cut in pieces[1:]:
        loudness = loudness * one(*cut)
    return loudness


def gaussian(key, dims, scale, reach, split=(), held_as=jnp.bfloat16):
    gain = shard_levels(key, dims, split, -0.22, 0.18) if split else 1.0
    values = jax.random.normal(key, dims, jnp.float32) * scale * gain
    return jnp.minimum(jnp.maximum(values, -reach), reach).astype(held_as)


def setup_inputs(seed: int = 0) -> dict:
    streams_of = jax.random.split(jax.random.key(seed), 22)
    hidden_in = gaussian(streams_of[0], (BATCH, LEN, D), 1.0, 6.0, ((0, 8), (1, 4)))
    memory = gaussian(streams_of[1], (BATCH, MEM, D), 1.0, 6.0, ((0, 8), (1, 4)))
    lengths = draw_lengths(jax.random.fold_in(streams_of[21], 71), 0)
    out_grad = gaussian(streams_of[3], (BATCH, LEN, D), 1.0, 6.0, ((0, 8), (1, 4)))
    self_in_weight = gaussian(streams_of[4], (D, 3 * D), (D * 2 // 3) ** -0.5, 0.21875, ((0, 8),))
    self_query_bias = gaussian(streams_of[5], (D,), 0.5, 3.0, ((0, 8),))
    self_value_bias = gaussian(streams_of[6], (D,), 0.05, 0.29882812, ((0, 8),))
    self_out_weight = gaussian(streams_of[7], (D, D), 0.5, 3.0, ((0, 8),))
    self_out_bias = gaussian(streams_of[8], (D,), 0.5, 3.0, ((0, 8),))
    cross_query_weight = gaussian(streams_of[9], (D, D), (D * 2 // 3) ** -0.5, 0.21875, ((0, 8),))
    cross_query_bias = gaussian(streams_of[10], (D,), 0.5, 3.0, ((0, 8),))
    memory_weight = gaussian(streams_of[11], (D, 2 * D), (D * 2 // 3) ** -0.5, 0.21875, ((0, 8),))
    memory_value_bias = gaussian(streams_of[12], (D,), 0.05, 0.29882812, ((0, 8),))
    cross_out_weight = gaussian(streams_of[13], (D, D), 0.5, 3.0, ((0, 8),))
    cross_out_bias = gaussian(streams_of[14], (D,), 0.5, 3.0, ((0, 8),))
    ffn_in_weight = gaussian(streams_of[15], (D, FF), D ** -0.5, 0.1875, ((0, 8),))
    ffn_in_bias = gaussian(streams_of[16], (FF,), 0.5, 3.0, ((0, 8),))
    ffn_out_weight = gaussian(streams_of[17], (FF, D), (FF // 32) ** -0.5, 0.5, ((0, 8),))
    ffn_out_bias = gaussian(streams_of[18], (D,), 0.5, 3.0, ((0, 8),))
    norm_gain = jnp.clip(1.0 + 0.15 * jax.random.normal(streams_of[19], (3, D), jnp.float32), 0.25, 1.75).astype(jnp.bfloat16)
    norm_bias = gaussian(streams_of[20], (3, D), 0.3, 2.0, ((1, 8),))
    return dict(hidden_in=hidden_in, memory=memory, lengths=lengths, out_grad=out_grad, self_in_weight=self_in_weight, self_query_bias=self_query_bias, self_value_bias=self_value_bias, self_out_weight=self_out_weight, self_out_bias=self_out_bias, cross_query_weight=cross_query_weight, cross_query_bias=cross_query_bias, memory_weight=memory_weight, memory_value_bias=memory_value_bias, cross_out_weight=cross_out_weight, cross_out_bias=cross_out_bias, ffn_in_weight=ffn_in_weight, ffn_in_bias=ffn_in_bias, ffn_out_weight=ffn_out_weight, ffn_out_bias=ffn_out_bias, norm_gain=norm_gain, norm_bias=norm_bias)


@jax.custom_vjp
def low(v):
    return lax.optimization_barrier(v.astype(jnp.bfloat16)).astype(jnp.float32)

@jax.custom_vjp
def low_back(v):
    return v

def low_keep(v):
    return (low(v), None)

def low_pass(kept, grad):
    return (grad,)

def back_keep(v):
    return (v, None)

def back_low(kept, grad):
    return (low(grad),)
low.defvjp(low_keep, low_pass)
low_back.defvjp(back_keep, back_low)
alpha_scale = 300.0 ** 0.25
layer_eps = 1e-05
score_scale = 0.125
masked_value = -1e+30
gelu_coef = 0.7978845608028654
gelu_cube = 0.044715

def matmul(left, right):
    return jnp.dot(left, right, precision=lax.Precision.HIGHEST)

def gelu_tanh(values):
    return 0.5 * values * (1.0 + jnp.tanh(gelu_coef * (values + gelu_cube * values * values * values)))

def layer_norm(values, gain_row, shift_row):
    center = values - lax.optimization_barrier(jnp.mean(values, axis=-1, keepdims=True))
    variance = lax.optimization_barrier(jnp.mean(center * center, axis=-1, keepdims=True))
    return center * lax.rsqrt(variance + layer_eps) * gain_row + shift_row

def attention(queries, key_rows, value_rows, seq_length):
    total, width = queries.shape
    heads = width // HD
    query_heads = queries.reshape(total, heads, HD)
    key_heads = key_rows.reshape(key_rows.shape[0], heads, HD)
    value_heads = value_rows.reshape(value_rows.shape[0], heads, HD)
    qblock = min(512, total)
    key_pos = jnp.arange(key_rows.shape[0]).astype(jnp.int32)

    def one_block(block_index):
        first_row = (block_index * qblock).astype(jnp.int32)
        query_part = lax.dynamic_slice_in_dim(query_heads, first_row, qblock, 0)
        scores = jnp.einsum('qhd,khd->hqk', query_part, key_heads, precision=lax.Precision.HIGHEST) * score_scale
        if seq_length is not None:
            query_pos = first_row + jnp.arange(qblock).astype(jnp.int32)
            causal = key_pos[None, :] // BLK <= query_pos[:, None] // BLK
            allowed = causal & (key_pos[None, :] < seq_length)
            scores = jnp.where(allowed[None], scores, masked_value)
        scores = low_back(scores)
        weights_low = low(jax.nn.softmax(scores, axis=-1))
        return jnp.einsum('hqk,khd->qhd', weights_low, value_heads, precision=lax.Precision.HIGHEST)
    blocks = lax.map(jax.checkpoint(one_block), jnp.arange(total // qblock).astype(jnp.int32))
    return blocks.reshape(total, width)

def forward(params, hidden, mem_rows, seq_length):
    w_qkv, b_query, b_value, w_attn_out, b_attn_out, w_cross_q, b_cross_q, w_mem, b_mem_value, w_cross_out, b_cross_out, w_ffn_in, b_ffn_in, w_ffn_out, b_ffn_out, gain_all, shift_all = params
    width = hidden.shape[1]
    zeros_row = jnp.zeros((width,), jnp.float32)
    qkv = low_back(low(matmul(low(hidden), w_qkv) + jnp.concatenate([b_query, zeros_row, b_value])))
    attn = low_back(low(attention(qkv[:, :width], qkv[:, width:2 * width], qkv[:, 2 * width:], seq_length)))
    branch = low_back(matmul(attn, w_attn_out) + b_attn_out)
    first = layer_norm(alpha_scale * hidden + branch, gain_all[0], shift_all[0])
    cross_query = low_back(low(matmul(low(first), w_cross_q) + b_cross_q))
    kv_mem = low_back(low(matmul(low(mem_rows), w_mem) + jnp.concatenate([zeros_row, b_mem_value])))
    cross_attn = low_back(low(attention(cross_query, kv_mem[:, :width], kv_mem[:, width:], None)))
    cross_branch = low_back(matmul(cross_attn, w_cross_out) + b_cross_out)
    second = layer_norm(alpha_scale * first + cross_branch, gain_all[1], shift_all[1])
    pre_act = low_back(matmul(low(second), w_ffn_in) + b_ffn_in)
    hidden_act = low(gelu_tanh(pre_act))
    ffn_branch = low_back(matmul(hidden_act, w_ffn_out) + b_ffn_out)
    return layer_norm(alpha_scale * second + ffn_branch, gain_all[2], shift_all[2])

def reference(hidden_in, memory, lengths, out_grad, self_in_weight, self_query_bias, self_value_bias, self_out_weight, self_out_bias, cross_query_weight, cross_query_bias, memory_weight, memory_value_bias, cross_out_weight, cross_out_bias, ffn_in_weight, ffn_in_bias, ffn_out_weight, ffn_out_bias, norm_gain, norm_bias):
    params = tuple((item.astype(jnp.float32) for item in (self_in_weight, self_query_bias, self_value_bias, self_out_weight, self_out_bias, cross_query_weight, cross_query_bias, memory_weight, memory_value_bias, cross_out_weight, cross_out_bias, ffn_in_weight, ffn_in_bias, ffn_out_weight, ffn_out_bias, norm_gain, norm_bias)))

    def per_sequence(summed, items):
        hidden_seq, memory_seq, length_seq, grad_seq = items

        def local_forward(hidden_arg, memory_arg, param_arg):
            return forward(param_arg, hidden_arg, memory_arg, length_seq)
        result, pullback = jax.vjp(local_forward, hidden_seq.astype(jnp.float32), memory_seq.astype(jnp.float32), params)
        grad_hidden, grad_mem, grad_params = pullback(grad_seq.astype(jnp.float32))
        summed = jax.tree.map(jnp.add, summed, grad_params)
        return (summed, (result.astype(jnp.bfloat16), grad_hidden.astype(jnp.bfloat16), grad_mem.astype(jnp.bfloat16)))
    initial = jax.tree.map(jnp.zeros_like, params)
    grads, (layer_out, input_grad, memory_grad) = lax.scan(per_sequence, initial, (hidden_in, memory, lengths, out_grad))
    return (layer_out, input_grad, memory_grad, grads[0], grads[1], grads[2], grads[3], grads[4], grads[5], grads[6], grads[7], grads[8], grads[9], grads[10], grads[11], grads[12], grads[13], grads[14], grads[15], grads[16])
```

```python
import functools

import jax
import jax.numpy as jnp
from jax import lax
from jax.experimental import pallas as pl
from jax.experimental.pallas import tpu as pltpu
from jax.sharding import PartitionSpec as P

HD = 64
BLK = 256
CORES = 2

alpha_scale = 300.0**0.25
layer_eps = 1e-05
score_scale = 0.125
masked_value = -1e30
gelu_coef = 0.7978845608028654
gelu_cube = 0.044715

f32 = jnp.float32
bf16 = jnp.bfloat16
vmem_limit = 56 * 1024 * 1024


def dot(left, right, dims):
    return lax.dot_general(left, right, (dims, ((), ())), preferred_element_type=f32)


nn = ((1,), (0,))
nt = ((1,), (1,))
tn = ((0,), (0,))


def key_cases(total_keys, causal, block_index, visit):
    if not causal:
        visit(total_keys)
        return
    blocks = total_keys // BLK
    cases = min(4, blocks)
    for case in range(cases):
        low, high = case * blocks // cases, (case + 1) * blocks // cases

        @pl.when((block_index >= low) & (block_index < high))
        def _(high=high):
            visit(high * BLK)


def mask_scores(scores, first_key, limit):
    key_pos = first_key + lax.broadcasted_iota(jnp.int32, scores.shape, 0)
    return jnp.where(key_pos < limit, scores, masked_value)


def forward_kernel(causal, heads, chunk, len_ref, q_ref, k_ref, v_ref, o_ref, lse_ref):
    block_index = pl.program_id(1)
    total_keys = k_ref.shape[0]
    limit = jnp.minimum(len_ref[0], (block_index + 1) * BLK) if causal else 0
    rows = q_ref.shape[0]

    if total_keys <= chunk:

        def visit(key_count):
            outs, lses = [], []
            for h in range(heads):
                cols = slice(h * HD, (h + 1) * HD)
                query = q_ref[:, cols] * jnp.asarray(score_scale, bf16)
                scores = dot(k_ref[:key_count, cols], query, nt)
                if causal:
                    scores = mask_scores(scores, 0, limit)
                top = jnp.max(scores, axis=0, keepdims=True)
                weights = jnp.exp(scores - top)
                totals = jnp.sum(weights, axis=0, keepdims=True)
                low = (weights * (1.0 / totals)).astype(bf16)
                outs.append(dot(low, v_ref[:key_count, cols], tn).astype(bf16))
                lses.append(top + jnp.log(totals))
            o_ref[...] = outs[0] if heads == 1 else jnp.concatenate(outs, axis=1)
            lse_ref[0] = lses[0] if heads == 1 else jnp.concatenate(lses, axis=0)

        key_cases(total_keys, causal, block_index, visit)
    else:
        live = ((block_index + 1) * BLK + chunk - 1) // chunk if causal else total_keys // chunk
        outs, lses = [], []
        for h in range(heads):
            cols = slice(h * HD, (h + 1) * HD)
            query = q_ref[:, cols] * jnp.asarray(score_scale, bf16)

            def step(n, carry, cols=cols, query=query):
                top, totals, acc = carry
                span = pl.ds(pl.multiple_of(n * chunk, chunk), chunk)
                scores = dot(k_ref[span, cols], query, nt)
                if causal:
                    scores = mask_scores(scores, n * chunk, limit)
                new_top = jnp.maximum(top, jnp.max(scores, axis=0, keepdims=True))
                decay = jnp.exp(top - new_top)
                weights = jnp.exp(scores - new_top)
                totals = totals * decay + jnp.sum(weights, axis=0, keepdims=True)
                acc = acc * decay + dot(v_ref[span, cols], weights.astype(bf16), tn)
                return new_top, totals, acc

            start = (
                jnp.full((1, rows), masked_value, f32),
                jnp.zeros((1, rows), f32),
                jnp.zeros((HD, rows), f32),
            )
            top, totals, acc = lax.fori_loop(0, live, step, start)
            outs.append((acc / totals).T.astype(bf16))
            lses.append(top + jnp.log(totals))
        o_ref[...] = outs[0] if heads == 1 else jnp.concatenate(outs, axis=1)
        lse_ref[0] = lses[0] if heads == 1 else jnp.concatenate(lses, axis=0)


def backward_kernel(
    causal, heads, chunk, len_ref, q_ref, k_ref, v_ref, g_ref, lse_ref, dq_ref, dk_ref, dv_ref,
    dk_acc, dv_acc
):
    block_index = pl.program_id(1)
    total_keys = k_ref.shape[0]
    limit = jnp.minimum(len_ref[0], (block_index + 1) * BLK) if causal else 0

    @pl.when(block_index == 0)
    def _():
        dk_acc[...] = jnp.zeros_like(dk_acc)
        dv_acc[...] = jnp.zeros_like(dv_acc)

    def probabilities(query, span, cols, first_key, lse):
        scores = dot(k_ref[span, cols], query, nt)
        if causal:
            scores = mask_scores(scores, first_key, limit)
        return jnp.exp(scores - lse)

    if total_keys <= chunk:

        def visit(key_count):
            span = slice(0, key_count)
            dqs = []
            for h in range(heads):
                cols = slice(h * HD, (h + 1) * HD)
                query = q_ref[:, cols] * jnp.asarray(score_scale, bf16)
                grad = g_ref[:, cols]
                weights = probabilities(query, span, cols, 0, lse_ref[0, h : h + 1, :])
                dv_acc[h, span, :] += dot(weights.astype(bf16), grad, nn)
                grad_weights = dot(v_ref[span, cols], grad, nt)
                row_term = jnp.sum(grad_weights * weights, axis=0, keepdims=True)
                low = (weights * (grad_weights - row_term)).astype(bf16)
                dk_acc[h, span, :] += dot(low, query, nn)
                dqs.append((dot(low, k_ref[span, cols], tn) * score_scale).astype(bf16))
            dq_ref[...] = dqs[0] if heads == 1 else jnp.concatenate(dqs, axis=1)

        key_cases(total_keys, causal, block_index, visit)
    else:
        live = ((block_index + 1) * BLK + chunk - 1) // chunk if causal else total_keys // chunk
        rows = q_ref.shape[0]
        dqs = []
        for h in range(heads):
            cols = slice(h * HD, (h + 1) * HD)
            query = q_ref[:, cols] * jnp.asarray(score_scale, bf16)
            grad = g_ref[:, cols]
            lse = lse_ref[0, h : h + 1, :]

            def sums(n, row_term, cols=cols, query=query, grad=grad, lse=lse):
                span = pl.ds(pl.multiple_of(n * chunk, chunk), chunk)
                weights = probabilities(query, span, cols, n * chunk, lse)
                grad_weights = dot(v_ref[span, cols], grad, nt)
                return row_term + jnp.sum(grad_weights * weights, axis=0, keepdims=True)

            row_term = lax.fori_loop(0, live, sums, jnp.zeros((1, rows), f32))

            def step(n, acc, h=h, cols=cols, query=query, grad=grad, lse=lse, row_term=row_term):
                span = pl.ds(pl.multiple_of(n * chunk, chunk), chunk)
                weights = probabilities(query, span, cols, n * chunk, lse)
                dv_acc[h, span, :] += dot(weights.astype(bf16), grad, nn)
                grad_weights = dot(v_ref[span, cols], grad, nt)
                low = (weights * (grad_weights - row_term)).astype(bf16)
                dk_acc[h, span, :] += dot(low, query, nn)
                return acc + dot(low, k_ref[span, cols], tn)

            acc = lax.fori_loop(0, live, step, jnp.zeros((rows, HD), f32))
            dqs.append((acc * score_scale).astype(bf16))
        dq_ref[...] = dqs[0] if heads == 1 else jnp.concatenate(dqs, axis=1)

    @pl.when(block_index == pl.num_programs(1) - 1)
    def _():
        for ref, acc in ((dk_ref, dk_acc), (dv_ref, dv_acc)):
            parts = [acc[h].astype(bf16) for h in range(heads)]
            ref[...] = parts[0] if heads == 1 else jnp.concatenate(parts, axis=1)


def attention_specs(total_q, total_k, width):
    block = min(2 * HD, width)
    heads = block // HD
    groups = width // block
    rows = min(BLK, total_q)
    chunk = min(1024, total_k)
    q_spec = pl.BlockSpec((rows, block), lambda g, i, _: (i, g))
    k_spec = pl.BlockSpec((total_k, block), lambda g, i, _: (0, g))
    l_spec = pl.BlockSpec((1, heads, rows), lambda g, i, _: (g, 0, i))
    return block, heads, groups, rows, chunk, q_spec, k_spec, l_spec


def attend_forward(queries, keys, values, lengths, causal):
    total_q, width = queries.shape
    total_k = keys.shape[0]
    block, heads, groups, rows, chunk, q_spec, k_spec, l_spec = attention_specs(
        total_q, total_k, width
    )
    work = total_q * total_k * width
    return pl.pallas_call(
        functools.partial(forward_kernel, causal, heads, chunk),
        grid_spec=pltpu.PrefetchScalarGridSpec(
            num_scalar_prefetch=1,
            grid=(groups, total_q // rows),
            in_specs=[q_spec, k_spec, k_spec],
            out_specs=[q_spec, l_spec],
        ),
        out_shape=[
            jax.ShapeDtypeStruct((total_q, width), bf16),
            jax.ShapeDtypeStruct((groups, heads, total_q), f32),
        ],
        compiler_params=pltpu.CompilerParams(vmem_limit_bytes=vmem_limit),
        cost_estimate=pl.CostEstimate(
            flops=4 * work, bytes_accessed=8 * total_k * width, transcendentals=work // HD
        ),
    )(lengths, queries, keys, values)


def attend_back(queries, keys, values, grads, lse, lengths, causal):
    total_q, width = queries.shape
    total_k = keys.shape[0]
    block, heads, groups, rows, chunk, q_spec, k_spec, l_spec = attention_specs(
        total_q, total_k, width
    )
    work = total_q * total_k * width
    return pl.pallas_call(
        functools.partial(backward_kernel, causal, heads, chunk),
        grid_spec=pltpu.PrefetchScalarGridSpec(
            num_scalar_prefetch=1,
            grid=(groups, total_q // rows),
            in_specs=[q_spec, k_spec, k_spec, q_spec, l_spec],
            out_specs=[q_spec, k_spec, k_spec],
            scratch_shapes=[
                pltpu.VMEM((heads, total_k, HD), f32),
                pltpu.VMEM((heads, total_k, HD), f32),
            ],
        ),
        out_shape=[
            jax.ShapeDtypeStruct((total_q, width), bf16),
            jax.ShapeDtypeStruct((total_k, width), bf16),
            jax.ShapeDtypeStruct((total_k, width), bf16),
        ],
        compiler_params=pltpu.CompilerParams(vmem_limit_bytes=vmem_limit),
        cost_estimate=pl.CostEstimate(
            flops=10 * work, bytes_accessed=16 * total_k * width, transcendentals=work // HD
        ),
    )(lengths, queries, keys, values, grads, lse)


def assemble(arrays, moves, shape):
    dtype = arrays[0].dtype
    if any(m[2] % 16 or m[4] % 128 or m[1] % 16 or m[3] % 128 for m in moves):
        result = jnp.zeros(shape, dtype)
        for index, row, rows, col, cols, to_row, to_col in moves:
            part = arrays[index][row : row + rows, col : col + cols]
            result = lax.dynamic_update_slice(result, part, (to_row, to_col))
        return result
    count = len(arrays)
    places = jnp.stack([jnp.asarray(p, jnp.int32) for m in moves for p in (m[5], m[6])])

    def kernel(places_ref, *refs):
        sources, target, sems = refs[:count], refs[count], refs[count + 1]
        copies = []
        for n, (index, row, rows, col, cols, _, _) in enumerate(moves):
            to_row = pl.multiple_of(places_ref[2 * n], rows)
            to_col = pl.multiple_of(places_ref[2 * n + 1], cols)
            copies.append(
                pltpu.make_async_copy(
                    sources[index].at[pl.ds(row, rows), pl.ds(col, cols)],
                    target.at[pl.ds(to_row, rows), pl.ds(to_col, cols)],
                    sems.at[n],
                )
            )
        for copy in copies:
            copy.start()
        for copy in copies:
            copy.wait()

    return pl.pallas_call(
        kernel,
        grid_spec=pltpu.PrefetchScalarGridSpec(
            num_scalar_prefetch=1,
            grid=(1,),
            in_specs=[pl.BlockSpec(memory_space=pl.ANY)] * count,
            out_specs=pl.BlockSpec(memory_space=pltpu.VMEM),
            scratch_shapes=[pltpu.SemaphoreType.DMA((len(moves),))],
        ),
        out_shape=jax.ShapeDtypeStruct(shape, dtype),
        compiler_params=pltpu.CompilerParams(vmem_limit_bytes=vmem_limit),
        cost_estimate=pl.CostEstimate(
            flops=0,
            bytes_accessed=2 * sum(a.size * a.dtype.itemsize for a in arrays),
            transcendentals=0,
        ),
    )(places, *arrays)


def gelu_both(values):
    inner = gelu_coef * (values + gelu_cube * values * values * values)
    tangent = jnp.tanh(inner)
    output = 0.5 * values * (1.0 + tangent)
    slope = 0.5 * (1.0 + tangent) + 0.5 * values * (1.0 - tangent * tangent) * gelu_coef * (
        1.0 + 3.0 * gelu_cube * values * values
    )
    return (output, slope)


def layer_norm(values, gain_row, shift_row):
    center = values - jnp.mean(values, axis=-1, keepdims=True)
    inverse = lax.rsqrt(jnp.mean(center * center, axis=-1, keepdims=True) + layer_eps)
    normed = center * inverse
    return (normed * gain_row + shift_row, normed, inverse)


def norm_back(grad_rows, normed, inverse, gain_row):
    scaled = grad_rows * gain_row
    inner_term = scaled - jnp.mean(scaled, axis=-1, keepdims=True)
    inner_term = inner_term - normed * jnp.mean(scaled * normed, axis=-1, keepdims=True)
    return (
        inverse * inner_term,
        jnp.sum(grad_rows * normed, axis=0),
        jnp.sum(grad_rows, axis=0),
    )


def column_sum(array):
    return jnp.sum(array.astype(f32), axis=0)


def after(value, *earlier):
    return lax.optimization_barrier((value, *earlier))[0]


def solution(mesh):
    S, F = mesh.shape["seq"], mesh.shape["fsdp"]
    Y = S // CORES
    Z = 4 if F % 4 == 0 else 1
    X = F // Z

    core_perm = [(n, n ^ 1) for n in range(S)]

    def y_perm(k):
        return [(y * CORES + c, (y + k) % Y * CORES + c) for y in range(Y) for c in range(CORES)]

    def z_perm(k):
        return [(z * X + x, (z + k) % Z * X + x) for z in range(Z) for x in range(X)]

    def x_perm(k):
        return [(z * X + x, z * X + (x + k) % X) for z in range(Z) for x in range(X)]

    def core_swap(array):
        return lax.ppermute(array, "seq", core_perm)

    def y_shift(array, k):
        return lax.ppermute(array, "seq", y_perm(k % Y)) if k % Y else array

    def z_shift(array, k):
        return lax.ppermute(array, "fsdp", z_perm(k % Z)) if k % Z else array

    def x_shift(array, k):
        return lax.ppermute(array, "fsdp", x_perm(k % X)) if k % X else array

    def local(
        hidden_in,
        memory,
        lengths,
        out_grad,
        self_in_weight,
        self_query_bias,
        self_value_bias,
        self_out_weight,
        self_out_bias,
        cross_query_weight,
        cross_query_bias,
        memory_weight,
        memory_value_bias,
        cross_out_weight,
        cross_out_bias,
        ffn_in_weight,
        ffn_in_bias,
        ffn_out_weight,
        ffn_out_bias,
        norm_gain,
        norm_bias,
    ):
        s = lax.axis_index("seq")
        y, c = s // CORES, s % CORES
        f = lax.axis_index("fsdp")
        z, x = f // X, f % X
        _, t, D = hidden_in.shape
        T = S * t
        hw = D // S
        FF = ffn_in_weight.shape[1]
        shard = D // F
        part = shard // S
        fw = FF // (F * S)
        hidden_in, memory, out_grad = hidden_in[0], memory[0], out_grad[0]

        relative = [(k, e) for e in range(CORES) for k in range(Y)]

        def seq_of(k, e):
            return lax.rem(y - k + Y, Y) * CORES + (c if e == 0 else 1 - c)

        def seq_gather(array):
            own = [y_shift(array, k) for k in range(Y)]
            return own + [core_swap(a) for a in own]

        def seq_scatter(parts):
            chip = []
            for k in reversed(range(Y)):
                other = core_swap(parts[(k, 1)].astype(bf16))
                chip.append((k, parts[(k, 0)].astype(f32) + other.astype(f32)))
            total = None
            for k, value in chip:
                value = y_shift(value.astype(bf16), -k).astype(f32) if k else value
                total = value if total is None else total + value
            return total

        def fsdp_gather(chunk):
            pieces = []
            for kz in range(Z):
                column = z_shift(chunk, kz)
                for kx in range(X):
                    pieces.append(x_shift(column, kx))
            return pieces

        def fsdp_place(pieces):
            rows, cols = pieces[0].shape
            moves = []
            for n in range(F):
                kz, kx = n // X, n % X
                where = lax.rem(z - kz + Z, Z) * X + lax.rem(x - kx + X, X)
                moves.append((n, 0, rows, 0, cols, where * rows, 0))
            return assemble(pieces, moves, (F * rows, cols))

        def fsdp_scatter(grads):
            rows, cols = grads.shape[0] // F, grads.shape[1]
            view = grads.reshape(Z, X, rows, cols)
            total = lax.dynamic_index_in_dim(view, x, 1, keepdims=False).astype(f32)
            for kx in range(1, X):
                sent = lax.dynamic_index_in_dim(view, lax.rem(x + kx, X), 1, keepdims=False)
                total = total + x_shift(sent.astype(bf16), kx).astype(f32)
            low = total.astype(bf16)
            own = lax.dynamic_index_in_dim(low, z, 0, keepdims=False).astype(f32)
            for kz in range(1, Z):
                sent = lax.dynamic_index_in_dim(low, lax.rem(z + kz, Z), 0, keepdims=False)
                own = own + z_shift(sent, kz).astype(f32)
            return own.astype(bf16)

        def finish(own):
            rows, cols = own.shape
            pieces = seq_gather(own)
            moves = [
                (n, 0, rows, 0, cols, seq_of(k, e) * rows, 0)
                for n, (k, e) in enumerate(relative)
            ]
            return assemble(pieces, moves, (S * rows, cols)).reshape(S, rows, cols).astype(f32)

        def pick(array, start, size):
            return lax.dynamic_slice_in_dim(array, start, size, 1)

        small_list = [
            self_query_bias, self_value_bias, self_out_bias, cross_query_bias, memory_value_bias,
            cross_out_bias, ffn_out_bias, norm_gain.reshape(-1), norm_bias.reshape(-1), ffn_in_bias,
        ]
        small = jnp.concatenate(small_list)
        small = lax.all_to_all(
            jnp.broadcast_to(small[None], (F, small.shape[0])), "fsdp", 0, 0, tiled=True
        ).astype(f32)
        smalls = []
        at = 0
        for _ in range(7):
            smalls.append(small[:, at : at + shard].reshape(D))
            at += shard
        b_query, b_value, b_attn_out, b_cross_q, b_mem_value, b_cross_out, b_ffn_out = smalls
        gains = small[:, at : at + 3 * shard].reshape(F, 3, shard).swapaxes(0, 1).reshape(3, D)
        at += 3 * shard
        shifts = small[:, at : at + 3 * shard].reshape(F, 3, shard).swapaxes(0, 1).reshape(3, D)
        at += 3 * shard
        b_ffn_in = lax.dynamic_index_in_dim(
            small[:, at:].reshape(F, S, fw), s, 1, keepdims=False
        ).reshape(F * fw)

        def group_row(row):
            return lax.dynamic_slice_in_dim(row, s * hw, hw, 0)

        chunk_qkv = jnp.concatenate(
            [pick(self_in_weight, m * D + s * hw, hw) for m in range(3)], axis=1
        )
        chunk_mid = jnp.concatenate(
            [pick(memory_weight, m * D + s * hw, hw) for m in range(2)]
            + [pick(cross_query_weight, s * hw, hw)],
            axis=1,
        )
        chunk_out = jnp.concatenate(
            [
                lax.dynamic_slice_in_dim(w, s * part, part, 0)
                for w in (self_out_weight, cross_out_weight)
            ],
            axis=0,
        )
        chunk_fin = lax.dynamic_index_in_dim(
            ffn_in_weight.reshape(shard, F, S, fw), s, 2, keepdims=False
        ).reshape(shard, F * fw)
        chunk_fout = lax.dynamic_slice_in_dim(ffn_out_weight, s * fw, fw, 0)

        got_qkv = fsdp_gather(chunk_qkv)
        x_blocks = seq_gather(hidden_in)
        got_mid = fsdp_gather(after(chunk_mid, got_qkv[-1]))
        m_blocks = seq_gather(after(memory, x_blocks[-1]))
        got_out = fsdp_gather(after(chunk_out, got_qkv[-1]))
        got_fin = fsdp_gather(after(chunk_fin, got_mid[-1]))
        got_fout = fsdp_gather(after(chunk_fout, got_fin[-1]))

        w_qkv = fsdp_place(got_qkv)
        block_moves = [
            (n, 0, t, 0, D, seq_of(k, e) * t, 0) for n, (k, e) in enumerate(relative)
        ]
        x_all = assemble(x_blocks, block_moves, (T, D))
        qkv_bias = jnp.concatenate([group_row(b_query), jnp.zeros((hw,), f32), group_row(b_value)])
        qkv = (dot(x_all, w_qkv, nn) + qkv_bias).astype(bf16)
        q_self, k_self, v_self = (qkv[:, m * hw : (m + 1) * hw] for m in range(3))
        self_attn, self_lse = attend_forward(q_self, k_self, v_self, lengths, True)

        w_mid = fsdp_place(got_mid)
        w_mem, cq_quarter = w_mid[:, : 2 * hw], w_mid[:, 2 * hw :]
        m_all = jnp.concatenate(m_blocks, axis=0)
        mem_bias = jnp.concatenate([jnp.zeros((hw,), f32), group_row(b_mem_value)])
        kv_mem = (dot(m_all, w_mem, nn) + mem_bias).astype(bf16)

        def all_rows(parts_of):
            return assemble(
                parts_of,
                [(n, 0, t, 0, hw, 0, seq_of(k, e) * hw) for n, (k, e) in enumerate(relative)],
                (t, D),
            )

        def heads_to_rows(array):
            blocks = array.reshape(S, t, hw)
            mine = []
            for k, e in relative:
                target = lax.rem(y + k, Y) * CORES + (c if e == 0 else 1 - c)
                sent = lax.dynamic_index_in_dim(blocks, target, 0, keepdims=False)
                sent = y_shift(sent, k)
                mine.append(core_swap(sent) if e else sent)
            return all_rows(mine)

        def rows_to_heads(array):
            mine = []
            for k, e in relative:
                target = lax.rem(y + k, Y) * CORES + (c if e == 0 else 1 - c)
                sent = y_shift(pick(array, target * hw, hw), k)
                mine.append(core_swap(sent) if e else sent)
            return assemble(
                mine,
                [(n, 0, t, 0, hw, seq_of(k, e) * t, 0) for n, (k, e) in enumerate(relative)],
                (T, hw),
            )

        attn_tok = heads_to_rows(self_attn)
        mem_chips = [y_shift(kv_mem, k) for k in range(Y)]
        mem_key = jnp.concatenate([m[:, :hw] for m in mem_chips], axis=1)
        mem_value = jnp.concatenate([m[:, hw:] for m in mem_chips], axis=1)

        out_quarter = fsdp_place(got_out)
        out_pieces = seq_gather(out_quarter)
        own_moves = [[], []]
        for n, (k, e) in enumerate(relative):
            for which in range(2):
                for shard_index in range(F):
                    own_moves[which].append(
                        (
                            n, shard_index * 2 * part + which * part, part, 0, D,
                            shard_index * shard + seq_of(k, e) * part, 0,
                        )
                    )
        w_attn_out = assemble(out_pieces, own_moves[0], (D, D))
        w_cross_out = assemble(out_pieces, own_moves[1], (D, D))
        cq_pieces = seq_gather(cq_quarter)
        w_cross_q = jnp.concatenate(cq_pieces, axis=1)
        b_cq = jnp.concatenate(
            [lax.dynamic_slice_in_dim(b_cross_q, seq_of(k, e) * hw, hw, 0) for k, e in relative]
        )
        half = Y * hw

        x_float = hidden_in.astype(f32)
        branch = dot(attn_tok, w_attn_out, nn) + b_attn_out
        first, normed_one, inverse_one = layer_norm(
            alpha_scale * x_float + branch, gains[0], shifts[0]
        )
        first_low = first.astype(bf16)
        cq_rows = (dot(first_low, w_cross_q, nn) + b_cq).astype(bf16)

        cross_q = jnp.concatenate([cq_rows[:, :half], core_swap(cq_rows[:, half:])], axis=0)
        cross_attn, cross_lse = attend_forward(cross_q, mem_key, mem_value, lengths, False)
        cross_other = core_swap(cross_attn[t:])
        cross_tok = assemble(
            [cross_attn, cross_other],
            [(e, 0, t, k * hw, hw, 0, seq_of(k, e) * hw) for k, e in relative],
            (t, D),
        )
        cross_branch = dot(cross_tok, w_cross_out, nn) + b_cross_out
        second, normed_two, inverse_two = layer_norm(
            alpha_scale * first + cross_branch, gains[1], shifts[1]
        )
        second_low = second.astype(bf16)

        w_fin = fsdp_place(got_fin)
        w_fout = fsdp_place(got_fout)
        second_all = jnp.concatenate(seq_gather(second_low), axis=0)
        pre_act = dot(second_all, w_fin, nn) + b_ffn_in
        act_value, act_slope = gelu_both(pre_act)
        hidden_low = act_value.astype(bf16)
        ffn_part = dot(hidden_low, w_fout, nn)

        def by_owner(array):
            return {ke: array[n * t : (n + 1) * t] for n, ke in enumerate(relative)}

        ffn_branch = seq_scatter(by_owner(ffn_part)) + b_ffn_out
        result, normed_three, inverse_three = layer_norm(
            alpha_scale * second + ffn_branch, gains[2], shifts[2]
        )
        layer_out = result.astype(bf16)

        d_three, gain_three, shift_three = norm_back(
            out_grad.astype(f32), normed_three, inverse_three, gains[2]
        )
        d_ffn = d_three.astype(bf16)
        d_ffn_all = jnp.concatenate(seq_gather(d_ffn), axis=0)
        d_hidden = dot(d_ffn_all, w_fout, nt)
        d_pre = (act_slope * d_hidden).astype(bf16)
        d_second_part = dot(d_pre, w_fin, nt)
        d_second = alpha_scale * d_three + seq_scatter(by_owner(d_second_part))
        grad_fout = dot(hidden_low, d_ffn_all, tn).astype(bf16)
        own_fout = fsdp_scatter(grad_fout)
        grad_fin = dot(second_all, d_pre, tn).astype(bf16)
        own_fin = fsdp_scatter(grad_fin)

        d_two, gain_two, shift_two = norm_back(d_second, normed_two, inverse_two, gains[1])
        d_cross = d_two.astype(bf16)
        d_cross_tok = dot(d_cross, w_cross_out, nt).astype(bf16)
        keep, send = (
            jnp.concatenate([pick(d_cross_tok, seq_of(k, e) * hw, hw) for k in range(Y)], axis=1)
            for e in range(CORES)
        )
        d_cross_heads = jnp.concatenate([keep, core_swap(send)], axis=0)
        dq_cross, dk_mem, dv_mem = attend_back(
            cross_q, mem_key, mem_value, d_cross_heads, cross_lse, lengths, False
        )
        d_cq_rows = jnp.concatenate([dq_cross[:t], core_swap(dq_cross[t:])], axis=1)
        d_first = alpha_scale * d_two + dot(d_cq_rows, w_cross_q, nt)
        grad_cross_out = dot(cross_tok, d_cross, tn)
        grad_cq = dot(first_low, d_cq_rows, tn)
        d_mem = None
        for k in range(Y):
            sent = jnp.concatenate([d[:, k * hw : (k + 1) * hw] for d in (dk_mem, dv_mem)], axis=1)
            got = y_shift(sent, -k).astype(f32)
            d_mem = got if d_mem is None else d_mem + got
        d_mem = d_mem.astype(bf16)
        grad_mem = dot(m_all, d_mem, tn).astype(bf16)
        memory_grad = seq_scatter(by_owner(dot(d_mem, w_mem, nt))).astype(bf16)

        d_one, gain_one, shift_one = norm_back(d_first, normed_one, inverse_one, gains[0])
        d_branch = d_one.astype(bf16)
        d_attn_heads = rows_to_heads(dot(d_branch, w_attn_out, nt).astype(bf16))
        grad_self_out = dot(attn_tok, d_branch, tn)
        dq_self, dk_self, dv_self = attend_back(
            q_self, k_self, v_self, d_attn_heads, self_lse, lengths, True
        )
        d_qkv = jnp.concatenate([dq_self, dk_self, dv_self], axis=1)
        grad_qkv = dot(x_all, d_qkv, tn).astype(bf16)
        own_qkv = fsdp_scatter(grad_qkv)
        input_part = dot(d_qkv, w_qkv, nt).reshape(S, t, D)
        input_sum = seq_scatter(
            {
                (k, e): lax.dynamic_index_in_dim(input_part, seq_of(k, e), 0, keepdims=False)
                for k, e in relative
            }
        )
        input_grad = (alpha_scale * d_one + input_sum).astype(bf16)

        def out_parts(grad):
            view = grad.astype(bf16).reshape(F, S, part, D)
            return {
                (k, e): lax.dynamic_index_in_dim(view, seq_of(k, e), 1, keepdims=False)
                for k, e in relative
            }

        own_cross_out = seq_scatter(out_parts(grad_cross_out)).astype(bf16)
        own_self_out = seq_scatter(out_parts(grad_self_out)).astype(bf16)
        own_cq = seq_scatter(
            {ke: grad_cq[:, n * hw : (n + 1) * hw] for n, ke in enumerate(relative)}
        ).astype(bf16)
        own_mid = fsdp_scatter(jnp.concatenate([grad_mem, own_cq], axis=1))
        own_out = fsdp_scatter(
            jnp.concatenate([own_self_out, own_cross_out], axis=1).reshape(F * 2 * part, D)
        )

        all_fout = finish(own_fout).reshape(S * fw, D)
        all_fin = (
            finish(own_fin).reshape(S, shard, F, fw).transpose(1, 2, 0, 3).reshape(shard, FF)
        )
        all_mid = finish(own_mid)
        all_mem = (
            all_mid[:, :, : 2 * hw]
            .reshape(S, shard, 2, hw)
            .transpose(1, 2, 0, 3)
            .reshape(shard, 2 * D)
        )
        all_cq = all_mid[:, :, 2 * hw :].transpose(1, 0, 2).reshape(shard, D)
        all_out = finish(own_out).reshape(S, 2, part, D)
        all_self_out = all_out[:, 0].reshape(shard, D)
        all_cross_out = all_out[:, 1].reshape(shard, D)
        all_qkv = (
            finish(own_qkv).reshape(S, shard, 3, hw).transpose(1, 2, 0, 3).reshape(shard, 3 * D)
        )

        def spread(row):
            return lax.dynamic_update_slice_in_dim(jnp.zeros((D,), f32), row, s * hw, 0)

        d_cq_sum = column_sum(d_cq_rows)
        cq_bias = jnp.zeros((D,), f32)
        for n, (k, e) in enumerate(relative):
            cq_bias = lax.dynamic_update_slice_in_dim(
                cq_bias, d_cq_sum[n * hw : (n + 1) * hw], seq_of(k, e) * hw, 0
            )
        fin_bias = lax.dynamic_update_slice_in_dim(
            jnp.zeros((F, S, fw), f32), column_sum(d_pre).reshape(F, 1, fw), s, 1
        ).reshape(F, S * fw)
        small_grads = jnp.concatenate(
            [
                row.reshape(F, shard)
                for row in (
                    spread(column_sum(dq_self)), spread(column_sum(dv_self)), column_sum(d_branch),
                    cq_bias, spread(column_sum(d_mem[:, hw:])), column_sum(d_cross),
                    column_sum(d_ffn), gain_one, gain_two, gain_three, shift_one, shift_two,
                    shift_three,
                )
            ]
            + [fin_bias],
            axis=1,
        )
        small_own = jnp.sum(lax.all_to_all(small_grads, "fsdp", 0, 0, tiled=True), axis=0)
        small_own = lax.psum(small_own, "seq")
        rows = [small_own[n * shard : (n + 1) * shard] for n in range(13)]
        return (
            layer_out[None],
            input_grad[None],
            memory_grad[None],
            all_qkv,
            rows[0],
            rows[1],
            all_self_out,
            rows[2],
            all_cq,
            rows[3],
            all_mem,
            rows[4],
            all_cross_out,
            rows[5],
            all_fin,
            small_own[13 * shard :],
            all_fout,
            rows[6],
            jnp.stack(rows[7:10]),
            jnp.stack(rows[10:13]),
        )

    by_row, rows_1d = P("fsdp", None), P("fsdp")
    tokens, norms = P("fsdp", "seq", None), P(None, "fsdp")
    in_specs = (
        tokens, tokens, rows_1d, tokens, by_row, rows_1d, rows_1d, by_row, rows_1d, by_row, rows_1d,
        by_row, rows_1d, by_row, rows_1d, by_row, rows_1d, by_row, rows_1d, norms, norms,
    )
    out_specs = (
        tokens, tokens, tokens, by_row, rows_1d, rows_1d, by_row, rows_1d, by_row, rows_1d, by_row,
        rows_1d, by_row, rows_1d, by_row, rows_1d, by_row, rows_1d, norms, norms,
    )
    return jax.shard_map(local, mesh=mesh, in_specs=in_specs, out_specs=out_specs, check_vma=False)
```

```python
import functools

import jax
import jax.numpy as jnp
from jax import lax
from jax.experimental import pallas as pl
from jax.experimental.pallas import tpu as pltpu
from jax.sharding import PartitionSpec as P

HD = 64
BLK = 256
CORES = 2

alpha_scale = 300.0**0.25
layer_eps = 1e-05
score_scale = 0.125
masked_value = -1e30
gelu_coef = 0.7978845608028654
gelu_cube = 0.044715

f32 = jnp.float32
bf16 = jnp.bfloat16
vmem_limit = 56 * 1024 * 1024


def dot(left, right, dims):
    return lax.dot_general(left, right, (dims, ((), ())), preferred_element_type=f32)


nn = ((1,), (0,))
nt = ((1,), (1,))
tn = ((0,), (0,))


def key_cases(total_keys, causal, block_index, visit):
    if not causal:
        visit(total_keys)
        return
    blocks = total_keys // BLK
    cases = min(4, blocks)
    for case in range(cases):
        low, high = case * blocks // cases, (case + 1) * blocks // cases

        @pl.when((block_index >= low) & (block_index < high))
        def _(high=high):
            visit(high * BLK)


def mask_scores(scores, first_key, limit):
    key_pos = first_key + lax.broadcasted_iota(jnp.int32, scores.shape, 0)
    return jnp.where(key_pos < limit, scores, masked_value)


def forward_kernel(causal, heads, chunk, len_ref, q_ref, k_ref, v_ref, o_ref, lse_ref):
    block_index = pl.program_id(1)
    total_keys = k_ref.shape[0]
    limit = jnp.minimum(len_ref[0], (block_index + 1) * BLK) if causal else 0
    rows = q_ref.shape[0]

    if total_keys <= chunk:

        def visit(key_count):
            outs, lses = [], []
            for h in range(heads):
                cols = slice(h * HD, (h + 1) * HD)
                query = q_ref[:, cols] * jnp.asarray(score_scale, bf16)
                scores = dot(k_ref[:key_count, cols], query, nt)
                if causal:
                    scores = mask_scores(scores, 0, limit)
                top = jnp.max(scores, axis=0, keepdims=True)
                weights = jnp.exp(scores - top)
                totals = jnp.sum(weights, axis=0, keepdims=True)
                low = (weights * (1.0 / totals)).astype(bf16)
                outs.append(dot(low, v_ref[:key_count, cols], tn).astype(bf16))
                lses.append(top + jnp.log(totals))
            o_ref[...] = outs[0] if heads == 1 else jnp.concatenate(outs, axis=1)
            lse_ref[0] = lses[0] if heads == 1 else jnp.concatenate(lses, axis=0)

        key_cases(total_keys, causal, block_index, visit)
    else:
        live = ((block_index + 1) * BLK + chunk - 1) // chunk if causal else total_keys // chunk
        outs, lses = [], []
        for h in range(heads):
            cols = slice(h * HD, (h + 1) * HD)
            query = q_ref[:, cols] * jnp.asarray(score_scale, bf16)

            def step(n, carry, cols=cols, query=query):
                top, totals, acc = carry
                span = pl.ds(pl.multiple_of(n * chunk, chunk), chunk)
                scores = dot(k_ref[span, cols], query, nt)
                if causal:
                    scores = mask_scores(scores, n * chunk, limit)
                new_top = jnp.maximum(top, jnp.max(scores, axis=0, keepdims=True))
                decay = jnp.exp(top - new_top)
                weights = jnp.exp(scores - new_top)
                totals = totals * decay + jnp.sum(weights, axis=0, keepdims=True)
                acc = acc * decay + dot(v_ref[span, cols], weights.astype(bf16), tn)
                return new_top, totals, acc

            start = (
                jnp.full((1, rows), masked_value, f32),
                jnp.zeros((1, rows), f32),
                jnp.zeros((HD, rows), f32),
            )
            top, totals, acc = lax.fori_loop(0, live, step, start)
            outs.append((acc / totals).T.astype(bf16))
            lses.append(top + jnp.log(totals))
        o_ref[...] = outs[0] if heads == 1 else jnp.concatenate(outs, axis=1)
        lse_ref[0] = lses[0] if heads == 1 else jnp.concatenate(lses, axis=0)


def backward_kernel(
    causal, heads, chunk, len_ref, q_ref, k_ref, v_ref, g_ref, lse_ref, dq_ref, dk_ref, dv_ref,
    dk_acc, dv_acc
):
    block_index = pl.program_id(1)
    total_keys = k_ref.shape[0]
    limit = jnp.minimum(len_ref[0], (block_index + 1) * BLK) if causal else 0

    @pl.when(block_index == 0)
    def _():
        dk_acc[...] = jnp.zeros_like(dk_acc)
        dv_acc[...] = jnp.zeros_like(dv_acc)

    def probabilities(query, span, cols, first_key, lse):
        scores = dot(k_ref[span, cols], query, nt)
        if causal:
            scores = mask_scores(scores, first_key, limit)
        return jnp.exp(scores - lse)

    if total_keys <= chunk:

        def visit(key_count):
            span = slice(0, key_count)
            dqs = []
            for h in range(heads):
                cols = slice(h * HD, (h + 1) * HD)
                query = q_ref[:, cols] * jnp.asarray(score_scale, bf16)
                grad = g_ref[:, cols]
                weights = probabilities(query, span, cols, 0, lse_ref[0, h : h + 1, :])
                dv_acc[h, span, :] += dot(weights.astype(bf16), grad, nn)
                grad_weights = dot(v_ref[span, cols], grad, nt)
                row_term = jnp.sum(grad_weights * weights, axis=0, keepdims=True)
                low = (weights * (grad_weights - row_term)).astype(bf16)
                dk_acc[h, span, :] += dot(low, query, nn)
                dqs.append((dot(low, k_ref[span, cols], tn) * score_scale).astype(bf16))
            dq_ref[...] = dqs[0] if heads == 1 else jnp.concatenate(dqs, axis=1)

        key_cases(total_keys, causal, block_index, visit)
    else:
        live = ((block_index + 1) * BLK + chunk - 1) // chunk if causal else total_keys // chunk
        rows = q_ref.shape[0]
        dqs = []
        for h in range(heads):
            cols = slice(h * HD, (h + 1) * HD)
            query = q_ref[:, cols] * jnp.asarray(score_scale, bf16)
            grad = g_ref[:, cols]
            lse = lse_ref[0, h : h + 1, :]

            def sums(n, row_term, cols=cols, query=query, grad=grad, lse=lse):
                span = pl.ds(pl.multiple_of(n * chunk, chunk), chunk)
                weights = probabilities(query, span, cols, n * chunk, lse)
                grad_weights = dot(v_ref[span, cols], grad, nt)
                return row_term + jnp.sum(grad_weights * weights, axis=0, keepdims=True)

            row_term = lax.fori_loop(0, live, sums, jnp.zeros((1, rows), f32))

            def step(n, acc, h=h, cols=cols, query=query, grad=grad, lse=lse, row_term=row_term):
                span = pl.ds(pl.multiple_of(n * chunk, chunk), chunk)
                weights = probabilities(query, span, cols, n * chunk, lse)
                dv_acc[h, span, :] += dot(weights.astype(bf16), grad, nn)
                grad_weights = dot(v_ref[span, cols], grad, nt)
                low = (weights * (grad_weights - row_term)).astype(bf16)
                dk_acc[h, span, :] += dot(low, query, nn)
                return acc + dot(low, k_ref[span, cols], tn)

            acc = lax.fori_loop(0, live, step, jnp.zeros((rows, HD), f32))
            dqs.append((acc * score_scale).astype(bf16))
        dq_ref[...] = dqs[0] if heads == 1 else jnp.concatenate(dqs, axis=1)

    @pl.when(block_index == pl.num_programs(1) - 1)
    def _():
        for ref, acc in ((dk_ref, dk_acc), (dv_ref, dv_acc)):
            parts = [acc[h].astype(bf16) for h in range(heads)]
            ref[...] = parts[0] if heads == 1 else jnp.concatenate(parts, axis=1)


def attention_specs(total_q, total_k, width):
    block = min(2 * HD, width)
    heads = block // HD
    groups = width // block
    rows = min(BLK, total_q)
    chunk = min(1024, total_k)
    q_spec = pl.BlockSpec((rows, block), lambda g, i, _: (i, g))
    k_spec = pl.BlockSpec((total_k, block), lambda g, i, _: (0, g))
    l_spec = pl.BlockSpec((1, heads, rows), lambda g, i, _: (g, 0, i))
    return block, heads, groups, rows, chunk, q_spec, k_spec, l_spec


def attend_forward(queries, keys, values, lengths, causal):
    total_q, width = queries.shape
    total_k = keys.shape[0]
    block, heads, groups, rows, chunk, q_spec, k_spec, l_spec = attention_specs(
        total_q, total_k, width
    )
    work = total_q * total_k * width
    return pl.pallas_call(
        functools.partial(forward_kernel, causal, heads, chunk),
        grid_spec=pltpu.PrefetchScalarGridSpec(
            num_scalar_prefetch=1,
            grid=(groups, total_q // rows),
            in_specs=[q_spec, k_spec, k_spec],
            out_specs=[q_spec, l_spec],
        ),
        out_shape=[
            jax.ShapeDtypeStruct((total_q, width), bf16),
            jax.ShapeDtypeStruct((groups, heads, total_q), f32),
        ],
        compiler_params=pltpu.CompilerParams(vmem_limit_bytes=vmem_limit),
        cost_estimate=pl.CostEstimate(
            flops=4 * work, bytes_accessed=8 * total_k * width, transcendentals=work // HD
        ),
    )(lengths, queries, keys, values)


def attend_back(queries, keys, values, grads, lse, lengths, causal):
    total_q, width = queries.shape
    total_k = keys.shape[0]
    block, heads, groups, rows, chunk, q_spec, k_spec, l_spec = attention_specs(
        total_q, total_k, width
    )
    work = total_q * total_k * width
    return pl.pallas_call(
        functools.partial(backward_kernel, causal, heads, chunk),
        grid_spec=pltpu.PrefetchScalarGridSpec(
            num_scalar_prefetch=1,
            grid=(groups, total_q // rows),
            in_specs=[q_spec, k_spec, k_spec, q_spec, l_spec],
            out_specs=[q_spec, k_spec, k_spec],
            scratch_shapes=[
                pltpu.VMEM((heads, total_k, HD), f32),
                pltpu.VMEM((heads, total_k, HD), f32),
            ],
        ),
        out_shape=[
            jax.ShapeDtypeStruct((total_q, width), bf16),
            jax.ShapeDtypeStruct((total_k, width), bf16),
            jax.ShapeDtypeStruct((total_k, width), bf16),
        ],
        compiler_params=pltpu.CompilerParams(vmem_limit_bytes=vmem_limit),
        cost_estimate=pl.CostEstimate(
            flops=10 * work, bytes_accessed=16 * total_k * width, transcendentals=work // HD
        ),
    )(lengths, queries, keys, values, grads, lse)


def assemble(arrays, moves, shape):
    dtype = arrays[0].dtype
    if any(m[2] % 16 or m[4] % 128 or m[1] % 16 or m[3] % 128 for m in moves):
        result = jnp.zeros(shape, dtype)
        for index, row, rows, col, cols, to_row, to_col in moves:
            part = arrays[index][row : row + rows, col : col + cols]
            result = lax.dynamic_update_slice(result, part, (to_row, to_col))
        return result
    count = len(arrays)
    places = jnp.stack([jnp.asarray(p, jnp.int32) for m in moves for p in (m[5], m[6])])

    def kernel(places_ref, *refs):
        sources, target, sems = refs[:count], refs[count], refs[count + 1]
        copies = []
        for n, (index, row, rows, col, cols, _, _) in enumerate(moves):
            to_row = pl.multiple_of(places_ref[2 * n], rows)
            to_col = pl.multiple_of(places_ref[2 * n + 1], cols)
            copies.append(
                pltpu.make_async_copy(
                    sources[index].at[pl.ds(row, rows), pl.ds(col, cols)],
                    target.at[pl.ds(to_row, rows), pl.ds(to_col, cols)],
                    sems.at[n],
                )
            )
        for copy in copies:
            copy.start()
        for copy in copies:
            copy.wait()

    return pl.pallas_call(
        kernel,
        grid_spec=pltpu.PrefetchScalarGridSpec(
            num_scalar_prefetch=1,
            grid=(1,),
            in_specs=[pl.BlockSpec(memory_space=pl.ANY)] * count,
            out_specs=pl.BlockSpec(memory_space=pltpu.VMEM),
            scratch_shapes=[pltpu.SemaphoreType.DMA((len(moves),))],
        ),
        out_shape=jax.ShapeDtypeStruct(shape, dtype),
        compiler_params=pltpu.CompilerParams(vmem_limit_bytes=vmem_limit),
        cost_estimate=pl.CostEstimate(
            flops=0,
            bytes_accessed=2 * sum(a.size * a.dtype.itemsize for a in arrays),
            transcendentals=0,
        ),
    )(places, *arrays)


def gelu_both(values):
    inner = gelu_coef * (values + gelu_cube * values * values * values)
    tangent = jnp.tanh(inner)
    output = 0.5 * values * (1.0 + tangent)
    slope = 0.5 * (1.0 + tangent) + 0.5 * values * (1.0 - tangent * tangent) * gelu_coef * (
        1.0 + 3.0 * gelu_cube * values * values
    )
    return (output, slope)


def layer_norm(values, gain_row, shift_row):
    center = values - jnp.mean(values, axis=-1, keepdims=True)
    inverse = lax.rsqrt(jnp.mean(center * center, axis=-1, keepdims=True) + layer_eps)
    normed = center * inverse
    return (normed * gain_row + shift_row, normed, inverse)


def norm_back(grad_rows, normed, inverse, gain_row):
    scaled = grad_rows * gain_row
    inner_term = scaled - jnp.mean(scaled, axis=-1, keepdims=True)
    inner_term = inner_term - normed * jnp.mean(scaled * normed, axis=-1, keepdims=True)
    return (
        inverse * inner_term,
        jnp.sum(grad_rows * normed, axis=0),
        jnp.sum(grad_rows, axis=0),
    )


def column_sum(array):
    return jnp.sum(array.astype(f32), axis=0)


def after(value, *earlier):
    return lax.optimization_barrier((value, *earlier))[0]


def general_layer(mesh):
    S, F = mesh.shape["seq"], mesh.shape["fsdp"]
    Y = S // CORES
    Z = 4 if F % 4 == 0 else 1
    X = F // Z

    core_perm = [(n, n ^ 1) for n in range(S)]

    def y_perm(k):
        return [(y * CORES + c, (y + k) % Y * CORES + c) for y in range(Y) for c in range(CORES)]

    def z_perm(k):
        return [(z * X + x, (z + k) % Z * X + x) for z in range(Z) for x in range(X)]

    def x_perm(k):
        return [(z * X + x, z * X + (x + k) % X) for z in range(Z) for x in range(X)]

    def core_swap(array):
        return lax.ppermute(array, "seq", core_perm)

    def y_shift(array, k):
        return lax.ppermute(array, "seq", y_perm(k % Y)) if k % Y else array

    def z_shift(array, k):
        return lax.ppermute(array, "fsdp", z_perm(k % Z)) if k % Z else array

    def x_shift(array, k):
        return lax.ppermute(array, "fsdp", x_perm(k % X)) if k % X else array

    def local(
        hidden_in,
        memory,
        lengths,
        out_grad,
        self_in_weight,
        self_query_bias,
        self_value_bias,
        self_out_weight,
        self_out_bias,
        cross_query_weight,
        cross_query_bias,
        memory_weight,
        memory_value_bias,
        cross_out_weight,
        cross_out_bias,
        ffn_in_weight,
        ffn_in_bias,
        ffn_out_weight,
        ffn_out_bias,
        norm_gain,
        norm_bias,
    ):
        s = lax.axis_index("seq")
        y, c = s // CORES, s % CORES
        f = lax.axis_index("fsdp")
        z, x = f // X, f % X
        _, t, D = hidden_in.shape
        T = S * t
        hw = D // S
        FF = ffn_in_weight.shape[1]
        shard = D // F
        part = shard // S
        fw = FF // (F * S)
        hidden_in, memory, out_grad = hidden_in[0], memory[0], out_grad[0]

        relative = [(k, e) for e in range(CORES) for k in range(Y)]

        def seq_of(k, e):
            return lax.rem(y - k + Y, Y) * CORES + (c if e == 0 else 1 - c)

        def seq_gather(array):
            own = [y_shift(array, k) for k in range(Y)]
            return own + [core_swap(a) for a in own]

        def seq_scatter(parts):
            chip = []
            for k in reversed(range(Y)):
                other = core_swap(parts[(k, 1)].astype(bf16))
                chip.append((k, parts[(k, 0)].astype(f32) + other.astype(f32)))
            total = None
            for k, value in chip:
                value = y_shift(value.astype(bf16), -k).astype(f32) if k else value
                total = value if total is None else total + value
            return total

        def fsdp_gather(chunk):
            pieces = []
            for kz in range(Z):
                column = z_shift(chunk, kz)
                for kx in range(X):
                    pieces.append(x_shift(column, kx))
            return pieces

        def fsdp_place(pieces):
            rows, cols = pieces[0].shape
            moves = []
            for n in range(F):
                kz, kx = n // X, n % X
                where = lax.rem(z - kz + Z, Z) * X + lax.rem(x - kx + X, X)
                moves.append((n, 0, rows, 0, cols, where * rows, 0))
            return assemble(pieces, moves, (F * rows, cols))

        def fsdp_scatter(grads):
            rows, cols = grads.shape[0] // F, grads.shape[1]
            view = grads.reshape(Z, X, rows, cols)
            total = lax.dynamic_index_in_dim(view, x, 1, keepdims=False).astype(f32)
            for kx in range(1, X):
                sent = lax.dynamic_index_in_dim(view, lax.rem(x + kx, X), 1, keepdims=False)
                total = total + x_shift(sent.astype(bf16), kx).astype(f32)
            low = total.astype(bf16)
            own = lax.dynamic_index_in_dim(low, z, 0, keepdims=False).astype(f32)
            for kz in range(1, Z):
                sent = lax.dynamic_index_in_dim(low, lax.rem(z + kz, Z), 0, keepdims=False)
                own = own + z_shift(sent, kz).astype(f32)
            return own.astype(bf16)

        def finish(own):
            rows, cols = own.shape
            pieces = seq_gather(own)
            moves = [
                (n, 0, rows, 0, cols, seq_of(k, e) * rows, 0)
                for n, (k, e) in enumerate(relative)
            ]
            return assemble(pieces, moves, (S * rows, cols)).reshape(S, rows, cols).astype(f32)

        def pick(array, start, size):
            return lax.dynamic_slice_in_dim(array, start, size, 1)

        small_list = [
            self_query_bias, self_value_bias, self_out_bias, cross_query_bias, memory_value_bias,
            cross_out_bias, ffn_out_bias, norm_gain.reshape(-1), norm_bias.reshape(-1), ffn_in_bias,
        ]
        small = jnp.concatenate(small_list)
        small = lax.all_to_all(
            jnp.broadcast_to(small[None], (F, small.shape[0])), "fsdp", 0, 0, tiled=True
        ).astype(f32)
        smalls = []
        at = 0
        for _ in range(7):
            smalls.append(small[:, at : at + shard].reshape(D))
            at += shard
        b_query, b_value, b_attn_out, b_cross_q, b_mem_value, b_cross_out, b_ffn_out = smalls
        gains = small[:, at : at + 3 * shard].reshape(F, 3, shard).swapaxes(0, 1).reshape(3, D)
        at += 3 * shard
        shifts = small[:, at : at + 3 * shard].reshape(F, 3, shard).swapaxes(0, 1).reshape(3, D)
        at += 3 * shard
        b_ffn_in = lax.dynamic_index_in_dim(
            small[:, at:].reshape(F, S, fw), s, 1, keepdims=False
        ).reshape(F * fw)

        def group_row(row):
            return lax.dynamic_slice_in_dim(row, s * hw, hw, 0)

        chunk_qkv = jnp.concatenate(
            [pick(self_in_weight, m * D + s * hw, hw) for m in range(3)], axis=1
        )
        chunk_mid = jnp.concatenate(
            [pick(memory_weight, m * D + s * hw, hw) for m in range(2)]
            + [pick(cross_query_weight, s * hw, hw)],
            axis=1,
        )
        chunk_out = jnp.concatenate(
            [
                lax.dynamic_slice_in_dim(w, s * part, part, 0)
                for w in (self_out_weight, cross_out_weight)
            ],
            axis=0,
        )
        chunk_fin = lax.dynamic_index_in_dim(
            ffn_in_weight.reshape(shard, F, S, fw), s, 2, keepdims=False
        ).reshape(shard, F * fw)
        chunk_fout = lax.dynamic_slice_in_dim(ffn_out_weight, s * fw, fw, 0)

        got_qkv = fsdp_gather(chunk_qkv)
        x_blocks = seq_gather(hidden_in)
        got_mid = fsdp_gather(after(chunk_mid, got_qkv[-1]))
        m_blocks = seq_gather(after(memory, x_blocks[-1]))
        got_out = fsdp_gather(after(chunk_out, got_qkv[-1]))
        got_fin = fsdp_gather(after(chunk_fin, got_mid[-1]))
        got_fout = fsdp_gather(after(chunk_fout, got_fin[-1]))

        w_qkv = fsdp_place(got_qkv)
        block_moves = [
            (n, 0, t, 0, D, seq_of(k, e) * t, 0) for n, (k, e) in enumerate(relative)
        ]
        x_all = assemble(x_blocks, block_moves, (T, D))
        qkv_bias = jnp.concatenate([group_row(b_query), jnp.zeros((hw,), f32), group_row(b_value)])
        qkv = (dot(x_all, w_qkv, nn) + qkv_bias).astype(bf16)
        q_self, k_self, v_self = (qkv[:, m * hw : (m + 1) * hw] for m in range(3))
        self_attn, self_lse = attend_forward(q_self, k_self, v_self, lengths, True)

        w_mid = fsdp_place(got_mid)
        w_mem, cq_quarter = w_mid[:, : 2 * hw], w_mid[:, 2 * hw :]
        m_all = jnp.concatenate(m_blocks, axis=0)
        mem_bias = jnp.concatenate([jnp.zeros((hw,), f32), group_row(b_mem_value)])
        kv_mem = (dot(m_all, w_mem, nn) + mem_bias).astype(bf16)

        def all_rows(parts_of):
            return assemble(
                parts_of,
                [(n, 0, t, 0, hw, 0, seq_of(k, e) * hw) for n, (k, e) in enumerate(relative)],
                (t, D),
            )

        def heads_to_rows(array):
            blocks = array.reshape(S, t, hw)
            mine = []
            for k, e in relative:
                target = lax.rem(y + k, Y) * CORES + (c if e == 0 else 1 - c)
                sent = lax.dynamic_index_in_dim(blocks, target, 0, keepdims=False)
                sent = y_shift(sent, k)
                mine.append(core_swap(sent) if e else sent)
            return all_rows(mine)

        def rows_to_heads(array):
            mine = []
            for k, e in relative:
                target = lax.rem(y + k, Y) * CORES + (c if e == 0 else 1 - c)
                sent = y_shift(pick(array, target * hw, hw), k)
                mine.append(core_swap(sent) if e else sent)
            return assemble(
                mine,
                [(n, 0, t, 0, hw, seq_of(k, e) * t, 0) for n, (k, e) in enumerate(relative)],
                (T, hw),
            )

        attn_tok = heads_to_rows(self_attn)
        mem_chips = [y_shift(kv_mem, k) for k in range(Y)]
        mem_key = jnp.concatenate([m[:, :hw] for m in mem_chips], axis=1)
        mem_value = jnp.concatenate([m[:, hw:] for m in mem_chips], axis=1)

        out_quarter = fsdp_place(got_out)
        out_pieces = seq_gather(out_quarter)
        own_moves = [[], []]
        for n, (k, e) in enumerate(relative):
            for which in range(2):
                for shard_index in range(F):
                    own_moves[which].append(
                        (
                            n, shard_index * 2 * part + which * part, part, 0, D,
                            shard_index * shard + seq_of(k, e) * part, 0,
                        )
                    )
        w_attn_out = assemble(out_pieces, own_moves[0], (D, D))
        w_cross_out = assemble(out_pieces, own_moves[1], (D, D))
        cq_pieces = seq_gather(cq_quarter)
        w_cross_q = jnp.concatenate(cq_pieces, axis=1)
        b_cq = jnp.concatenate(
            [lax.dynamic_slice_in_dim(b_cross_q, seq_of(k, e) * hw, hw, 0) for k, e in relative]
        )
        half = Y * hw

        x_float = hidden_in.astype(f32)
        branch = dot(attn_tok, w_attn_out, nn) + b_attn_out
        first, normed_one, inverse_one = layer_norm(
            alpha_scale * x_float + branch, gains[0], shifts[0]
        )
        first_low = first.astype(bf16)
        cq_rows = (dot(first_low, w_cross_q, nn) + b_cq).astype(bf16)

        cross_q = jnp.concatenate([cq_rows[:, :half], core_swap(cq_rows[:, half:])], axis=0)
        cross_attn, cross_lse = attend_forward(cross_q, mem_key, mem_value, lengths, False)
        cross_other = core_swap(cross_attn[t:])
        cross_tok = assemble(
            [cross_attn, cross_other],
            [(e, 0, t, k * hw, hw, 0, seq_of(k, e) * hw) for k, e in relative],
            (t, D),
        )
        cross_branch = dot(cross_tok, w_cross_out, nn) + b_cross_out
        second, normed_two, inverse_two = layer_norm(
            alpha_scale * first + cross_branch, gains[1], shifts[1]
        )
        second_low = second.astype(bf16)

        w_fin = fsdp_place(got_fin)
        w_fout = fsdp_place(got_fout)
        second_all = jnp.concatenate(seq_gather(second_low), axis=0)
        pre_act = dot(second_all, w_fin, nn) + b_ffn_in
        act_value, act_slope = gelu_both(pre_act)
        hidden_low = act_value.astype(bf16)
        ffn_part = dot(hidden_low, w_fout, nn)

        def by_owner(array):
            return {ke: array[n * t : (n + 1) * t] for n, ke in enumerate(relative)}

        ffn_branch = seq_scatter(by_owner(ffn_part)) + b_ffn_out
        result, normed_three, inverse_three = layer_norm(
            alpha_scale * second + ffn_branch, gains[2], shifts[2]
        )
        layer_out = result.astype(bf16)

        d_three, gain_three, shift_three = norm_back(
            out_grad.astype(f32), normed_three, inverse_three, gains[2]
        )
        d_ffn = d_three.astype(bf16)
        d_ffn_all = jnp.concatenate(seq_gather(d_ffn), axis=0)
        d_hidden = dot(d_ffn_all, w_fout, nt)
        d_pre = (act_slope * d_hidden).astype(bf16)
        d_second_part = dot(d_pre, w_fin, nt)
        d_second = alpha_scale * d_three + seq_scatter(by_owner(d_second_part))
        grad_fout = dot(hidden_low, d_ffn_all, tn).astype(bf16)
        own_fout = fsdp_scatter(grad_fout)
        grad_fin = dot(second_all, d_pre, tn).astype(bf16)
        own_fin = fsdp_scatter(grad_fin)

        d_two, gain_two, shift_two = norm_back(d_second, normed_two, inverse_two, gains[1])
        d_cross = d_two.astype(bf16)
        d_cross_tok = dot(d_cross, w_cross_out, nt).astype(bf16)
        keep, send = (
            jnp.concatenate([pick(d_cross_tok, seq_of(k, e) * hw, hw) for k in range(Y)], axis=1)
            for e in range(CORES)
        )
        d_cross_heads = jnp.concatenate([keep, core_swap(send)], axis=0)
        dq_cross, dk_mem, dv_mem = attend_back(
            cross_q, mem_key, mem_value, d_cross_heads, cross_lse, lengths, False
        )
        d_cq_rows = jnp.concatenate([dq_cross[:t], core_swap(dq_cross[t:])], axis=1)
        d_first = alpha_scale * d_two + dot(d_cq_rows, w_cross_q, nt)
        grad_cross_out = dot(cross_tok, d_cross, tn)
        grad_cq = dot(first_low, d_cq_rows, tn)
        d_mem = None
        for k in range(Y):
            sent = jnp.concatenate([d[:, k * hw : (k + 1) * hw] for d in (dk_mem, dv_mem)], axis=1)
            got = y_shift(sent, -k).astype(f32)
            d_mem = got if d_mem is None else d_mem + got
        d_mem = d_mem.astype(bf16)
        grad_mem = dot(m_all, d_mem, tn).astype(bf16)
        memory_grad = seq_scatter(by_owner(dot(d_mem, w_mem, nt))).astype(bf16)

        d_one, gain_one, shift_one = norm_back(d_first, normed_one, inverse_one, gains[0])
        d_branch = d_one.astype(bf16)
        d_attn_heads = rows_to_heads(dot(d_branch, w_attn_out, nt).astype(bf16))
        grad_self_out = dot(attn_tok, d_branch, tn)
        dq_self, dk_self, dv_self = attend_back(
            q_self, k_self, v_self, d_attn_heads, self_lse, lengths, True
        )
        d_qkv = jnp.concatenate([dq_self, dk_self, dv_self], axis=1)
        grad_qkv = dot(x_all, d_qkv, tn).astype(bf16)
        own_qkv = fsdp_scatter(grad_qkv)
        input_part = dot(d_qkv, w_qkv, nt).reshape(S, t, D)
        input_sum = seq_scatter(
            {
                (k, e): lax.dynamic_index_in_dim(input_part, seq_of(k, e), 0, keepdims=False)
                for k, e in relative
            }
        )
        input_grad = (alpha_scale * d_one + input_sum).astype(bf16)

        def out_parts(grad):
            view = grad.astype(bf16).reshape(F, S, part, D)
            return {
                (k, e): lax.dynamic_index_in_dim(view, seq_of(k, e), 1, keepdims=False)
                for k, e in relative
            }

        own_cross_out = seq_scatter(out_parts(grad_cross_out)).astype(bf16)
        own_self_out = seq_scatter(out_parts(grad_self_out)).astype(bf16)
        own_cq = seq_scatter(
            {ke: grad_cq[:, n * hw : (n + 1) * hw] for n, ke in enumerate(relative)}
        ).astype(bf16)
        own_mid = fsdp_scatter(jnp.concatenate([grad_mem, own_cq], axis=1))
        own_out = fsdp_scatter(
            jnp.concatenate([own_self_out, own_cross_out], axis=1).reshape(F * 2 * part, D)
        )

        all_fout = finish(own_fout).reshape(S * fw, D)
        all_fin = (
            finish(own_fin).reshape(S, shard, F, fw).transpose(1, 2, 0, 3).reshape(shard, FF)
        )
        all_mid = finish(own_mid)
        all_mem = (
            all_mid[:, :, : 2 * hw]
            .reshape(S, shard, 2, hw)
            .transpose(1, 2, 0, 3)
            .reshape(shard, 2 * D)
        )
        all_cq = all_mid[:, :, 2 * hw :].transpose(1, 0, 2).reshape(shard, D)
        all_out = finish(own_out).reshape(S, 2, part, D)
        all_self_out = all_out[:, 0].reshape(shard, D)
        all_cross_out = all_out[:, 1].reshape(shard, D)
        all_qkv = (
            finish(own_qkv).reshape(S, shard, 3, hw).transpose(1, 2, 0, 3).reshape(shard, 3 * D)
        )

        def spread(row):
            return lax.dynamic_update_slice_in_dim(jnp.zeros((D,), f32), row, s * hw, 0)

        d_cq_sum = column_sum(d_cq_rows)
        cq_bias = jnp.zeros((D,), f32)
        for n, (k, e) in enumerate(relative):
            cq_bias = lax.dynamic_update_slice_in_dim(
                cq_bias, d_cq_sum[n * hw : (n + 1) * hw], seq_of(k, e) * hw, 0
            )
        fin_bias = lax.dynamic_update_slice_in_dim(
            jnp.zeros((F, S, fw), f32), column_sum(d_pre).reshape(F, 1, fw), s, 1
        ).reshape(F, S * fw)
        small_grads = jnp.concatenate(
            [
                row.reshape(F, shard)
                for row in (
                    spread(column_sum(dq_self)), spread(column_sum(dv_self)), column_sum(d_branch),
                    cq_bias, spread(column_sum(d_mem[:, hw:])), column_sum(d_cross),
                    column_sum(d_ffn), gain_one, gain_two, gain_three, shift_one, shift_two,
                    shift_three,
                )
            ]
            + [fin_bias],
            axis=1,
        )
        small_own = jnp.sum(lax.all_to_all(small_grads, "fsdp", 0, 0, tiled=True), axis=0)
        small_own = lax.psum(small_own, "seq")
        rows = [small_own[n * shard : (n + 1) * shard] for n in range(13)]
        return (
            layer_out[None],
            input_grad[None],
            memory_grad[None],
            all_qkv,
            rows[0],
            rows[1],
            all_self_out,
            rows[2],
            all_cq,
            rows[3],
            all_mem,
            rows[4],
            all_cross_out,
            rows[5],
            all_fin,
            small_own[13 * shard :],
            all_fout,
            rows[6],
            jnp.stack(rows[7:10]),
            jnp.stack(rows[10:13]),
        )

    return local


short = pl.CostEstimate(flops=1024, bytes_accessed=1024, transcendentals=0)

small_rows = 24


def hbm(array):
    return ("hbm", array)


def stage(body, where, ins, outs, scratch=(), limit=vmem_limit):
    specs, arrays = [], []
    for item in ins:
        if isinstance(item, tuple):
            specs.append(pl.BlockSpec(memory_space=pl.ANY))
            arrays.append(item[1])
        else:
            specs.append(pl.BlockSpec(memory_space=pltpu.VMEM))
            arrays.append(item)
    n_in, n_out = len(arrays), len(outs)

    def kernel(w, *refs):
        body(w, refs[:n_in], refs[n_in : n_in + n_out], refs[n_in + n_out :])

    return pl.pallas_call(
        kernel,
        grid_spec=pltpu.PrefetchScalarGridSpec(
            num_scalar_prefetch=1,
            grid=(1,),
            in_specs=specs,
            out_specs=[pl.BlockSpec(memory_space=pltpu.VMEM)] * n_out,
            scratch_shapes=list(scratch),
        ),
        out_shape=[jax.ShapeDtypeStruct(shape, dtype) for shape, dtype in outs],
        compiler_params=pltpu.CompilerParams(vmem_limit_bytes=limit),
        cost_estimate=short,
    )(where, *arrays)


class Copies:
    def __init__(self, sems):
        self.sems, self.list = sems, []

    def add(self, source, target):
        copy = pltpu.make_async_copy(source, target, self.sems.at[len(self.list)])
        copy.start()
        self.list.append(copy)
        return copy

    def wait(self):
        for copy in self.list:
            copy.wait()
        self.list = []


def span(index, size):
    return pl.ds(pl.multiple_of(index * size, size), size)


def norm_rows(values, gain_row, shift_row):
    center = values - jnp.mean(values, axis=-1, keepdims=True)
    inverse = lax.rsqrt(jnp.mean(center * center, axis=-1, keepdims=True) + layer_eps)
    normed = center * inverse
    return normed * gain_row + shift_row, normed, inverse


def norm_rows_back(grad_rows, normed, inverse, gain_row):
    scaled = grad_rows * gain_row
    inner = scaled - jnp.mean(scaled, axis=-1, keepdims=True)
    inner = inner - normed * jnp.mean(scaled * normed, axis=-1, keepdims=True)
    return (
        inverse * inner,
        jnp.sum(grad_rows * normed, axis=0, keepdims=True),
        jnp.sum(grad_rows, axis=0, keepdims=True),
    )


def row_sum(array):
    return jnp.sum(array.astype(f32), axis=0, keepdims=True)


def tiled_layer(mesh):
    S, F = mesh.shape["seq"], mesh.shape["fsdp"]
    Z = 4 if F % 4 == 0 else 1
    X = F // Z
    SEQ, MINE, AT_X, LENGTH = 0, S, S + 1, S + 2

    core_perm = [(n, n ^ 1) for n in range(S)]
    y_perm = [(n, n ^ 2) for n in range(S)]

    def core_swap(array):
        return lax.ppermute(array, "seq", core_perm)

    def y_swap(array):
        return lax.ppermute(array, "seq", y_perm)

    z_groups = [[z * X + x for z in range(Z)] for x in range(X)]

    def z_exchange(array):
        return lax.all_to_all(array, "fsdp", 0, 0, axis_index_groups=z_groups, tiled=True)

    def x_shift(array, k):
        perm = [(z * X + x, z * X + (x + k) % X) for z in range(Z) for x in range(X)]
        return lax.ppermute(array, "fsdp", perm) if k % X else array

    def seq_gather(array):
        far = y_swap(array)
        return [array, far, core_swap(array), core_swap(far)]

    def tied(values):
        return lax.optimization_barrier(list(values))

    def z_gather(copies):
        return z_exchange(copies)

    def x_gather(column):
        rows, cols = column.shape[0] // Z, column.shape[1]
        return [a.reshape(Z, rows, cols) for a in (column, x_shift(column, 1))]

    def heads_to_positions(array):
        return lax.all_to_all(array, "seq", 0, 0, tiled=True)

    def local(
        hidden_in,
        memory,
        lengths,
        out_grad,
        self_in_weight,
        self_query_bias,
        self_value_bias,
        self_out_weight,
        self_out_bias,
        cross_query_weight,
        cross_query_bias,
        memory_weight,
        memory_value_bias,
        cross_out_weight,
        cross_out_bias,
        ffn_in_weight,
        ffn_in_bias,
        ffn_out_weight,
        ffn_out_bias,
        norm_gain,
        norm_bias,
    ):
        s, f = lax.axis_index("seq"), lax.axis_index("fsdp")
        z, x = f // X, f % X
        _, t, D = hidden_in.shape
        T = S * t
        hw = D // S
        FF = ffn_in_weight.shape[1]
        shard = D // F
        fw = FF // (F * S)
        half = 2 * hw
        per_group = hw // shard
        part = shard // S
        deep = shard // 2
        rest_cols = D + half
        hidden_in, memory, out_grad = hidden_in[0], memory[0], out_grad[0]
        where = jnp.stack(
            [s, s ^ 2, s ^ 1, s ^ 3, s, x, lengths[0]]
        ).astype(jnp.int32)

        def prepare_qkv(w, ins, outs, _):
            weight, out = ins[0], outs[0]
            me = w[MINE]
            for m in range(3):
                lanes = pl.ds(pl.multiple_of(m * D + me * hw, hw), hw)
                for k in range(Z):
                    out[k, 0:shard, m * hw : (m + 1) * hw] = weight[:, lanes]
            rows = [ins[n][...].reshape(1, shard) for n in range(1, 8)]
            rows += [ins[8][...], ins[9][...]]
            rows += [
                ins[10][n * fw : (n + 1) * fw].reshape(1, fw) for n in range(S)
            ]
            packed = jnp.concatenate([r.astype(f32) for r in rows], axis=0)
            first = packed[0:16].astype(bf16)
            rest = jnp.concatenate(
                [packed[16:], jnp.zeros((32 - packed.shape[0], shard), f32)], axis=0
            ).astype(bf16)
            below = jnp.concatenate(
                [first, rest, jnp.zeros((16, 3 * hw - 2 * shard), bf16)], axis=1
            )
            for k in range(Z):
                out[k, shard : shard + 16, :] = below

        (chunk_qkv,) = stage(
            prepare_qkv,
            where,
            [
                self_in_weight, self_query_bias, self_value_bias, self_out_bias, cross_query_bias,
                memory_value_bias, cross_out_bias, ffn_out_bias, norm_gain, norm_bias, ffn_in_bias,
            ],
            [((Z, shard + 16, 3 * hw), bf16)],
        )

        def prepare_rest(w, ins, outs, _):
            query, own, cross = ins
            out = outs[0]
            core = lax.rem(w[MINE], 2)
            out[0:deep, 0:D] = own[span(core, deep), :]
            out[deep:, 0:D] = cross[span(core, deep), :]
            out[:, D : D + hw] = query[:, span(w[SEQ], hw)]
            out[:, D + hw :] = query[:, span(w[SEQ + 1], hw)]

        (chunk_rest,) = stage(
            prepare_rest,
            where,
            [cross_query_weight, self_out_weight, cross_out_weight],
            [((shard, rest_cols), bf16)],
        )

        def prepare_mem(w, ins, outs, _):
            for m in range(2):
                lanes = pl.ds(pl.multiple_of(m * D + w[MINE] * hw, hw), hw)
                for k in range(Z):
                    outs[0][k, :, m * hw : (m + 1) * hw] = ins[0][:, lanes]

        (chunk_mem,) = stage(prepare_mem, where, [memory_weight], [((Z, shard, 2 * hw), bf16)])

        def prepare_ffn(w, ins, outs, _):
            me = w[MINE]
            for n in range(F):
                lanes = pl.ds(pl.multiple_of(n * S * fw + me * fw, fw), fw)
                outs[0][0:shard, n * fw : (n + 1) * fw] = ins[0][:, lanes]
            outs[0][shard:, :] = ins[1][span(me, fw), :]

        (chunk_ffn,) = stage(
            prepare_ffn, where, [ffn_in_weight, ffn_out_weight], [((shard + fw, D), bf16)]
        )

        hidden_far = y_swap(after(hidden_in, chunk_qkv))
        z_qkv = z_gather(chunk_qkv.reshape(Z * (shard + 16), 3 * hw))
        z_qkv, hidden_far, chunk_rest, chunk_mem, chunk_ffn = tied(
            [z_qkv, hidden_far, chunk_rest, chunk_mem, chunk_ffn]
        )
        rest_own = lax.all_gather(chunk_rest, "fsdp", axis=0, tiled=True)
        x_blocks = [hidden_in, hidden_far, core_swap(hidden_in), core_swap(hidden_far)]
        got_qkv = x_gather(z_qkv)
        memory_far = y_swap(after(memory, hidden_far))
        z_mem = z_gather(after(chunk_mem, z_qkv).reshape(Z * shard, 2 * hw))
        got_qkv[0], z_mem, memory_far = tied([got_qkv[0], z_mem, memory_far])
        m_blocks = [memory, memory_far, core_swap(memory), core_swap(memory_far)]
        got_mem = x_gather(z_mem)

        def project_qkv(w, ins, outs, scratch):
            blocks, pieces = ins[:S], ins[S:]
            qkv, small = outs
            x_all, weight, packed, sems = scratch
            copies = Copies(sems)
            for k in range(2):
                at = w[AT_X] if k == 0 else 1 - w[AT_X]
                copies.add(pieces[k].at[:, pl.ds(0, shard)], weight.at[:, at])
                copies.add(pieces[k].at[:, pl.ds(shard, 16), pl.ds(0, 2 * shard)], packed.at[:, at])
            for n in range(S):
                copies.add(blocks[n], x_all.at[span(w[SEQ + n], t)])
            copies.wait()
            small[...] = jnp.zeros_like(small)
            for n in range(F):
                lanes = slice(n * shard, (n + 1) * shard)
                small[0:16, lanes] = packed[n // X, n % X, :, 0:shard].astype(f32)
                small[16:24, lanes] = packed[n // X, n % X, 0:8, shard : 2 * shard].astype(f32)
            mine = span(w[MINE], hw)
            biases = [small[0:1, mine], jnp.zeros((1, hw), f32), small[1:2, mine]]
            for n in range(S):
                rows = slice(n * t, (n + 1) * t)
                for m in range(3):
                    cols = slice(m * hw, (m + 1) * hw)
                    value = dot(x_all[rows, :], weight[..., cols].reshape(D, hw), nn) + biases[m]
                    qkv[rows, cols] = value.astype(bf16)

        qkv, small = stage(
            project_qkv,
            where,
            [hbm(b) for b in x_blocks] + [hbm(p) for p in got_qkv],
            [((T, 3 * hw), bf16), ((small_rows, D), f32)],
            [
                pltpu.VMEM((T, D), bf16),
                pltpu.VMEM((Z, X, shard, 3 * hw), bf16),
                pltpu.VMEM((Z, X, 16, 2 * shard), bf16),
                pltpu.SemaphoreType.DMA((4 + S,)),
            ],
        )

        pairs = hw // (2 * HD)
        pair = 2 * HD

        def qkv_spec(m):
            return pl.BlockSpec((T, pair), lambda g, i, _: (0, m * pairs + g))

        def self_forward(w, q_ref, k_ref, v_ref, o_ref, lse_ref):
            i = pl.program_id(1)
            limit = jnp.minimum(w[LENGTH], (i + 1) * BLK)

            def visit(key_count):
                parts, lses = [], []
                for h in range(2):
                    cols = slice(h * HD, (h + 1) * HD)
                    query = q_ref[:, cols] * jnp.asarray(score_scale, bf16)
                    scores = mask_scores(dot(k_ref[:key_count, cols], query, nt), 0, limit)
                    top = jnp.max(scores, axis=0, keepdims=True)
                    weights = jnp.exp(scores - top)
                    totals = jnp.sum(weights, axis=0, keepdims=True)
                    low = (weights * (1.0 / totals)).astype(bf16)
                    parts.append(dot(low, v_ref[:key_count, cols], tn).astype(bf16))
                    lses.append(top + jnp.log(totals))
                o_ref[...] = jnp.concatenate(parts, axis=1)
                lse_ref[0] = jnp.concatenate(lses, axis=0)

            key_cases(T, True, i, visit)

        q_block = pl.BlockSpec((t, pair), lambda g, i, _: (i, g))
        row_block = pl.BlockSpec((t, pair), lambda g, i, _: (0, g))
        lse_block = pl.BlockSpec((1, 2, t), lambda g, i, _: (g, 0, i))
        self_attn, self_lse = pl.pallas_call(
            self_forward,
            grid_spec=pltpu.PrefetchScalarGridSpec(
                num_scalar_prefetch=1,
                grid=(pairs, S),
                in_specs=[q_block, qkv_spec(1), qkv_spec(2)],
                out_specs=[q_block, lse_block],
            ),
            out_shape=[
                jax.ShapeDtypeStruct((T, hw), bf16),
                jax.ShapeDtypeStruct((pairs, 2, T), f32),
            ],
            compiler_params=pltpu.CompilerParams(vmem_limit_bytes=vmem_limit),
            cost_estimate=short,
        )(where, qkv, qkv, qkv)
        attn = heads_to_positions(self_attn)
        rest_own = after(rest_own, self_attn)
        rest_other = core_swap(rest_own)
        rest = [r.reshape(F, shard, rest_cols) for r in (rest_own, rest_other)]

        w_ffn = lax.all_gather(after(chunk_ffn, qkv), "fsdp", axis=0, tiled=True).reshape(
            F, shard + fw, D
        )
        def project_memory(w, ins, outs, scratch):
            blocks, pieces, small_ref = ins[:S], ins[S : S + 2], ins[S + 2]
            kv, weight = outs
            m_all, sems = scratch
            copies = Copies(sems)
            for k in range(2):
                copies.add(pieces[k], weight.at[:, w[AT_X] if k == 0 else 1 - w[AT_X]])
            for n in range(S):
                copies.add(blocks[n], m_all.at[pl.ds(n * t, t)])
            copies.wait()
            bias = jnp.concatenate(
                [jnp.zeros((1, hw), f32), small_ref[4:5, span(w[MINE], hw)]], axis=1
            )
            for n in range(S):
                rows = slice(n * t, (n + 1) * t)
                value = dot(m_all[rows, :], weight[...].reshape(D, 2 * hw), nn) + bias
                kv[rows, :] = value.astype(bf16)

        kv_own, w_mem = stage(
            project_memory,
            where,
            [hbm(b) for b in m_blocks] + [hbm(p) for p in got_mem] + [after(small, attn)],
            [((T, 2 * hw), bf16), ((Z, X, shard, 2 * hw), bf16)],
            [pltpu.VMEM((T, D), bf16), pltpu.SemaphoreType.DMA((2 + S,))],
        )
        w_mem = w_mem.reshape(D, 2 * hw)
        kv_far = y_swap(kv_own)

        def load_out(copies, w, rest_refs, which, target):
            core = lax.rem(w[MINE], 2)
            for e in range(2):
                copies.add(
                    rest_refs[e].at[:, pl.ds(which * deep, deep), pl.ds(0, D)],
                    target.at[:, core if e == 0 else 1 - core],
                )

        def group_rows(weight, group):
            return weight[pl.ds(group * per_group, per_group)].reshape(hw, D)

        out_scratch = pltpu.VMEM((F, 2, deep, D), bf16)
        cq_scratch = pltpu.VMEM((2, F, shard, half), bf16)

        def first_stage(w, ins, outs, scratch):
            attn_ref, rest_refs, x_ref, small_ref = ins[0], ins[1:3], ins[3], ins[4]
            normed_ref, inverse_ref, low_ref, keep_ref, send_ref = outs
            weight, cq, sems = scratch
            copies = Copies(sems)
            load_out(copies, w, rest_refs, 0, weight)
            for e in range(2):
                copies.add(rest_refs[e].at[:, :, pl.ds(D, half)], cq.at[e])
            copies.wait()
            total = alpha_scale * x_ref[...].astype(f32) + small_ref[2:3, :]
            for n in range(S):
                total = total + dot(attn_ref[n * t : (n + 1) * t, :], group_rows(weight, n), nn)
            value, normed, inverse = norm_rows(total, small_ref[7:8, :], small_ref[10:11, :])
            normed_ref[...] = normed
            inverse_ref[...] = inverse
            low = value.astype(bf16)
            low_ref[...] = low
            for e, target in ((1, send_ref), (0, keep_ref)):
                bias = jnp.concatenate(
                    [small_ref[3:4, span(w[SEQ + 2 * e + k], hw)] for k in range(2)], axis=1
                )
                target[...] = (dot(low, cq[e].reshape(D, half), nn) + bias).astype(bf16)

        normed_one, inverse_one, first_low, cq_keep, cq_send = stage(
            first_stage,
            where,
            [attn] + [hbm(r) for r in rest] + [hidden_in, small],
            [
                ((t, D), f32), ((t, 1), f32), ((t, D), bf16), ((t, half), bf16), ((t, half), bf16),
            ],
            [out_scratch, cq_scratch, pltpu.SemaphoreType.DMA((4,))],
        )
        cq_other = core_swap(cq_send)

        def kv_specs():
            near = [
                pl.BlockSpec((T, pair), lambda g, i, _, m=m: (0, m * pairs + jnp.minimum(g, pairs - 1)))
                for m in range(2)
            ]
            far = [
                pl.BlockSpec((T, pair), lambda g, i, _, m=m: (0, m * pairs + jnp.maximum(g - pairs, 0)))
                for m in range(2)
            ]
            return near + far

        cross_lse_block = pl.BlockSpec((1, 2, t), lambda g, i, _: (g, 0, i))

        def cross_forward(w, qa_ref, qb_ref, k0, v0, k1, v1, oa_ref, ob_ref, lse_ref):
            g, i = pl.program_id(0), pl.program_id(1)

            def run(q_ref, k_ref, v_ref, o_ref):
                parts, lses = [], []
                for h in range(2):
                    cols = slice(h * HD, (h + 1) * HD)
                    query = q_ref[:, cols] * jnp.asarray(score_scale, bf16)
                    scores = dot(k_ref[:, cols], query, nt)
                    top = jnp.max(scores, axis=0, keepdims=True)
                    weights = jnp.exp(scores - top)
                    totals = jnp.sum(weights, axis=0, keepdims=True)
                    low = (weights * (1.0 / totals)).astype(bf16)
                    parts.append(dot(low, v_ref[:, cols], tn).astype(bf16))
                    lses.append(top + jnp.log(totals))
                o_ref[...] = jnp.concatenate(parts, axis=1)
                lse_ref[0] = jnp.concatenate(lses, axis=0)

            for gi, (k_ref, v_ref) in enumerate(((k0, v0), (k1, v1))):
                for qi, (q_ref, o_ref) in enumerate(((qa_ref, oa_ref), (qb_ref, ob_ref))):

                    @pl.when((g // pairs == gi) & (i == qi))
                    def _(q_ref=q_ref, k_ref=k_ref, v_ref=v_ref, o_ref=o_ref):
                        run(q_ref, k_ref, v_ref, o_ref)

        cross_keep, cross_send, cross_lse = pl.pallas_call(
            cross_forward,
            grid_spec=pltpu.PrefetchScalarGridSpec(
                num_scalar_prefetch=1,
                grid=(2 * pairs, 2),
                in_specs=[row_block, row_block] + kv_specs(),
                out_specs=[row_block, row_block, cross_lse_block],
            ),
            out_shape=[jax.ShapeDtypeStruct((t, half), bf16)] * 2
            + [jax.ShapeDtypeStruct((2 * pairs, 2, 2 * t), f32)],
            compiler_params=pltpu.CompilerParams(vmem_limit_bytes=vmem_limit),
            cost_estimate=short,
        )(where, cq_keep, cq_other, kv_own, kv_own, kv_far, kv_far)
        cross_other = core_swap(cross_send)

        def halves(keep_ref, other_ref):
            return [
                ref[:, h * hw : (h + 1) * hw] for ref in (keep_ref, other_ref) for h in range(2)
            ]

        def second_stage(w, ins, outs, scratch):
            keep_ref, other_ref, normed_one_ref, small_ref = ins[:4]
            rest_refs = ins[4:]
            normed_ref, inverse_ref, low_ref = outs
            weight, sems = scratch
            copies = Copies(sems)
            load_out(copies, w, rest_refs, 1, weight)
            copies.wait()
            first = normed_one_ref[...] * small_ref[7:8, :] + small_ref[10:11, :]
            total = alpha_scale * first + small_ref[5:6, :]
            for n, piece in enumerate(halves(keep_ref, other_ref)):
                total = total + dot(piece, group_rows(weight, w[SEQ + n]), nn)
            value, normed, inverse = norm_rows(total, small_ref[8:9, :], small_ref[11:12, :])
            normed_ref[...] = normed
            inverse_ref[...] = inverse
            low_ref[...] = value.astype(bf16)

        normed_two, inverse_two, second_low = stage(
            second_stage,
            where,
            [cross_keep, cross_other, normed_one, small] + [hbm(r) for r in rest],
            [((t, D), f32), ((t, 1), f32), ((t, D), bf16)],
            [out_scratch, pltpu.SemaphoreType.DMA((2,))],
        )
        second = seq_gather(second_low)

        ffn_scratch = [
            pltpu.VMEM((F, shard, D), bf16),
            pltpu.VMEM((F, fw, D), bf16),
            pltpu.SemaphoreType.DMA((2,)),
        ]

        def load_ffn(w_ref, scratch):
            copies = Copies(scratch[2])
            copies.add(w_ref.at[:, pl.ds(0, shard)], scratch[0])
            copies.add(w_ref.at[:, pl.ds(shard, fw)], scratch[1])
            copies.wait()
            return scratch[0], scratch[1]

        def ffn_forward(w, ins, outs, scratch):
            block_refs, small_ref, w_ref = ins[:2], ins[2], ins[3]
            part_refs, hidden_ref, slope_ref = outs[:2], outs[2], outs[3]
            w_in, w_out = load_ffn(w_ref, scratch)
            bias = small_ref[pl.ds(13 + w[MINE], 1), :]
            for n in range(2):
                rows = slice(n * t, (n + 1) * t)
                pre = dot(block_refs[n][...], w_in[...].reshape(D, F * fw), nn) + bias
                value, slope = gelu_both(pre)
                low = value.astype(bf16)
                hidden_ref[rows, :] = low
                slope_ref[rows, :] = slope.astype(bf16)
                out = dot(low, w_out[...].reshape(F * fw, D), nn)
                part_refs[n][...] = out.astype(part_refs[n].dtype)

        def ffn_call(blocks):
            return stage(
                ffn_forward,
                where,
                blocks + [small, hbm(w_ffn)],
                [((t, D), bf16), ((t, D), bf16), ((2 * t, F * fw), bf16), ((2 * t, F * fw), bf16)],
                ffn_scratch,
            )

        ffn_part_0, ffn_part_2, hidden_a, slope_a = ffn_call([second[0], second[2]])
        ffn_near = core_swap(ffn_part_2)
        ffn_part_1, ffn_part_3, hidden_b, slope_b = ffn_call([second[1], second[3]])

        def add_pair(left, right):
            return (left.astype(f32) + right.astype(f32)).astype(bf16)

        ffn_far = y_swap(add_pair(ffn_part_1, core_swap(ffn_part_3)))

        def third_stage(w, ins, outs, _):
            a, b, far, normed_two_ref, small_ref, grad_ref = ins
            out_ref, d_ref, low_ref, sums_ref = outs
            second_rows = normed_two_ref[...] * small_ref[8:9, :] + small_ref[11:12, :]
            branch = a[...].astype(f32) + b[...].astype(f32) + far[...].astype(f32)
            total = alpha_scale * second_rows + branch + small_ref[6:7, :]
            value, normed, inverse = norm_rows(total, small_ref[9:10, :], small_ref[12:13, :])
            out_ref[...] = value.astype(bf16)
            d, gain, shift = norm_rows_back(
                grad_ref[...].astype(f32), normed, inverse, small_ref[9:10, :]
            )
            d_ref[...] = d
            low = d.astype(bf16)
            low_ref[...] = low
            sums_ref[0:1, :] = row_sum(low)
            sums_ref[1:2, :] = gain
            sums_ref[2:3, :] = shift

        layer_out, d_three, d_ffn_own, sums_three = stage(
            third_stage,
            where,
            [ffn_part_0, ffn_near, ffn_far, normed_two, small, out_grad],
            [((t, D), bf16), ((t, D), f32), ((t, D), bf16), ((8, D), f32)],
        )
        d_ffn = seq_gather(d_ffn_own)

        def ffn_backward(w, ins, outs, scratch):
            block_refs, slope_ref, w_ref = ins[:2], ins[2], ins[3]
            part_refs, d_pre_ref = outs[:2], outs[2]
            w_in, w_out = load_ffn(w_ref, scratch)
            for n in range(2):
                rows = slice(n * t, (n + 1) * t)
                d_hidden = dot(block_refs[n][...], w_out[...].reshape(F * fw, D), nt)
                d_pre = (slope_ref[rows, :].astype(f32) * d_hidden).astype(bf16)
                d_pre_ref[rows, :] = d_pre
                out = dot(d_pre, w_in[...].reshape(D, F * fw), nt)
                part_refs[n][...] = out.astype(bf16)

        def ffn_back_call(blocks, slope):
            return stage(
                ffn_backward,
                where,
                blocks + [slope, hbm(w_ffn)],
                [((t, D), bf16), ((t, D), bf16), ((2 * t, F * fw), bf16)],
                ffn_scratch,
            )

        d2_part_0, d2_part_2, d_pre_a = ffn_back_call([d_ffn[0], d_ffn[2]], slope_a)
        d2_near = core_swap(d2_part_2)
        d2_part_1, d2_part_3, d_pre_b = ffn_back_call([d_ffn[1], d_ffn[3]], slope_b)
        d2_sent = add_pair(d2_part_1, core_swap(d2_part_3))
        d2_far = y_swap(d2_sent)

        def ffn_grads(w, ins, outs, scratch):
            x_refs, g_refs, hidden_a_ref, hidden_b_ref, pre_a_ref, pre_b_ref = (
                ins[0:4], ins[4:8], *ins[8:12],
            )
            grads, sums_ref = outs
            x_rows, g_rows = scratch
            for n in range(S):
                at = (0, 2, 1, 3)[n] * t
                x_rows[at : at + t, :] = x_refs[n][...]
                g_rows[at : at + t, :] = g_refs[n][...]
            for n in range(F):
                cols = slice(n * fw, (n + 1) * fw)
                rows = slice(n * shard, (n + 1) * shard)
                value = dot(x_rows[: 2 * t, rows], pre_a_ref[...], tn)
                value = value + dot(x_rows[2 * t :, rows], pre_b_ref[...], tn)
                grads[n, 0:shard, :] = value.astype(bf16)
                value = dot(hidden_a_ref[:, cols], g_rows[: 2 * t, :], tn)
                value = value + dot(hidden_b_ref[:, cols], g_rows[2 * t :, :], tn)
                grads[n, shard:, :] = value.astype(bf16)
            sums_ref[0:1, :] = row_sum(pre_a_ref[...]) + row_sum(pre_b_ref[...])

        grad_ffn, sums_ffn = stage(
            ffn_grads,
            where,
            second + d_ffn + [after(hidden_a, d2_sent), hidden_b, d_pre_a, d_pre_b],
            [((F, shard + fw, D), bf16), ((8, D), f32)],
            [pltpu.VMEM((T, D), bf16), pltpu.VMEM((T, D), bf16)],
        )
        own_ffn = lax.psum_scatter(
            grad_ffn.reshape(F * (shard + fw), D), "fsdp", scatter_dimension=0, tiled=True
        )

        def second_back(w, ins, outs, scratch):
            a, b, far, d_three_ref, normed_ref, inverse_ref, small_ref = ins[:7]
            rest_refs = ins[7:]
            d_ref, low_ref, keep_ref, send_ref, sums_ref = outs
            weight, sems = scratch
            copies = Copies(sems)
            load_out(copies, w, rest_refs, 1, weight)
            total = alpha_scale * d_three_ref[...]
            total = total + a[...].astype(f32) + b[...].astype(f32) + far[...].astype(f32)
            d, gain, shift = norm_rows_back(
                total, normed_ref[...], inverse_ref[...], small_ref[8:9, :]
            )
            d_ref[...] = d
            low = d.astype(bf16)
            low_ref[...] = low
            sums_ref[0:1, :] = row_sum(low)
            sums_ref[1:2, :] = gain
            sums_ref[2:3, :] = shift
            copies.wait()
            for n in range(S):
                target = keep_ref if n < 2 else send_ref
                value = dot(low, group_rows(weight, w[SEQ + n]), nt)
                target[:, (n % 2) * hw : (n % 2 + 1) * hw] = value.astype(bf16)

        d_two, d_cross, dc_keep, dc_send, sums_two = stage(
            second_back,
            where,
            [d2_part_0, d2_near, d2_far, after(d_three, grad_ffn), normed_two, inverse_two, small]
            + [hbm(r) for r in rest],
            [
                ((t, D), f32), ((t, D), bf16), ((t, half), bf16), ((t, half), bf16), ((8, D), f32),
            ],
            [out_scratch, pltpu.SemaphoreType.DMA((2,))],
        )
        dc_other = core_swap(dc_send)

        def backward_pair(q_ref, k_ref, v_ref, g_ref, lse_ref, key_count, limit, dk_acc, dv_acc):
            dqs = []
            for h in range(2):
                cols = slice(h * HD, (h + 1) * HD)
                query = q_ref[:, cols] * jnp.asarray(score_scale, bf16)
                grad = g_ref[:, cols]
                scores = dot(k_ref[:key_count, cols], query, nt)
                if limit is not None:
                    scores = mask_scores(scores, 0, limit)
                weights = jnp.exp(scores - lse_ref[0, h : h + 1, :])
                dv_acc[h, :key_count, :] += dot(weights.astype(bf16), grad, nn)
                grad_weights = dot(v_ref[:key_count, cols], grad, nt)
                row_term = jnp.sum(grad_weights * weights, axis=0, keepdims=True)
                low = (weights * (grad_weights - row_term)).astype(bf16)
                dk_acc[h, :key_count, :] += dot(low, query, nn)
                dqs.append((dot(low, k_ref[:key_count, cols], tn) * score_scale).astype(bf16))
            return jnp.concatenate(dqs, axis=1)

        def sums_out(ref, acc):
            ref[...] = jnp.concatenate([acc[h].astype(bf16) for h in range(2)], axis=1)

        def cross_backward(
            w, qa, qb, k0, v0, k1, v1, ga, gb, lse_ref, da, db, dk0, dv0, dk1, dv1, dk_acc, dv_acc
        ):
            g, i = pl.program_id(0), pl.program_id(1)

            @pl.when(i == 0)
            def _():
                dk_acc[...] = jnp.zeros_like(dk_acc)
                dv_acc[...] = jnp.zeros_like(dv_acc)

            for gi, (k_ref, v_ref) in enumerate(((k0, v0), (k1, v1))):
                for qi, (q_ref, g_ref, d_ref) in enumerate(((qa, ga, da), (qb, gb, db))):

                    @pl.when((g // pairs == gi) & (i == qi))
                    def _(q_ref=q_ref, g_ref=g_ref, d_ref=d_ref, k_ref=k_ref, v_ref=v_ref):
                        d_ref[...] = backward_pair(
                            q_ref, k_ref, v_ref, g_ref, lse_ref, T, None, dk_acc, dv_acc
                        )

            for gi, (dk_ref, dv_ref) in enumerate(((dk0, dv0), (dk1, dv1))):

                @pl.when((g // pairs == gi) & (i == 1))
                def _(dk_ref=dk_ref, dv_ref=dv_ref):
                    sums_out(dk_ref, dk_acc)
                    sums_out(dv_ref, dv_acc)

        def near_block(m):
            return pl.BlockSpec((T, pair), lambda g, i, _: (0, jnp.minimum(g, pairs - 1)))

        def far_block(m):
            return pl.BlockSpec((T, pair), lambda g, i, _: (0, jnp.maximum(g - pairs, 0)))

        acc_scratch = [pltpu.VMEM((2, T, HD), f32), pltpu.VMEM((2, T, HD), f32)]
        dq_keep, dq_send, dk_own, dv_own, dk_far, dv_far = pl.pallas_call(
            cross_backward,
            grid_spec=pltpu.PrefetchScalarGridSpec(
                num_scalar_prefetch=1,
                grid=(2 * pairs, 2),
                in_specs=[row_block, row_block]
                + kv_specs()
                + [row_block, row_block, cross_lse_block],
                out_specs=[row_block, row_block]
                + [near_block(0), near_block(1), far_block(0), far_block(1)],
                scratch_shapes=acc_scratch,
            ),
            out_shape=[jax.ShapeDtypeStruct((t, half), bf16)] * 2
            + [jax.ShapeDtypeStruct((T, hw), bf16)] * 4,
            compiler_params=pltpu.CompilerParams(vmem_limit_bytes=vmem_limit),
            cost_estimate=short,
        )(
            where, cq_keep, cq_other, kv_own, kv_own, kv_far, kv_far, dc_keep, dc_other,
            cross_lse,
        )
        dq_other = core_swap(dq_send)

        def first_back(w, ins, outs, scratch):
            keep_ref, other_ref, d_two_ref, normed_ref, inverse_ref, small_ref = ins[:6]
            rest_refs = ins[6:]
            d_ref, low_ref = outs[0], outs[1]
            sent_ref, sums_ref = outs[2], outs[3]
            weight, cq, sems = scratch
            copies = Copies(sems)
            for e in range(2):
                copies.add(rest_refs[e].at[:, :, pl.ds(D, half)], cq.at[e])
            load_out(copies, w, rest_refs, 0, weight)
            copies.wait()
            total = alpha_scale * d_two_ref[...]
            for e, ref in enumerate((keep_ref, other_ref)):
                total = total + dot(ref[...], cq[e].reshape(D, half), nt)
            for n, piece in enumerate(halves(keep_ref, other_ref)):
                sums_ref[3:4, span(w[SEQ + n], hw)] = row_sum(piece)
            d, gain, shift = norm_rows_back(
                total, normed_ref[...], inverse_ref[...], small_ref[7:8, :]
            )
            d_ref[...] = d
            low = d.astype(bf16)
            low_ref[...] = low
            sums_ref[0:1, :] = row_sum(low)
            sums_ref[1:2, :] = gain
            sums_ref[2:3, :] = shift
            for n in range(S):
                value = dot(low, group_rows(weight, n), nt)
                sent_ref[n * t : (n + 1) * t, :] = value.astype(bf16)

        d_one, d_branch, d_attn_sent, sums_one = stage(
            first_back,
            where,
            [dq_keep, dq_other, d_two, normed_one, inverse_one, small] + [hbm(r) for r in rest],
            [((t, D), f32), ((t, D), bf16), ((T, hw), bf16), ((8, D), f32)],
            [out_scratch, cq_scratch, pltpu.SemaphoreType.DMA((4,))],
        )
        d_attn = heads_to_positions(d_attn_sent)

        def middle_grads(w, ins, outs, scratch):
            dq_keep_ref, dq_other_ref, low_ref, attn_ref, d_one_ref, co_keep, co_other, d_two_ref = ins
            own, cross = scratch
            core = lax.rem(w[MINE], 2)
            for e, ref in enumerate((dq_keep_ref, dq_other_ref)):
                value = dot(low_ref[...], ref[...], tn)
                outs[e][:, :, D:] = value.astype(bf16).reshape(F, shard, half)
            for n, piece in enumerate(halves(co_keep, co_other)):
                value = dot(piece, d_two_ref[...], tn).astype(bf16)
                cross[pl.ds(w[SEQ + n] * per_group, per_group)] = value.reshape(
                    per_group, 2, deep, D
                )
                value = dot(attn_ref[n * t : (n + 1) * t, :], d_one_ref[...], tn).astype(bf16)
                own[n * per_group : (n + 1) * per_group] = value.reshape(per_group, 2, deep, D)
            for e in range(2):
                at = core if e == 0 else 1 - core
                outs[e][:, 0:deep, 0:D] = own[:, at]
                outs[e][:, deep:, 0:D] = cross[:, at]

        middle_keep, middle_send = stage(
            middle_grads,
            where,
            [dq_keep, dq_other, first_low, attn, after(d_branch, d_attn_sent), cross_keep]
            + [cross_other, d_cross],
            [((F, shard, rest_cols), bf16)] * 2,
            [out_scratch, out_scratch],
        )
        middle_got = core_swap(middle_send)

        def scatter_terms(parts):
            return [parts[0], core_swap(parts[2]), y_swap(add_pair(parts[1], core_swap(parts[3])))]

        def split_x(w, value, keep_ref, send_ref):
            size = keep_ref.shape[0] // Z
            for n in range(Z):
                rows = slice(n * size, (n + 1) * size)
                keep_ref[rows, :] = value[span(n * X + w[AT_X], size), :]
                send_ref[rows, :] = value[span(n * X + 1 - w[AT_X], size), :]

        def z_sum(sent):
            rows, cols = sent.shape[0] // Z, sent.shape[1]
            terms = z_exchange(sent).reshape(Z, rows, cols)
            return jnp.sum(terms.astype(f32), axis=0).astype(bf16)

        dk_got, dv_got = (y_swap(after(d, d_attn)) for d in (dk_far, dv_far))

        def pack_rest(w, ins, outs, _):
            for n in range(Z):
                for out, at in ((outs[0], w[AT_X]), (outs[1], 1 - w[AT_X])):
                    value = ins[0][n * X + at].astype(f32) + ins[1][n * X + at].astype(f32)
                    out[n * shard : (n + 1) * shard, :] = value.astype(bf16)

        rest_keep, rest_send = stage(
            pack_rest,
            where,
            [middle_keep, middle_got],
            [((Z * shard, rest_cols), bf16)] * 2,
        )
        rest_got = x_shift(rest_send, 1)

        def self_backward(
            w, q_ref, k_ref, v_ref, g_ref, lse_ref, dq_ref, dk_ref, dv_ref, dk_acc, dv_acc
        ):
            i = pl.program_id(1)

            @pl.when(i == 0)
            def _():
                dk_acc[...] = jnp.zeros_like(dk_acc)
                dv_acc[...] = jnp.zeros_like(dv_acc)

            limit = jnp.minimum(w[LENGTH], (i + 1) * BLK)

            def visit(key_count):
                dq_ref[...] = backward_pair(
                    q_ref, k_ref, v_ref, g_ref, lse_ref, key_count, limit, dk_acc, dv_acc
                )

            key_cases(T, True, i, visit)

            @pl.when(i == S - 1)
            def _():
                sums_out(dk_ref, dk_acc)
                sums_out(dv_ref, dv_acc)

        key_block = pl.BlockSpec((T, pair), lambda g, i, _: (0, g))
        dq_self, dk_self, dv_self = pl.pallas_call(
            self_backward,
            grid_spec=pltpu.PrefetchScalarGridSpec(
                num_scalar_prefetch=1,
                grid=(pairs, S),
                in_specs=[q_block, qkv_spec(1), qkv_spec(2), q_block, lse_block],
                out_specs=[q_block, key_block, key_block],
                scratch_shapes=acc_scratch,
            ),
            out_shape=[jax.ShapeDtypeStruct((T, hw), bf16)] * 3,
            compiler_params=pltpu.CompilerParams(vmem_limit_bytes=vmem_limit),
            cost_estimate=short,
        )(where, qkv, qkv, qkv, d_attn, after(self_lse, rest_keep))

        tall = shard + 16

        def place_small(small_sums, value):
            for n in range(F):
                lanes = slice(n * shard, (n + 1) * shard)
                at = n * tall + shard
                value[at : at + 16, 0:shard] = small_sums[0:16, lanes].astype(bf16)
                rest_rows = [small_sums[16:, lanes], jnp.zeros((32 - small_rows, shard), f32)]
                value[at : at + 16, shard : 2 * shard] = jnp.concatenate(
                    rest_rows, axis=0
                ).astype(bf16)

        def last_grads(w, ins, outs, scratch):
            dq, dk, dv, one, two, three, ffn = ins[:7]
            mem_refs, weight = ins[7:11], ins[11]
            blocks, mem_blocks = ins[12 : 12 + S], ins[12 + S :]
            keep_ref, send_ref = outs[S], outs[S + 1]
            x_all, m_all, d_all, value, small_sums, sems = scratch
            copies = Copies(sems)
            for n in range(S):
                copies.add(blocks[n], x_all.at[span(w[SEQ + n], t)])
            for n in range(S):
                copies.add(mem_blocks[n], m_all.at[pl.ds(n * t, t)])
            for m in range(2):
                near, far = mem_refs[m], mem_refs[2 + m]
                for n in range(S):
                    rows = slice(n * t, (n + 1) * t)
                    total = near[rows, :].astype(f32) + far[rows, :].astype(f32)
                    d_all[rows, m * hw : (m + 1) * hw] = total.astype(bf16)
            for n in (3, 2, 1, 0):
                total = dot(d_all[n * t : (n + 1) * t, :], weight[...], nt)
                outs[n][...] = total.astype(bf16)
            copies.wait()

            def store(grad, cols):
                for n in range(F):
                    value[n * tall : n * tall + shard, cols] = grad[n * shard : (n + 1) * shard]

            for m, d in enumerate((dq, dk, dv)):
                grad = dot(x_all[...], d[...], tn).astype(bf16)
                store(grad, slice(m * hw, (m + 1) * hw))
            grad = dot(m_all[...], d_all[...], tn).astype(bf16)
            store(grad, slice(3 * hw, 5 * hw))
            small_sums[...] = jnp.zeros_like(small_sums)
            mine = span(w[MINE], hw)
            small_sums[0:1, mine] = row_sum(dq[...])
            small_sums[1:2, mine] = row_sum(dv[...])
            small_sums[4:5, mine] = row_sum(d_all[:, hw:])
            rows = [
                (2, one, 0), (3, one, 3), (5, two, 0), (6, three, 0), (7, one, 1), (8, two, 1),
                (9, three, 1), (10, one, 2), (11, two, 2), (12, three, 2),
            ]
            for at, ref, row in rows:
                small_sums[at : at + 1, :] = ref[row : row + 1, :]
            small_sums[pl.ds(13 + w[MINE], 1), :] = ffn[0:1, :]
            place_small(small_sums, value)
            split_x(w, value, keep_ref, send_ref)

        *mem_parts, last_keep, last_send = stage(
            last_grads,
            where,
            [dq_self, dk_self, dv_self, sums_one, sums_two, sums_three, sums_ffn]
            + [dk_own, dv_own, dk_got, dv_got, w_mem]
            + [hbm(b) for b in x_blocks + m_blocks],
            [((t, D), bf16)] * S + [((Z * tall, 5 * hw), bf16)] * 2,
            [
                pltpu.VMEM((T, D), bf16),
                pltpu.VMEM((T, D), bf16),
                pltpu.VMEM((T, 2 * hw), bf16),
                pltpu.VMEM((F * tall, 5 * hw), bf16),
                pltpu.VMEM((small_rows, D), f32),
                pltpu.SemaphoreType.DMA((2 * S,)),
            ],
        )
        last_got = x_shift(last_send, 1)
        rest_sent = add_pair(rest_keep, after(rest_got, last_keep))

        def input_parts(w, ins, outs, scratch):
            grads, pieces = ins[:3], ins[3:]
            weight, sems = scratch
            copies = Copies(sems)
            for k in range(2):
                at = w[AT_X] if k == 0 else 1 - w[AT_X]
                copies.add(pieces[k].at[:, pl.ds(0, shard)], weight.at[:, at])
            copies.wait()
            for n in (3, 2, 1, 0):
                rows = span(w[SEQ + n], t)
                value = None
                for m in range(3):
                    part_of = weight[..., m * hw : (m + 1) * hw].reshape(D, hw)
                    term = dot(grads[m][rows, :], part_of, nt)
                    value = term if value is None else value + term
                outs[n][...] = value.astype(bf16)

        in_parts = stage(
            input_parts,
            where,
            [after(dq_self, rest_sent), dk_self, dv_self] + [hbm(p) for p in got_qkv],
            [((t, D), bf16)] * S,
            [pltpu.VMEM((Z, X, shard, 3 * hw), bf16), pltpu.SemaphoreType.DMA((2,))],
        )
        in_terms = scatter_terms(in_parts)
        memory_grad = sum(term.astype(f32) for term in scatter_terms(mem_parts)).astype(bf16)
        input_grad = (
            alpha_scale * d_one + sum(term.astype(f32) for term in in_terms)
        ).astype(bf16)


        def finish_ffn(w, ins, outs, _):
            for n in range(S):
                for m in range(F):
                    lanes = pl.ds(pl.multiple_of(m * S * fw + w[SEQ + n] * fw, fw), fw)
                    outs[0][:, lanes] = ins[n][0:shard, m * fw : (m + 1) * fw].astype(f32)
                outs[1][span(w[SEQ + n], fw), :] = ins[n][shard:, :].astype(f32)

        grad_fin, grad_fout = stage(
            finish_ffn,
            where,
            seq_gather(after(own_ffn, last_keep)),
            [((shard, FF), f32), ((S * fw, D), f32)],
        )

        own_rest = z_sum(rest_sent)
        last_sent = add_pair(
            last_keep, after(last_got, own_rest, grad_fin, input_grad, memory_grad)
        )
        own_last = z_sum(last_sent)

        def sum_chips(w, ins, outs, _):
            near, away = ins
            out = outs[0]
            out[:, 0:D] = (near[:, 0:D].astype(f32) + away[:, 0:D].astype(f32)).astype(bf16)
            for k in range(2):
                mine = slice(D + k * hw, D + (k + 1) * hw)
                theirs = slice(D + (1 - k) * hw, D + (2 - k) * hw)
                out[:, mine] = (near[:, mine].astype(f32) + away[:, theirs].astype(f32)).astype(bf16)

        (rest_sum,) = stage(
            sum_chips, where, [own_rest, y_swap(own_rest)], [((shard, rest_cols), bf16)]
        )

        def finish_rest(w, ins, outs, _):
            query, own, cross = outs
            core = lax.rem(w[MINE], 2)
            for e in range(2):
                rows = span(core if e == 0 else 1 - core, deep)
                own[rows, :] = ins[e][0:deep, 0:D].astype(f32)
                cross[rows, :] = ins[e][deep:, 0:D].astype(f32)
                for k in range(2):
                    query[:, span(w[SEQ + 2 * e + k], hw)] = ins[e][
                        :, D + k * hw : D + (k + 1) * hw
                    ].astype(f32)

        grad_query, grad_self_out, grad_cross_out = stage(
            finish_rest, where, [rest_sum, core_swap(rest_sum)], [((shard, D), f32)] * 3
        )

        def finish_last(w, ins, outs, _):
            for n in range(S):
                group = w[SEQ + n] * hw
                for m in range(5):
                    target, at = (outs[0], m) if m < 3 else (outs[1], m - 3)
                    lanes = pl.ds(pl.multiple_of(at * D + group, hw), hw)
                    target[:, lanes] = ins[n][0:shard, m * hw : (m + 1) * hw].astype(f32)
            outs[2][0:16, :] = sum(ins[n][shard:, 0:shard].astype(f32) for n in range(S))
            outs[2][16:, :] = sum(
                ins[n][shard : shard + 8, shard : 2 * shard].astype(f32) for n in range(S)
            )

        grad_self_in, grad_memory, small_own = stage(
            finish_last,
            where,
            seq_gather(own_last),
            [((shard, 3 * D), f32), ((shard, 2 * D), f32), ((small_rows, shard), f32)],
        )

        rows = [small_own[n] for n in range(7)]
        return (
            layer_out[None],
            input_grad[None],
            memory_grad[None],
            grad_self_in,
            rows[0],
            rows[1],
            grad_self_out,
            rows[2],
            grad_query,
            rows[3],
            grad_memory,
            rows[4],
            grad_cross_out,
            rows[5],
            grad_fin,
            small_own[13 : 13 + S].reshape(S * fw),
            grad_fout,
            rows[6],
            small_own[7:10],
            small_own[10:13],
        )

    return local


def solution(mesh):
    general, tiled = general_layer(mesh), tiled_layer(mesh)
    S, F = mesh.shape["seq"], mesh.shape["fsdp"]

    def local(*args):
        _, t, D = args[0].shape
        FF = args[15].shape[1]
        blocks = (D // F, D // S, FF // (F * S))
        whole_tiles = all(n % 128 == 0 for n in blocks) and D // F // 2 % 16 == 0
        if whole_tiles and S == 4 and F == 8 and t == BLK:
            return tiled(*args)
        return general(*args)

    by_row, rows_1d = P("fsdp", None), P("fsdp")
    tokens, norms = P("fsdp", "seq", None), P(None, "fsdp")
    in_specs = (
        tokens, tokens, rows_1d, tokens, by_row, rows_1d, rows_1d, by_row, rows_1d, by_row, rows_1d,
        by_row, rows_1d, by_row, rows_1d, by_row, rows_1d, by_row, rows_1d, norms, norms,
    )
    out_specs = (
        tokens, tokens, tokens, by_row, rows_1d, rows_1d, by_row, rows_1d, by_row, rows_1d, by_row,
        rows_1d, by_row, rows_1d, by_row, rows_1d, by_row, rows_1d, norms, norms,
    )
    return jax.shard_map(local, mesh=mesh, in_specs=in_specs, out_specs=out_specs, check_vma=False)
```

```python
import functools

import jax
import jax.numpy as jnp
from jax import lax
from jax.experimental import pallas as pl
from jax.experimental.pallas import tpu as pltpu
from jax.sharding import PartitionSpec as P

HD = 64
BLK = 256
CORES = 2

alpha_scale = 300.0**0.25
layer_eps = 1e-05
score_scale = 0.125
masked_value = -1e30
gelu_coef = 0.7978845608028654
gelu_cube = 0.044715

f32 = jnp.float32
bf16 = jnp.bfloat16
vmem_limit = 56 * 1024 * 1024


def dot(left, right, dims):
    return lax.dot_general(left, right, (dims, ((), ())), preferred_element_type=f32)


nn = ((1,), (0,))
nt = ((1,), (1,))
tn = ((0,), (0,))


def key_cases(total_keys, causal, block_index, visit):
    if not causal:
        visit(total_keys)
        return
    blocks = total_keys // BLK
    cases = min(4, blocks)
    for case in range(cases):
        low, high = case * blocks // cases, (case + 1) * blocks // cases

        @pl.when((block_index >= low) & (block_index < high))
        def _(high=high):
            visit(high * BLK)


def mask_scores(scores, first_key, limit):
    key_pos = first_key + lax.broadcasted_iota(jnp.int32, scores.shape, 0)
    return jnp.where(key_pos < limit, scores, masked_value)


def forward_kernel(causal, heads, chunk, len_ref, q_ref, k_ref, v_ref, o_ref, lse_ref):
    block_index = pl.program_id(1)
    total_keys = k_ref.shape[0]
    limit = jnp.minimum(len_ref[0], (block_index + 1) * BLK) if causal else 0
    rows = q_ref.shape[0]

    if total_keys <= chunk:

        def visit(key_count):
            outs, lses = [], []
            for h in range(heads):
                cols = slice(h * HD, (h + 1) * HD)
                query = q_ref[:, cols] * jnp.asarray(score_scale, bf16)
                scores = dot(k_ref[:key_count, cols], query, nt)
                if causal:
                    scores = mask_scores(scores, 0, limit)
                top = jnp.max(scores, axis=0, keepdims=True)
                weights = jnp.exp(scores - top)
                totals = jnp.sum(weights, axis=0, keepdims=True)
                low = (weights * (1.0 / totals)).astype(bf16)
                outs.append(dot(low, v_ref[:key_count, cols], tn).astype(bf16))
                lses.append(top + jnp.log(totals))
            o_ref[...] = outs[0] if heads == 1 else jnp.concatenate(outs, axis=1)
            lse_ref[0] = lses[0] if heads == 1 else jnp.concatenate(lses, axis=0)

        key_cases(total_keys, causal, block_index, visit)
    else:
        live = ((block_index + 1) * BLK + chunk - 1) // chunk if causal else total_keys // chunk
        outs, lses = [], []
        for h in range(heads):
            cols = slice(h * HD, (h + 1) * HD)
            query = q_ref[:, cols] * jnp.asarray(score_scale, bf16)

            def step(n, carry, cols=cols, query=query):
                top, totals, acc = carry
                span = pl.ds(pl.multiple_of(n * chunk, chunk), chunk)
                scores = dot(k_ref[span, cols], query, nt)
                if causal:
                    scores = mask_scores(scores, n * chunk, limit)
                new_top = jnp.maximum(top, jnp.max(scores, axis=0, keepdims=True))
                decay = jnp.exp(top - new_top)
                weights = jnp.exp(scores - new_top)
                totals = totals * decay + jnp.sum(weights, axis=0, keepdims=True)
                acc = acc * decay + dot(v_ref[span, cols], weights.astype(bf16), tn)
                return new_top, totals, acc

            start = (
                jnp.full((1, rows), masked_value, f32),
                jnp.zeros((1, rows), f32),
                jnp.zeros((HD, rows), f32),
            )
            top, totals, acc = lax.fori_loop(0, live, step, start)
            outs.append((acc / totals).T.astype(bf16))
            lses.append(top + jnp.log(totals))
        o_ref[...] = outs[0] if heads == 1 else jnp.concatenate(outs, axis=1)
        lse_ref[0] = lses[0] if heads == 1 else jnp.concatenate(lses, axis=0)


def backward_kernel(
    causal, heads, chunk, len_ref, q_ref, k_ref, v_ref, g_ref, lse_ref, dq_ref, dk_ref, dv_ref,
    dk_acc, dv_acc
):
    block_index = pl.program_id(1)
    total_keys = k_ref.shape[0]
    limit = jnp.minimum(len_ref[0], (block_index + 1) * BLK) if causal else 0

    @pl.when(block_index == 0)
    def _():
        dk_acc[...] = jnp.zeros_like(dk_acc)
        dv_acc[...] = jnp.zeros_like(dv_acc)

    def probabilities(query, span, cols, first_key, lse):
        scores = dot(k_ref[span, cols], query, nt)
        if causal:
            scores = mask_scores(scores, first_key, limit)
        return jnp.exp(scores - lse)

    if total_keys <= chunk:

        def visit(key_count):
            span = slice(0, key_count)
            dqs = []
            for h in range(heads):
                cols = slice(h * HD, (h + 1) * HD)
                query = q_ref[:, cols] * jnp.asarray(score_scale, bf16)
                grad = g_ref[:, cols]
                weights = probabilities(query, span, cols, 0, lse_ref[0, h : h + 1, :])
                dv_acc[h, span, :] += dot(weights.astype(bf16), grad, nn)
                grad_weights = dot(v_ref[span, cols], grad, nt)
                row_term = jnp.sum(grad_weights * weights, axis=0, keepdims=True)
                low = (weights * (grad_weights - row_term)).astype(bf16)
                dk_acc[h, span, :] += dot(low, query, nn)
                dqs.append((dot(low, k_ref[span, cols], tn) * score_scale).astype(bf16))
            dq_ref[...] = dqs[0] if heads == 1 else jnp.concatenate(dqs, axis=1)

        key_cases(total_keys, causal, block_index, visit)
    else:
        live = ((block_index + 1) * BLK + chunk - 1) // chunk if causal else total_keys // chunk
        rows = q_ref.shape[0]
        dqs = []
        for h in range(heads):
            cols = slice(h * HD, (h + 1) * HD)
            query = q_ref[:, cols] * jnp.asarray(score_scale, bf16)
            grad = g_ref[:, cols]
            lse = lse_ref[0, h : h + 1, :]

            def sums(n, row_term, cols=cols, query=query, grad=grad, lse=lse):
                span = pl.ds(pl.multiple_of(n * chunk, chunk), chunk)
                weights = probabilities(query, span, cols, n * chunk, lse)
                grad_weights = dot(v_ref[span, cols], grad, nt)
                return row_term + jnp.sum(grad_weights * weights, axis=0, keepdims=True)

            row_term = lax.fori_loop(0, live, sums, jnp.zeros((1, rows), f32))

            def step(n, acc, h=h, cols=cols, query=query, grad=grad, lse=lse, row_term=row_term):
                span = pl.ds(pl.multiple_of(n * chunk, chunk), chunk)
                weights = probabilities(query, span, cols, n * chunk, lse)
                dv_acc[h, span, :] += dot(weights.astype(bf16), grad, nn)
                grad_weights = dot(v_ref[span, cols], grad, nt)
                low = (weights * (grad_weights - row_term)).astype(bf16)
                dk_acc[h, span, :] += dot(low, query, nn)
                return acc + dot(low, k_ref[span, cols], tn)

            acc = lax.fori_loop(0, live, step, jnp.zeros((rows, HD), f32))
            dqs.append((acc * score_scale).astype(bf16))
        dq_ref[...] = dqs[0] if heads == 1 else jnp.concatenate(dqs, axis=1)

    @pl.when(block_index == pl.num_programs(1) - 1)
    def _():
        for ref, acc in ((dk_ref, dk_acc), (dv_ref, dv_acc)):
            parts = [acc[h].astype(bf16) for h in range(heads)]
            ref[...] = parts[0] if heads == 1 else jnp.concatenate(parts, axis=1)


def attention_specs(total_q, total_k, width):
    block = min(2 * HD, width)
    heads = block // HD
    groups = width // block
    rows = min(BLK, total_q)
    chunk = min(1024, total_k)
    q_spec = pl.BlockSpec((rows, block), lambda g, i, _: (i, g))
    k_spec = pl.BlockSpec((total_k, block), lambda g, i, _: (0, g))
    l_spec = pl.BlockSpec((1, heads, rows), lambda g, i, _: (g, 0, i))
    return block, heads, groups, rows, chunk, q_spec, k_spec, l_spec


def attend_forward(queries, keys, values, lengths, causal):
    total_q, width = queries.shape
    total_k = keys.shape[0]
    block, heads, groups, rows, chunk, q_spec, k_spec, l_spec = attention_specs(
        total_q, total_k, width
    )
    work = total_q * total_k * width
    return pl.pallas_call(
        functools.partial(forward_kernel, causal, heads, chunk),
        grid_spec=pltpu.PrefetchScalarGridSpec(
            num_scalar_prefetch=1,
            grid=(groups, total_q // rows),
            in_specs=[q_spec, k_spec, k_spec],
            out_specs=[q_spec, l_spec],
        ),
        out_shape=[
            jax.ShapeDtypeStruct((total_q, width), bf16),
            jax.ShapeDtypeStruct((groups, heads, total_q), f32),
        ],
        compiler_params=pltpu.CompilerParams(vmem_limit_bytes=vmem_limit),
        cost_estimate=pl.CostEstimate(
            flops=4 * work, bytes_accessed=8 * total_k * width, transcendentals=work // HD
        ),
    )(lengths, queries, keys, values)


def attend_back(queries, keys, values, grads, lse, lengths, causal):
    total_q, width = queries.shape
    total_k = keys.shape[0]
    block, heads, groups, rows, chunk, q_spec, k_spec, l_spec = attention_specs(
        total_q, total_k, width
    )
    work = total_q * total_k * width
    return pl.pallas_call(
        functools.partial(backward_kernel, causal, heads, chunk),
        grid_spec=pltpu.PrefetchScalarGridSpec(
            num_scalar_prefetch=1,
            grid=(groups, total_q // rows),
            in_specs=[q_spec, k_spec, k_spec, q_spec, l_spec],
            out_specs=[q_spec, k_spec, k_spec],
            scratch_shapes=[
                pltpu.VMEM((heads, total_k, HD), f32),
                pltpu.VMEM((heads, total_k, HD), f32),
            ],
        ),
        out_shape=[
            jax.ShapeDtypeStruct((total_q, width), bf16),
            jax.ShapeDtypeStruct((total_k, width), bf16),
            jax.ShapeDtypeStruct((total_k, width), bf16),
        ],
        compiler_params=pltpu.CompilerParams(vmem_limit_bytes=vmem_limit),
        cost_estimate=pl.CostEstimate(
            flops=10 * work, bytes_accessed=16 * total_k * width, transcendentals=work // HD
        ),
    )(lengths, queries, keys, values, grads, lse)


def assemble(arrays, moves, shape):
    dtype = arrays[0].dtype
    if any(m[2] % 16 or m[4] % 128 or m[1] % 16 or m[3] % 128 for m in moves):
        result = jnp.zeros(shape, dtype)
        for index, row, rows, col, cols, to_row, to_col in moves:
            part = arrays[index][row : row + rows, col : col + cols]
            result = lax.dynamic_update_slice(result, part, (to_row, to_col))
        return result
    count = len(arrays)
    places = jnp.stack([jnp.asarray(p, jnp.int32) for m in moves for p in (m[5], m[6])])

    def kernel(places_ref, *refs):
        sources, target, sems = refs[:count], refs[count], refs[count + 1]
        copies = []
        for n, (index, row, rows, col, cols, _, _) in enumerate(moves):
            to_row = pl.multiple_of(places_ref[2 * n], rows)
            to_col = pl.multiple_of(places_ref[2 * n + 1], cols)
            copies.append(
                pltpu.make_async_copy(
                    sources[index].at[pl.ds(row, rows), pl.ds(col, cols)],
                    target.at[pl.ds(to_row, rows), pl.ds(to_col, cols)],
                    sems.at[n],
                )
            )
        for copy in copies:
            copy.start()
        for copy in copies:
            copy.wait()

    return pl.pallas_call(
        kernel,
        grid_spec=pltpu.PrefetchScalarGridSpec(
            num_scalar_prefetch=1,
            grid=(1,),
            in_specs=[pl.BlockSpec(memory_space=pl.ANY)] * count,
            out_specs=pl.BlockSpec(memory_space=pltpu.VMEM),
            scratch_shapes=[pltpu.SemaphoreType.DMA((len(moves),))],
        ),
        out_shape=jax.ShapeDtypeStruct(shape, dtype),
        compiler_params=pltpu.CompilerParams(vmem_limit_bytes=vmem_limit),
        cost_estimate=pl.CostEstimate(
            flops=0,
            bytes_accessed=2 * sum(a.size * a.dtype.itemsize for a in arrays),
            transcendentals=0,
        ),
    )(places, *arrays)


def gelu_both(values):
    inner = gelu_coef * (values + gelu_cube * values * values * values)
    tangent = jnp.tanh(inner)
    output = 0.5 * values * (1.0 + tangent)
    slope = 0.5 * (1.0 + tangent) + 0.5 * values * (1.0 - tangent * tangent) * gelu_coef * (
        1.0 + 3.0 * gelu_cube * values * values
    )
    return (output, slope)


def layer_norm(values, gain_row, shift_row):
    center = values - jnp.mean(values, axis=-1, keepdims=True)
    inverse = lax.rsqrt(jnp.mean(center * center, axis=-1, keepdims=True) + layer_eps)
    normed = center * inverse
    return (normed * gain_row + shift_row, normed, inverse)


def norm_back(grad_rows, normed, inverse, gain_row):
    scaled = grad_rows * gain_row
    inner_term = scaled - jnp.mean(scaled, axis=-1, keepdims=True)
    inner_term = inner_term - normed * jnp.mean(scaled * normed, axis=-1, keepdims=True)
    return (
        inverse * inner_term,
        jnp.sum(grad_rows * normed, axis=0),
        jnp.sum(grad_rows, axis=0),
    )


def column_sum(array):
    return jnp.sum(array.astype(f32), axis=0)


def after(value, *earlier):
    return lax.optimization_barrier((value, *earlier))[0]


def general_layer(mesh):
    S, F = mesh.shape["seq"], mesh.shape["fsdp"]
    Y = S // CORES
    Z = 4 if F % 4 == 0 else 1
    X = F // Z

    core_perm = [(n, n ^ 1) for n in range(S)]

    def y_perm(k):
        return [(y * CORES + c, (y + k) % Y * CORES + c) for y in range(Y) for c in range(CORES)]

    def z_perm(k):
        return [(z * X + x, (z + k) % Z * X + x) for z in range(Z) for x in range(X)]

    def x_perm(k):
        return [(z * X + x, z * X + (x + k) % X) for z in range(Z) for x in range(X)]

    def core_swap(array):
        return lax.ppermute(array, "seq", core_perm)

    def y_shift(array, k):
        return lax.ppermute(array, "seq", y_perm(k % Y)) if k % Y else array

    def z_shift(array, k):
        return lax.ppermute(array, "fsdp", z_perm(k % Z)) if k % Z else array

    def x_shift(array, k):
        return lax.ppermute(array, "fsdp", x_perm(k % X)) if k % X else array

    def local(
        hidden_in,
        memory,
        lengths,
        out_grad,
        self_in_weight,
        self_query_bias,
        self_value_bias,
        self_out_weight,
        self_out_bias,
        cross_query_weight,
        cross_query_bias,
        memory_weight,
        memory_value_bias,
        cross_out_weight,
        cross_out_bias,
        ffn_in_weight,
        ffn_in_bias,
        ffn_out_weight,
        ffn_out_bias,
        norm_gain,
        norm_bias,
    ):
        s = lax.axis_index("seq")
        y, c = s // CORES, s % CORES
        f = lax.axis_index("fsdp")
        z, x = f // X, f % X
        _, t, D = hidden_in.shape
        T = S * t
        hw = D // S
        FF = ffn_in_weight.shape[1]
        shard = D // F
        part = shard // S
        fw = FF // (F * S)
        hidden_in, memory, out_grad = hidden_in[0], memory[0], out_grad[0]

        relative = [(k, e) for e in range(CORES) for k in range(Y)]

        def seq_of(k, e):
            return lax.rem(y - k + Y, Y) * CORES + (c if e == 0 else 1 - c)

        def seq_gather(array):
            own = [y_shift(array, k) for k in range(Y)]
            return own + [core_swap(a) for a in own]

        def seq_scatter(parts):
            chip = []
            for k in reversed(range(Y)):
                other = core_swap(parts[(k, 1)].astype(bf16))
                chip.append((k, parts[(k, 0)].astype(f32) + other.astype(f32)))
            total = None
            for k, value in chip:
                value = y_shift(value.astype(bf16), -k).astype(f32) if k else value
                total = value if total is None else total + value
            return total

        def fsdp_gather(chunk):
            pieces = []
            for kz in range(Z):
                column = z_shift(chunk, kz)
                for kx in range(X):
                    pieces.append(x_shift(column, kx))
            return pieces

        def fsdp_place(pieces):
            rows, cols = pieces[0].shape
            moves = []
            for n in range(F):
                kz, kx = n // X, n % X
                where = lax.rem(z - kz + Z, Z) * X + lax.rem(x - kx + X, X)
                moves.append((n, 0, rows, 0, cols, where * rows, 0))
            return assemble(pieces, moves, (F * rows, cols))

        def fsdp_scatter(grads):
            rows, cols = grads.shape[0] // F, grads.shape[1]
            view = grads.reshape(Z, X, rows, cols)
            total = lax.dynamic_index_in_dim(view, x, 1, keepdims=False).astype(f32)
            for kx in range(1, X):
                sent = lax.dynamic_index_in_dim(view, lax.rem(x + kx, X), 1, keepdims=False)
                total = total + x_shift(sent.astype(bf16), kx).astype(f32)
            low = total.astype(bf16)
            own = lax.dynamic_index_in_dim(low, z, 0, keepdims=False).astype(f32)
            for kz in range(1, Z):
                sent = lax.dynamic_index_in_dim(low, lax.rem(z + kz, Z), 0, keepdims=False)
                own = own + z_shift(sent, kz).astype(f32)
            return own.astype(bf16)

        def finish(own):
            rows, cols = own.shape
            pieces = seq_gather(own)
            moves = [
                (n, 0, rows, 0, cols, seq_of(k, e) * rows, 0)
                for n, (k, e) in enumerate(relative)
            ]
            return assemble(pieces, moves, (S * rows, cols)).reshape(S, rows, cols).astype(f32)

        def pick(array, start, size):
            return lax.dynamic_slice_in_dim(array, start, size, 1)

        small_list = [
            self_query_bias, self_value_bias, self_out_bias, cross_query_bias, memory_value_bias,
            cross_out_bias, ffn_out_bias, norm_gain.reshape(-1), norm_bias.reshape(-1), ffn_in_bias,
        ]
        small = jnp.concatenate(small_list)
        small = lax.all_to_all(
            jnp.broadcast_to(small[None], (F, small.shape[0])), "fsdp", 0, 0, tiled=True
        ).astype(f32)
        smalls = []
        at = 0
        for _ in range(7):
            smalls.append(small[:, at : at + shard].reshape(D))
            at += shard
        b_query, b_value, b_attn_out, b_cross_q, b_mem_value, b_cross_out, b_ffn_out = smalls
        gains = small[:, at : at + 3 * shard].reshape(F, 3, shard).swapaxes(0, 1).reshape(3, D)
        at += 3 * shard
        shifts = small[:, at : at + 3 * shard].reshape(F, 3, shard).swapaxes(0, 1).reshape(3, D)
        at += 3 * shard
        b_ffn_in = lax.dynamic_index_in_dim(
            small[:, at:].reshape(F, S, fw), s, 1, keepdims=False
        ).reshape(F * fw)

        def group_row(row):
            return lax.dynamic_slice_in_dim(row, s * hw, hw, 0)

        chunk_qkv = jnp.concatenate(
            [pick(self_in_weight, m * D + s * hw, hw) for m in range(3)], axis=1
        )
        chunk_mid = jnp.concatenate(
            [pick(memory_weight, m * D + s * hw, hw) for m in range(2)]
            + [pick(cross_query_weight, s * hw, hw)],
            axis=1,
        )
        chunk_out = jnp.concatenate(
            [
                lax.dynamic_slice_in_dim(w, s * part, part, 0)
                for w in (self_out_weight, cross_out_weight)
            ],
            axis=0,
        )
        chunk_fin = lax.dynamic_index_in_dim(
            ffn_in_weight.reshape(shard, F, S, fw), s, 2, keepdims=False
        ).reshape(shard, F * fw)
        chunk_fout = lax.dynamic_slice_in_dim(ffn_out_weight, s * fw, fw, 0)

        got_qkv = fsdp_gather(chunk_qkv)
        x_blocks = seq_gather(hidden_in)
        got_mid = fsdp_gather(after(chunk_mid, got_qkv[-1]))
        m_blocks = seq_gather(after(memory, x_blocks[-1]))
        got_out = fsdp_gather(after(chunk_out, got_qkv[-1]))
        got_fin = fsdp_gather(after(chunk_fin, got_mid[-1]))
        got_fout = fsdp_gather(after(chunk_fout, got_fin[-1]))

        w_qkv = fsdp_place(got_qkv)
        block_moves = [
            (n, 0, t, 0, D, seq_of(k, e) * t, 0) for n, (k, e) in enumerate(relative)
        ]
        x_all = assemble(x_blocks, block_moves, (T, D))
        qkv_bias = jnp.concatenate([group_row(b_query), jnp.zeros((hw,), f32), group_row(b_value)])
        qkv = (dot(x_all, w_qkv, nn) + qkv_bias).astype(bf16)
        q_self, k_self, v_self = (qkv[:, m * hw : (m + 1) * hw] for m in range(3))
        self_attn, self_lse = attend_forward(q_self, k_self, v_self, lengths, True)

        w_mid = fsdp_place(got_mid)
        w_mem, cq_quarter = w_mid[:, : 2 * hw], w_mid[:, 2 * hw :]
        m_all = jnp.concatenate(m_blocks, axis=0)
        mem_bias = jnp.concatenate([jnp.zeros((hw,), f32), group_row(b_mem_value)])
        kv_mem = (dot(m_all, w_mem, nn) + mem_bias).astype(bf16)

        def all_rows(parts_of):
            return assemble(
                parts_of,
                [(n, 0, t, 0, hw, 0, seq_of(k, e) * hw) for n, (k, e) in enumerate(relative)],
                (t, D),
            )

        def heads_to_rows(array):
            blocks = array.reshape(S, t, hw)
            mine = []
            for k, e in relative:
                target = lax.rem(y + k, Y) * CORES + (c if e == 0 else 1 - c)
                sent = lax.dynamic_index_in_dim(blocks, target, 0, keepdims=False)
                sent = y_shift(sent, k)
                mine.append(core_swap(sent) if e else sent)
            return all_rows(mine)

        def rows_to_heads(array):
            mine = []
            for k, e in relative:
                target = lax.rem(y + k, Y) * CORES + (c if e == 0 else 1 - c)
                sent = y_shift(pick(array, target * hw, hw), k)
                mine.append(core_swap(sent) if e else sent)
            return assemble(
                mine,
                [(n, 0, t, 0, hw, seq_of(k, e) * t, 0) for n, (k, e) in enumerate(relative)],
                (T, hw),
            )

        attn_tok = heads_to_rows(self_attn)
        mem_chips = [y_shift(kv_mem, k) for k in range(Y)]
        mem_key = jnp.concatenate([m[:, :hw] for m in mem_chips], axis=1)
        mem_value = jnp.concatenate([m[:, hw:] for m in mem_chips], axis=1)

        out_quarter = fsdp_place(got_out)
        out_pieces = seq_gather(out_quarter)
        own_moves = [[], []]
        for n, (k, e) in enumerate(relative):
            for which in range(2):
                for shard_index in range(F):
                    own_moves[which].append(
                        (
                            n, shard_index * 2 * part + which * part, part, 0, D,
                            shard_index * shard + seq_of(k, e) * part, 0,
                        )
                    )
        w_attn_out = assemble(out_pieces, own_moves[0], (D, D))
        w_cross_out = assemble(out_pieces, own_moves[1], (D, D))
        cq_pieces = seq_gather(cq_quarter)
        w_cross_q = jnp.concatenate(cq_pieces, axis=1)
        b_cq = jnp.concatenate(
            [lax.dynamic_slice_in_dim(b_cross_q, seq_of(k, e) * hw, hw, 0) for k, e in relative]
        )
        half = Y * hw

        x_float = hidden_in.astype(f32)
        branch = dot(attn_tok, w_attn_out, nn) + b_attn_out
        first, normed_one, inverse_one = layer_norm(
            alpha_scale * x_float + branch, gains[0], shifts[0]
        )
        first_low = first.astype(bf16)
        cq_rows = (dot(first_low, w_cross_q, nn) + b_cq).astype(bf16)

        cross_q = jnp.concatenate([cq_rows[:, :half], core_swap(cq_rows[:, half:])], axis=0)
        cross_attn, cross_lse = attend_forward(cross_q, mem_key, mem_value, lengths, False)
        cross_other = core_swap(cross_attn[t:])
        cross_tok = assemble(
            [cross_attn, cross_other],
            [(e, 0, t, k * hw, hw, 0, seq_of(k, e) * hw) for k, e in relative],
            (t, D),
        )
        cross_branch = dot(cross_tok, w_cross_out, nn) + b_cross_out
        second, normed_two, inverse_two = layer_norm(
            alpha_scale * first + cross_branch, gains[1], shifts[1]
        )
        second_low = second.astype(bf16)

        w_fin = fsdp_place(got_fin)
        w_fout = fsdp_place(got_fout)
        second_all = jnp.concatenate(seq_gather(second_low), axis=0)
        pre_act = dot(second_all, w_fin, nn) + b_ffn_in
        act_value, act_slope = gelu_both(pre_act)
        hidden_low = act_value.astype(bf16)
        ffn_part = dot(hidden_low, w_fout, nn)

        def by_owner(array):
            return {ke: array[n * t : (n + 1) * t] for n, ke in enumerate(relative)}

        ffn_branch = seq_scatter(by_owner(ffn_part)) + b_ffn_out
        result, normed_three, inverse_three = layer_norm(
            alpha_scale * second + ffn_branch, gains[2], shifts[2]
        )
        layer_out = result.astype(bf16)

        d_three, gain_three, shift_three = norm_back(
            out_grad.astype(f32), normed_three, inverse_three, gains[2]
        )
        d_ffn = d_three.astype(bf16)
        d_ffn_all = jnp.concatenate(seq_gather(d_ffn), axis=0)
        d_hidden = dot(d_ffn_all, w_fout, nt)
        d_pre = (act_slope * d_hidden).astype(bf16)
        d_second_part = dot(d_pre, w_fin, nt)
        d_second = alpha_scale * d_three + seq_scatter(by_owner(d_second_part))
        grad_fout = dot(hidden_low, d_ffn_all, tn).astype(bf16)
        own_fout = fsdp_scatter(grad_fout)
        grad_fin = dot(second_all, d_pre, tn).astype(bf16)
        own_fin = fsdp_scatter(grad_fin)

        d_two, gain_two, shift_two = norm_back(d_second, normed_two, inverse_two, gains[1])
        d_cross = d_two.astype(bf16)
        d_cross_tok = dot(d_cross, w_cross_out, nt).astype(bf16)
        keep, send = (
            jnp.concatenate([pick(d_cross_tok, seq_of(k, e) * hw, hw) for k in range(Y)], axis=1)
            for e in range(CORES)
        )
        d_cross_heads = jnp.concatenate([keep, core_swap(send)], axis=0)
        dq_cross, dk_mem, dv_mem = attend_back(
            cross_q, mem_key, mem_value, d_cross_heads, cross_lse, lengths, False
        )
        d_cq_rows = jnp.concatenate([dq_cross[:t], core_swap(dq_cross[t:])], axis=1)
        d_first = alpha_scale * d_two + dot(d_cq_rows, w_cross_q, nt)
        grad_cross_out = dot(cross_tok, d_cross, tn)
        grad_cq = dot(first_low, d_cq_rows, tn)
        d_mem = None
        for k in range(Y):
            sent = jnp.concatenate([d[:, k * hw : (k + 1) * hw] for d in (dk_mem, dv_mem)], axis=1)
            got = y_shift(sent, -k).astype(f32)
            d_mem = got if d_mem is None else d_mem + got
        d_mem = d_mem.astype(bf16)
        grad_mem = dot(m_all, d_mem, tn).astype(bf16)
        memory_grad = seq_scatter(by_owner(dot(d_mem, w_mem, nt))).astype(bf16)

        d_one, gain_one, shift_one = norm_back(d_first, normed_one, inverse_one, gains[0])
        d_branch = d_one.astype(bf16)
        d_attn_heads = rows_to_heads(dot(d_branch, w_attn_out, nt).astype(bf16))
        grad_self_out = dot(attn_tok, d_branch, tn)
        dq_self, dk_self, dv_self = attend_back(
            q_self, k_self, v_self, d_attn_heads, self_lse, lengths, True
        )
        d_qkv = jnp.concatenate([dq_self, dk_self, dv_self], axis=1)
        grad_qkv = dot(x_all, d_qkv, tn).astype(bf16)
        own_qkv = fsdp_scatter(grad_qkv)
        input_part = dot(d_qkv, w_qkv, nt).reshape(S, t, D)
        input_sum = seq_scatter(
            {
                (k, e): lax.dynamic_index_in_dim(input_part, seq_of(k, e), 0, keepdims=False)
                for k, e in relative
            }
        )
        input_grad = (alpha_scale * d_one + input_sum).astype(bf16)

        def out_parts(grad):
            view = grad.astype(bf16).reshape(F, S, part, D)
            return {
                (k, e): lax.dynamic_index_in_dim(view, seq_of(k, e), 1, keepdims=False)
                for k, e in relative
            }

        own_cross_out = seq_scatter(out_parts(grad_cross_out)).astype(bf16)
        own_self_out = seq_scatter(out_parts(grad_self_out)).astype(bf16)
        own_cq = seq_scatter(
            {ke: grad_cq[:, n * hw : (n + 1) * hw] for n, ke in enumerate(relative)}
        ).astype(bf16)
        own_mid = fsdp_scatter(jnp.concatenate([grad_mem, own_cq], axis=1))
        own_out = fsdp_scatter(
            jnp.concatenate([own_self_out, own_cross_out], axis=1).reshape(F * 2 * part, D)
        )

        all_fout = finish(own_fout).reshape(S * fw, D)
        all_fin = (
            finish(own_fin).reshape(S, shard, F, fw).transpose(1, 2, 0, 3).reshape(shard, FF)
        )
        all_mid = finish(own_mid)
        all_mem = (
            all_mid[:, :, : 2 * hw]
            .reshape(S, shard, 2, hw)
            .transpose(1, 2, 0, 3)
            .reshape(shard, 2 * D)
        )
        all_cq = all_mid[:, :, 2 * hw :].transpose(1, 0, 2).reshape(shard, D)
        all_out = finish(own_out).reshape(S, 2, part, D)
        all_self_out = all_out[:, 0].reshape(shard, D)
        all_cross_out = all_out[:, 1].reshape(shard, D)
        all_qkv = (
            finish(own_qkv).reshape(S, shard, 3, hw).transpose(1, 2, 0, 3).reshape(shard, 3 * D)
        )

        def spread(row):
            return lax.dynamic_update_slice_in_dim(jnp.zeros((D,), f32), row, s * hw, 0)

        d_cq_sum = column_sum(d_cq_rows)
        cq_bias = jnp.zeros((D,), f32)
        for n, (k, e) in enumerate(relative):
            cq_bias = lax.dynamic_update_slice_in_dim(
                cq_bias, d_cq_sum[n * hw : (n + 1) * hw], seq_of(k, e) * hw, 0
            )
        fin_bias = lax.dynamic_update_slice_in_dim(
            jnp.zeros((F, S, fw), f32), column_sum(d_pre).reshape(F, 1, fw), s, 1
        ).reshape(F, S * fw)
        small_grads = jnp.concatenate(
            [
                row.reshape(F, shard)
                for row in (
                    spread(column_sum(dq_self)), spread(column_sum(dv_self)), column_sum(d_branch),
                    cq_bias, spread(column_sum(d_mem[:, hw:])), column_sum(d_cross),
                    column_sum(d_ffn), gain_one, gain_two, gain_three, shift_one, shift_two,
                    shift_three,
                )
            ]
            + [fin_bias],
            axis=1,
        )
        small_own = jnp.sum(lax.all_to_all(small_grads, "fsdp", 0, 0, tiled=True), axis=0)
        small_own = lax.psum(small_own, "seq")
        rows = [small_own[n * shard : (n + 1) * shard] for n in range(13)]
        return (
            layer_out[None],
            input_grad[None],
            memory_grad[None],
            all_qkv,
            rows[0],
            rows[1],
            all_self_out,
            rows[2],
            all_cq,
            rows[3],
            all_mem,
            rows[4],
            all_cross_out,
            rows[5],
            all_fin,
            small_own[13 * shard :],
            all_fout,
            rows[6],
            jnp.stack(rows[7:10]),
            jnp.stack(rows[10:13]),
        )

    return local


short = pl.CostEstimate(flops=1024, bytes_accessed=1024, transcendentals=0)

small_rows = 24


def hbm(array):
    return ("hbm", array)


def stage(body, where, ins, outs, scratch=(), time=0):
    specs, arrays = [], []
    for item in ins:
        if isinstance(item, tuple):
            specs.append(pl.BlockSpec(memory_space=pl.ANY))
            arrays.append(item[1])
        else:
            specs.append(pl.BlockSpec(memory_space=pltpu.VMEM))
            arrays.append(item)
    n_in, n_out = len(arrays), len(outs)

    def kernel(w, *refs):
        body(w, refs[:n_in], refs[n_in : n_in + n_out], refs[n_in + n_out :])

    return pl.pallas_call(
        kernel,
        grid_spec=pltpu.PrefetchScalarGridSpec(
            num_scalar_prefetch=1,
            grid=(1,),
            in_specs=specs,
            out_specs=[pl.BlockSpec(memory_space=pltpu.VMEM)] * n_out,
            scratch_shapes=list(scratch),
        ),
        out_shape=[jax.ShapeDtypeStruct(shape, dtype) for shape, dtype in outs],
        compiler_params=pltpu.CompilerParams(vmem_limit_bytes=vmem_limit),
        cost_estimate=pl.CostEstimate(
            flops=1024, bytes_accessed=1024 + int(3.5e6 * time), transcendentals=0
        ),
    )(where, *arrays)


class Copies:
    def __init__(self, sems):
        self.sems, self.list = sems, []

    def add(self, source, target):
        copy = pltpu.make_async_copy(source, target, self.sems.at[len(self.list)])
        copy.start()
        self.list.append(copy)
        return copy

    def wait(self):
        for copy in self.list:
            copy.wait()
        self.list = []


def span(index, size):
    return pl.ds(pl.multiple_of(index * size, size), size)


def norm_rows(values, gain_row, shift_row):
    center = values - jnp.mean(values, axis=-1, keepdims=True)
    inverse = lax.rsqrt(jnp.mean(center * center, axis=-1, keepdims=True) + layer_eps)
    normed = center * inverse
    return normed * gain_row + shift_row, normed, inverse


def norm_rows_back(grad_rows, normed, inverse, gain_row):
    scaled = grad_rows * gain_row
    inner = scaled - jnp.mean(scaled, axis=-1, keepdims=True)
    inner = inner - normed * jnp.mean(scaled * normed, axis=-1, keepdims=True)
    return (
        inverse * inner,
        jnp.sum(grad_rows * normed, axis=0, keepdims=True),
        jnp.sum(grad_rows, axis=0, keepdims=True),
    )


def row_sum(array):
    return jnp.sum(array.astype(f32), axis=0, keepdims=True)


def tiled_layer(mesh):
    S, F = mesh.shape["seq"], mesh.shape["fsdp"]
    Z = 4 if F % 4 == 0 else 1
    X = F // Z
    SEQ, MINE, AT_X, LENGTH = 0, S, S + 1, S + 2

    core_perm = [(n, n ^ 1) for n in range(S)]
    y_perm = [(n, n ^ 2) for n in range(S)]
    diagonal_perm = [(n, n ^ 3) for n in range(S)]

    def core_swap(array):
        return lax.ppermute(array, "seq", core_perm)

    def y_swap(array):
        return lax.ppermute(array, "seq", y_perm)

    z_groups = [[z * X + x for z in range(Z)] for x in range(X)]

    def z_exchange(array):
        return lax.all_to_all(array, "fsdp", 0, 0, axis_index_groups=z_groups, tiled=True)

    def x_shift(array, k):
        perm = [(z * X + x, z * X + (x + k) % X) for z in range(Z) for x in range(X)]
        return lax.ppermute(array, "fsdp", perm) if k % X else array

    def seq_gather(array):
        far = y_swap(array)
        return [array, far, core_swap(array), core_swap(far)]

    def tied(values):
        return lax.optimization_barrier(list(values))

    def z_gather(copies):
        return z_exchange(copies)

    def x_gather(column):
        rows, cols = column.shape[0] // Z, column.shape[1]
        return [a.reshape(Z, rows, cols) for a in (column, x_shift(column, 1))]

    def exchange(parts):
        got = [y_swap(parts[1]), core_swap(parts[2]), lax.ppermute(parts[3], "seq", diagonal_perm)]
        return [parts[0], *tied(got)]

    def local(
        hidden_in,
        memory,
        lengths,
        out_grad,
        self_in_weight,
        self_query_bias,
        self_value_bias,
        self_out_weight,
        self_out_bias,
        cross_query_weight,
        cross_query_bias,
        memory_weight,
        memory_value_bias,
        cross_out_weight,
        cross_out_bias,
        ffn_in_weight,
        ffn_in_bias,
        ffn_out_weight,
        ffn_out_bias,
        norm_gain,
        norm_bias,
    ):
        s, f = lax.axis_index("seq"), lax.axis_index("fsdp")
        z, x = f // X, f % X
        _, t, D = hidden_in.shape
        T = S * t
        hw = D // S
        FF = ffn_in_weight.shape[1]
        shard = D // F
        fw = FF // (F * S)
        half = 2 * hw
        per_group = hw // shard
        part = shard // S
        deep = shard // 2
        rest_cols = D + half
        hidden_in, memory, out_grad = hidden_in[0], memory[0], out_grad[0]
        where = jnp.stack(
            [s, s ^ 2, s ^ 1, s ^ 3, s, x, lengths[0]]
        ).astype(jnp.int32)

        def prepare_rest(w, ins, outs, _):
            query, own, cross = ins
            out = outs[0]
            core = lax.rem(w[MINE], 2)
            out[0:deep, 0:D] = own[span(core, deep), :]
            out[deep:, 0:D] = cross[span(core, deep), :]
            out[:, D : D + hw] = query[:, span(w[SEQ], hw)]
            out[:, D + hw :] = query[:, span(w[SEQ + 1], hw)]

        (chunk_rest,) = stage(
            prepare_rest,
            where,
            [cross_query_weight, self_out_weight, cross_out_weight],
            [((shard, rest_cols), bf16)],
        )

        rest_own = lax.all_gather(chunk_rest, "fsdp", axis=0, tiled=True)

        def prepare_qkv(w, ins, outs, _):
            weight, out = ins[0], outs[0]
            me = w[MINE]
            for m in range(3):
                lanes = pl.ds(pl.multiple_of(m * D + me * hw, hw), hw)
                for k in range(Z):
                    out[k, 0:shard, m * hw : (m + 1) * hw] = weight[:, lanes]
            rows = [ins[n][...].reshape(1, shard) for n in range(1, 8)]
            rows += [ins[8][...], ins[9][...]]
            rows += [
                ins[10][n * fw : (n + 1) * fw].reshape(1, fw) for n in range(S)
            ]
            packed = jnp.concatenate([r.astype(f32) for r in rows], axis=0)
            first = packed[0:16].astype(bf16)
            rest = jnp.concatenate(
                [packed[16:], jnp.zeros((32 - packed.shape[0], shard), f32)], axis=0
            ).astype(bf16)
            below = jnp.concatenate(
                [first, rest, jnp.zeros((16, 3 * hw - 2 * shard), bf16)], axis=1
            )
            for k in range(Z):
                out[k, shard : shard + 16, :] = below

        (chunk_qkv,) = stage(
            prepare_qkv,
            where,
            [
                after(self_in_weight, chunk_rest), self_query_bias, self_value_bias, self_out_bias, cross_query_bias,
                memory_value_bias, cross_out_bias, ffn_out_bias, norm_gain, norm_bias, ffn_in_bias,
            ],
            [((Z, shard + 16, 3 * hw), bf16)],
        )

        def prepare_mem(w, ins, outs, _):
            for m in range(2):
                lanes = pl.ds(pl.multiple_of(m * D + w[MINE] * hw, hw), hw)
                for k in range(Z):
                    outs[0][k, :, m * hw : (m + 1) * hw] = ins[0][:, lanes]

        (chunk_mem,) = stage(prepare_mem, where, [memory_weight], [((Z, shard, 2 * hw), bf16)])

        def prepare_ffn(w, ins, outs, _):
            me = w[MINE]
            for n in range(F):
                lanes = pl.ds(pl.multiple_of(n * S * fw + me * fw, fw), fw)
                outs[0][0:shard, n * fw : (n + 1) * fw] = ins[0][:, lanes]
            outs[0][shard:, :] = ins[1][span(me, fw), :]

        (chunk_ffn,) = stage(
            prepare_ffn, where, [ffn_in_weight, ffn_out_weight], [((shard + fw, D), bf16)]
        )

        hidden_far = y_swap(after(hidden_in, chunk_qkv))
        z_qkv = z_gather(chunk_qkv.reshape(Z * (shard + 16), 3 * hw))
        z_qkv, hidden_far, chunk_mem, chunk_ffn = tied([z_qkv, hidden_far, chunk_mem, chunk_ffn])
        x_blocks = [hidden_in, hidden_far, core_swap(hidden_in), core_swap(hidden_far)]
        got_qkv = x_gather(z_qkv)
        memory_far = y_swap(after(memory, hidden_far))
        z_mem = z_gather(after(chunk_mem, z_qkv).reshape(Z * shard, 2 * hw))
        got_qkv[0], z_mem, memory_far = tied([got_qkv[0], z_mem, memory_far])
        m_blocks = [memory, memory_far, core_swap(memory), core_swap(memory_far)]
        got_mem = x_gather(z_mem)

        def project_qkv(w, ins, outs, scratch):
            blocks, pieces = ins[:S], ins[S:]
            qkv, small = outs
            x_all, weight, packed, sems = scratch
            copies = Copies(sems)
            for k in range(2):
                at = w[AT_X] if k == 0 else 1 - w[AT_X]
                copies.add(pieces[k].at[:, pl.ds(0, shard)], weight.at[:, at])
                copies.add(pieces[k].at[:, pl.ds(shard, 16), pl.ds(0, 2 * shard)], packed.at[:, at])
            for n in range(S):
                copies.add(blocks[n], x_all.at[span(w[SEQ + n], t)])
            copies.wait()
            small[...] = jnp.zeros_like(small)
            for n in range(F):
                lanes = slice(n * shard, (n + 1) * shard)
                small[0:16, lanes] = packed[n // X, n % X, :, 0:shard].astype(f32)
                small[16:24, lanes] = packed[n // X, n % X, 0:8, shard : 2 * shard].astype(f32)
            mine = span(w[MINE], hw)
            biases = [small[0:1, mine], jnp.zeros((1, hw), f32), small[1:2, mine]]
            for n in range(S):
                rows = slice(n * t, (n + 1) * t)
                for m in range(3):
                    cols = slice(m * hw, (m + 1) * hw)
                    value = dot(x_all[rows, :], weight[..., cols].reshape(D, hw), nn) + biases[m]
                    qkv[rows, cols] = value.astype(bf16)

        qkv, small = stage(
            project_qkv,
            where,
            [hbm(b) for b in x_blocks] + [hbm(p) for p in got_qkv],
            [((T, 3 * hw), bf16), ((small_rows, D), f32)],
            [
                pltpu.VMEM((T, D), bf16),
                pltpu.VMEM((Z, X, shard, 3 * hw), bf16),
                pltpu.VMEM((Z, X, 16, 2 * shard), bf16),
                pltpu.SemaphoreType.DMA((4 + S,)),
            ],
        )

        pairs = hw // (2 * HD)
        pair = 2 * HD

        def qkv_spec(m):
            return pl.BlockSpec((T, pair), lambda g, i, _: (0, m * pairs + g))

        rows_2 = 2 * t

        def masked(w, i, scores):
            key_pos = lax.broadcasted_iota(jnp.int32, scores.shape, 0)
            query_pos = i * rows_2 + lax.broadcasted_iota(jnp.int32, (1, rows_2), 1)
            limit = jnp.minimum(w[LENGTH], (query_pos // BLK + 1) * BLK)
            return jnp.where(key_pos < limit, scores, masked_value)

        def forward_pair(queries, k_ref, v_ref, key_count, mask, lse_ref):
            parts, lses = [], []
            for h in range(2):
                cols = slice(h * HD, (h + 1) * HD)
                query = queries[:, cols] * jnp.asarray(score_scale, bf16)
                scores = mask(dot(k_ref[:key_count, cols], query, nt))
                top = jnp.max(scores, axis=0, keepdims=True)
                weights = jnp.exp(scores - top)
                totals = jnp.sum(weights, axis=0, keepdims=True)
                value = dot(v_ref[:key_count, cols], weights.astype(bf16), tn)
                parts.append(value * (1.0 / totals))
                lses.append(top + jnp.log(totals))
            lse_ref[0] = jnp.concatenate(lses, axis=0)
            return jnp.concatenate(parts, axis=0).T.astype(bf16)

        def step_cases(i, visit):
            for n in range(T // rows_2):

                @pl.when(i == n)
                def _(n=n):
                    visit((n + 1) * rows_2)

        def self_forward(w, q_ref, k_ref, v_ref, *outs):
            i = pl.program_id(1)

            def visit(key_count):
                mask = functools.partial(masked, w, i)
                out = forward_pair(q_ref[...], k_ref, v_ref, key_count, mask, outs[S])
                for n in range(S):
                    for b in range(2):

                        @pl.when(w[SEQ + n] == 2 * i + b)
                        def _(n=n, b=b):
                            outs[n][...] = out[b * t : (b + 1) * t]

            step_cases(i, visit)

        q_block = pl.BlockSpec((rows_2, pair), lambda g, i, _: (i, g))
        row_block = pl.BlockSpec((t, pair), lambda g, i, _: (0, g))
        lse_block = pl.BlockSpec((1, 2, rows_2), lambda g, i, _: (g, 0, i))
        *attn_sent, self_lse = pl.pallas_call(
            self_forward,
            grid_spec=pltpu.PrefetchScalarGridSpec(
                num_scalar_prefetch=1,
                grid=(pairs, T // rows_2),
                in_specs=[q_block, qkv_spec(1), qkv_spec(2)],
                out_specs=[row_block] * S + [lse_block],
            ),
            out_shape=[jax.ShapeDtypeStruct((t, hw), bf16)] * S
            + [jax.ShapeDtypeStruct((pairs, 2, T), f32)],
            compiler_params=pltpu.CompilerParams(vmem_limit_bytes=vmem_limit),
            cost_estimate=short,
        )(where, qkv, qkv, qkv)
        attn = exchange(attn_sent)

        w_ffn = lax.all_gather(after(chunk_ffn, qkv), "fsdp", axis=0, tiled=True).reshape(
            F, shard + fw, D
        )
        def project_memory(w, ins, outs, scratch):
            blocks, pieces, small_ref = ins[:S], ins[S : S + 2], ins[S + 2]
            kv, weight = outs
            m_all, sems = scratch
            copies = Copies(sems)
            for k in range(2):
                copies.add(pieces[k], weight.at[:, w[AT_X] if k == 0 else 1 - w[AT_X]])
            for n in range(S):
                copies.add(blocks[n], m_all.at[pl.ds(n * t, t)])
            copies.wait()
            bias = jnp.concatenate(
                [jnp.zeros((1, hw), f32), small_ref[4:5, span(w[MINE], hw)]], axis=1
            )
            for n in range(S):
                rows = slice(n * t, (n + 1) * t)
                value = dot(m_all[rows, :], weight[...].reshape(D, 2 * hw), nn) + bias
                kv[rows, :] = value.astype(bf16)

        kv_own, w_mem = stage(
            project_memory,
            where,
            [hbm(b) for b in m_blocks] + [hbm(p) for p in got_mem] + [after(small, attn[1])],
            [((T, 2 * hw), bf16), ((Z, X, shard, 2 * hw), bf16)],
            [pltpu.VMEM((T, D), bf16), pltpu.SemaphoreType.DMA((2 + S,))],
        )
        w_mem = w_mem.reshape(D, 2 * hw)
        kv_far = y_swap(kv_own)
        rest_own = after(rest_own, kv_own)
        rest_other = core_swap(rest_own)
        rest = [r.reshape(F, shard, rest_cols) for r in (rest_own, rest_other)]

        def load_out(copies, w, rest_refs, which, target):
            core = lax.rem(w[MINE], 2)
            for e in range(2):
                copies.add(
                    rest_refs[e].at[:, pl.ds(which * deep, deep), pl.ds(0, D)],
                    target.at[:, core if e == 0 else 1 - core],
                )

        def group_rows(weight, group):
            return weight[pl.ds(group * per_group, per_group)].reshape(hw, D)

        out_scratch = pltpu.VMEM((F, 2, deep, D), bf16)
        cq_scratch = pltpu.VMEM((2, F, shard, half), bf16)

        def first_stage(w, ins, outs, scratch):
            pieces, rest_refs, x_ref, small_ref = ins[:S], ins[S : S + 2], ins[S + 2], ins[S + 3]
            normed_ref, inverse_ref, low_ref, keep_ref, send_ref = outs
            weight, cq, sems = scratch
            copies = Copies(sems)
            load_out(copies, w, rest_refs, 0, weight)
            for e in range(2):
                copies.add(rest_refs[e].at[:, :, pl.ds(D, half)], cq.at[e])
            copies.wait()
            total = alpha_scale * x_ref[...].astype(f32) + small_ref[2:3, :]
            for n in range(S):
                total = total + dot(pieces[n][...], group_rows(weight, w[SEQ + n]), nn)
            value, normed, inverse = norm_rows(total, small_ref[7:8, :], small_ref[10:11, :])
            normed_ref[...] = normed
            inverse_ref[...] = inverse
            low = value.astype(bf16)
            low_ref[...] = low
            for e, target in ((1, send_ref), (0, keep_ref)):
                bias = jnp.concatenate(
                    [small_ref[3:4, span(w[SEQ + 2 * e + k], hw)] for k in range(2)], axis=1
                )
                target[...] = (dot(low, cq[e].reshape(D, half), nn) + bias).astype(bf16)

        normed_one, inverse_one, first_low, cq_keep, cq_send = stage(
            first_stage,
            where,
            attn + [hbm(r) for r in rest] + [hidden_in, small],
            [
                ((t, D), f32), ((t, 1), f32), ((t, D), bf16), ((t, half), bf16), ((t, half), bf16),
            ],
            [out_scratch, cq_scratch, pltpu.SemaphoreType.DMA((4,))],
        )
        cq_other = core_swap(cq_send)

        def kv_specs():
            near = [
                pl.BlockSpec((T, pair), lambda g, i, _, m=m: (0, m * pairs + jnp.minimum(g, pairs - 1)))
                for m in range(2)
            ]
            far = [
                pl.BlockSpec((T, pair), lambda g, i, _, m=m: (0, m * pairs + jnp.maximum(g - pairs, 0)))
                for m in range(2)
            ]
            return near + far

        def cross_forward(w, qa_ref, qb_ref, k0, v0, k1, v1, oa_ref, ob_ref, lse_ref):
            g = pl.program_id(0)
            for gi, (k_ref, v_ref) in enumerate(((k0, v0), (k1, v1))):

                @pl.when(g // pairs == gi)
                def _(k_ref=k_ref, v_ref=v_ref):
                    queries = jnp.concatenate([qa_ref[...], qb_ref[...]], axis=0)
                    out = forward_pair(queries, k_ref, v_ref, T, lambda scores: scores, lse_ref)
                    oa_ref[...] = out[:t]
                    ob_ref[...] = out[t:]

        cross_keep, cross_send, cross_lse = pl.pallas_call(
            cross_forward,
            grid_spec=pltpu.PrefetchScalarGridSpec(
                num_scalar_prefetch=1,
                grid=(2 * pairs, 1),
                in_specs=[row_block, row_block] + kv_specs(),
                out_specs=[row_block, row_block, lse_block],
            ),
            out_shape=[jax.ShapeDtypeStruct((t, half), bf16)] * 2
            + [jax.ShapeDtypeStruct((2 * pairs, 2, 2 * t), f32)],
            compiler_params=pltpu.CompilerParams(vmem_limit_bytes=vmem_limit),
            cost_estimate=short,
        )(where, cq_keep, cq_other, kv_own, kv_own, kv_far, kv_far)
        cross_other = core_swap(cross_send)

        def halves(keep_ref, other_ref):
            return [
                ref[:, h * hw : (h + 1) * hw] for ref in (keep_ref, other_ref) for h in range(2)
            ]

        def second_stage(w, ins, outs, scratch):
            keep_ref, other_ref, normed_one_ref, small_ref = ins[:4]
            rest_refs = ins[4:]
            normed_ref, inverse_ref, low_ref = outs
            weight, sems = scratch
            copies = Copies(sems)
            load_out(copies, w, rest_refs, 1, weight)
            copies.wait()
            first = normed_one_ref[...] * small_ref[7:8, :] + small_ref[10:11, :]
            total = alpha_scale * first + small_ref[5:6, :]
            for n, piece in enumerate(halves(keep_ref, other_ref)):
                total = total + dot(piece, group_rows(weight, w[SEQ + n]), nn)
            value, normed, inverse = norm_rows(total, small_ref[8:9, :], small_ref[11:12, :])
            normed_ref[...] = normed
            inverse_ref[...] = inverse
            low_ref[...] = value.astype(bf16)

        normed_two, inverse_two, second_low = stage(
            second_stage,
            where,
            [cross_keep, cross_other, normed_one, small] + [hbm(r) for r in rest],
            [((t, D), f32), ((t, 1), f32), ((t, D), bf16)],
            [out_scratch, pltpu.SemaphoreType.DMA((2,))],
        )
        second_far = y_swap(second_low)
        second = [second_low, second_far, core_swap(second_low), None]

        ffn_scratch = [
            pltpu.VMEM((F, shard, D), bf16),
            pltpu.VMEM((F, fw, D), bf16),
            pltpu.SemaphoreType.DMA((2,)),
        ]

        def load_ffn(w_ref, scratch):
            copies = Copies(scratch[2])
            copies.add(w_ref.at[:, pl.ds(0, shard)], scratch[0])
            copies.add(w_ref.at[:, pl.ds(shard, fw)], scratch[1])
            copies.wait()
            return scratch[0], scratch[1]

        def ffn_forward(w, ins, outs, scratch):
            block_refs, small_ref, w_ref = ins[:2], ins[2], ins[3]
            part_refs, hidden_ref, slope_ref = outs[:2], outs[2], outs[3]
            w_in, w_out = load_ffn(w_ref, scratch)
            bias = small_ref[pl.ds(13 + w[MINE], 1), :]
            for n in range(2):
                rows = slice(n * t, (n + 1) * t)
                pre = dot(block_refs[n][...], w_in[...].reshape(D, F * fw), nn) + bias
                value, slope = gelu_both(pre)
                low = value.astype(bf16)
                hidden_ref[rows, :] = low
                slope_ref[rows, :] = slope.astype(bf16)
                out = dot(low, w_out[...].reshape(F * fw, D), nn)
                part_refs[n][...] = out.astype(part_refs[n].dtype)

        def ffn_call(blocks):
            return stage(
                ffn_forward,
                where,
                blocks + [small, hbm(w_ffn)],
                [((t, D), bf16), ((t, D), bf16), ((2 * t, F * fw), bf16), ((2 * t, F * fw), bf16)],
                ffn_scratch,
            )

        ffn_part_0, ffn_part_2, hidden_a, slope_a = ffn_call([second[0], second[2]])
        ffn_near = core_swap(ffn_part_2)
        second[1] = after(second_far, ffn_part_0)
        second[3] = core_swap(second[1])
        ffn_part_1, ffn_part_3, hidden_b, slope_b = ffn_call([second[1], second[3]])

        def add_pair(left, right):
            return (left.astype(f32) + right.astype(f32)).astype(bf16)

        ffn_far = y_swap(add_pair(ffn_part_1, core_swap(ffn_part_3)))

        def third_stage(w, ins, outs, _):
            a, b, far, normed_two_ref, small_ref, grad_ref = ins
            out_ref, d_ref, low_ref, sums_ref = outs
            second_rows = normed_two_ref[...] * small_ref[8:9, :] + small_ref[11:12, :]
            branch = a[...].astype(f32) + b[...].astype(f32) + far[...].astype(f32)
            total = alpha_scale * second_rows + branch + small_ref[6:7, :]
            value, normed, inverse = norm_rows(total, small_ref[9:10, :], small_ref[12:13, :])
            out_ref[...] = value.astype(bf16)
            d, gain, shift = norm_rows_back(
                grad_ref[...].astype(f32), normed, inverse, small_ref[9:10, :]
            )
            d_ref[...] = d
            low = d.astype(bf16)
            low_ref[...] = low
            sums_ref[0:1, :] = row_sum(low)
            sums_ref[1:2, :] = gain
            sums_ref[2:3, :] = shift

        layer_out, d_three, d_ffn_own, sums_three = stage(
            third_stage,
            where,
            [ffn_part_0, ffn_near, ffn_far, normed_two, small, out_grad],
            [((t, D), bf16), ((t, D), f32), ((t, D), bf16), ((8, D), f32)],
        )
        d_ffn_far = y_swap(d_ffn_own)
        d_ffn = [d_ffn_own, d_ffn_far, core_swap(d_ffn_own), None]

        def ffn_backward(w, ins, outs, scratch):
            block_refs, slope_ref, w_ref = ins[:2], ins[2], ins[3]
            part_refs, d_pre_ref = outs[:2], outs[2]
            w_in, w_out = load_ffn(w_ref, scratch)
            for n in range(2):
                rows = slice(n * t, (n + 1) * t)
                d_hidden = dot(block_refs[n][...], w_out[...].reshape(F * fw, D), nt)
                d_pre = (slope_ref[rows, :].astype(f32) * d_hidden).astype(bf16)
                d_pre_ref[rows, :] = d_pre
                out = dot(d_pre, w_in[...].reshape(D, F * fw), nt)
                part_refs[n][...] = out.astype(bf16)

        def ffn_back_call(blocks, slope):
            return stage(
                ffn_backward,
                where,
                blocks + [slope, hbm(w_ffn)],
                [((t, D), bf16), ((t, D), bf16), ((2 * t, F * fw), bf16)],
                ffn_scratch,
            )

        d2_part_0, d2_part_2, d_pre_a = ffn_back_call([d_ffn[0], d_ffn[2]], slope_a)
        d2_near = core_swap(d2_part_2)
        d_ffn[1] = after(d_ffn_far, d2_part_0)
        d_ffn[3] = core_swap(d_ffn[1])
        d2_part_1, d2_part_3, d_pre_b = ffn_back_call([d_ffn[1], d_ffn[3]], slope_b)
        d2_sent = add_pair(d2_part_1, core_swap(d2_part_3))
        d2_far = y_swap(d2_sent)

        def ffn_grads(w, ins, outs, scratch):
            x_refs, g_refs, hidden_a_ref, hidden_b_ref, pre_a_ref, pre_b_ref = (
                ins[0:4], ins[4:8], *ins[8:12],
            )
            grads, sums_ref = outs
            x_rows, g_rows = scratch
            for n in range(S):
                at = (0, 2, 1, 3)[n] * t
                x_rows[at : at + t, :] = x_refs[n][...]
                g_rows[at : at + t, :] = g_refs[n][...]
            for n in range(F):
                cols = slice(n * fw, (n + 1) * fw)
                rows = slice(n * shard, (n + 1) * shard)
                value = dot(x_rows[: 2 * t, rows], pre_a_ref[...], tn)
                value = value + dot(x_rows[2 * t :, rows], pre_b_ref[...], tn)
                grads[n, 0:shard, :] = value.astype(bf16)
                value = dot(hidden_a_ref[:, cols], g_rows[: 2 * t, :], tn)
                value = value + dot(hidden_b_ref[:, cols], g_rows[2 * t :, :], tn)
                grads[n, shard:, :] = value.astype(bf16)
            sums_ref[0:1, :] = row_sum(pre_a_ref[...]) + row_sum(pre_b_ref[...])

        grad_ffn, sums_ffn = stage(
            ffn_grads,
            where,
            second + d_ffn + [after(hidden_a, d2_sent), hidden_b, d_pre_a, d_pre_b],
            [((F, shard + fw, D), bf16), ((8, D), f32)],
            [pltpu.VMEM((T, D), bf16), pltpu.VMEM((T, D), bf16)],
            time=12,
        )
        def second_back(w, ins, outs, scratch):
            a, b, far, d_three_ref, normed_ref, inverse_ref, small_ref = ins[:7]
            rest_refs = ins[7:]
            d_ref, low_ref, keep_ref, send_ref, sums_ref = outs
            weight, sems = scratch
            copies = Copies(sems)
            load_out(copies, w, rest_refs, 1, weight)
            total = alpha_scale * d_three_ref[...]
            total = total + a[...].astype(f32) + b[...].astype(f32) + far[...].astype(f32)
            d, gain, shift = norm_rows_back(
                total, normed_ref[...], inverse_ref[...], small_ref[8:9, :]
            )
            d_ref[...] = d
            low = d.astype(bf16)
            low_ref[...] = low
            sums_ref[0:1, :] = row_sum(low)
            sums_ref[1:2, :] = gain
            sums_ref[2:3, :] = shift
            copies.wait()
            for n in range(S):
                target = keep_ref if n < 2 else send_ref
                value = dot(low, group_rows(weight, w[SEQ + n]), nt)
                target[:, (n % 2) * hw : (n % 2 + 1) * hw] = value.astype(bf16)

        d_two, d_cross, dc_keep, dc_send, sums_two = stage(
            second_back,
            where,
            [d2_part_0, d2_near, d2_far, after(d_three, grad_ffn), normed_two, inverse_two, small]
            + [hbm(r) for r in rest],
            [
                ((t, D), f32), ((t, D), bf16), ((t, half), bf16), ((t, half), bf16), ((8, D), f32),
            ],
            [out_scratch, pltpu.SemaphoreType.DMA((2,))],
        )
        dc_other = core_swap(dc_send)
        own_ffn = lax.psum_scatter(
            after(grad_ffn, d_cross).reshape(F * (shard + fw), D),
            "fsdp",
            scatter_dimension=0,
            tiled=True,
        )

        def backward_pair(queries, k_ref, v_ref, grads, lse_ref, key_count, mask, dk_acc, dv_acc):
            dqs = []
            for h in range(2):
                cols = slice(h * HD, (h + 1) * HD)
                query = queries[:, cols] * jnp.asarray(score_scale, bf16)
                grad = grads[:, cols]
                scores = mask(dot(k_ref[:key_count, cols], query, nt))
                weights = jnp.exp(scores - lse_ref[0, h : h + 1, :])
                dv_acc[h, :key_count, :] += dot(weights.astype(bf16), grad, nn)
                grad_weights = dot(v_ref[:key_count, cols], grad, nt)
                row_term = jnp.sum(grad_weights * weights, axis=0, keepdims=True)
                low = (weights * (grad_weights - row_term)).astype(bf16)
                dk_acc[h, :key_count, :] += dot(low, query, nn)
                dqs.append(dot(k_ref[:key_count, cols], low, tn) * score_scale)
            return jnp.concatenate(dqs, axis=0).T.astype(bf16)

        def sums_out(ref, acc):
            ref[...] = jnp.concatenate([acc[h].astype(bf16) for h in range(2)], axis=1)

        def cross_backward(
            w, qa, qb, k0, v0, k1, v1, ga, gb, lse_ref, da, db, dk0, dv0, dk1, dv1, dk_acc, dv_acc
        ):
            g = pl.program_id(0)
            dk_acc[...] = jnp.zeros_like(dk_acc)
            dv_acc[...] = jnp.zeros_like(dv_acc)
            for gi, (k_ref, v_ref, dk_ref, dv_ref) in enumerate(
                ((k0, v0, dk0, dv0), (k1, v1, dk1, dv1))
            ):

                @pl.when(g // pairs == gi)
                def _(k_ref=k_ref, v_ref=v_ref, dk_ref=dk_ref, dv_ref=dv_ref):
                    queries = jnp.concatenate([qa[...], qb[...]], axis=0)
                    grads = jnp.concatenate([ga[...], gb[...]], axis=0)
                    out = backward_pair(
                        queries, k_ref, v_ref, grads, lse_ref, T, lambda scores: scores, dk_acc,
                        dv_acc,
                    )
                    da[...] = out[:t]
                    db[...] = out[t:]
                    sums_out(dk_ref, dk_acc)
                    sums_out(dv_ref, dv_acc)

        def near_block(m):
            return pl.BlockSpec((T, pair), lambda g, i, _: (0, jnp.minimum(g, pairs - 1)))

        def far_block(m):
            return pl.BlockSpec((T, pair), lambda g, i, _: (0, jnp.maximum(g - pairs, 0)))

        acc_scratch = [pltpu.VMEM((2, T, HD), f32), pltpu.VMEM((2, T, HD), f32)]
        dq_keep, dq_send, dk_own, dv_own, dk_far, dv_far = pl.pallas_call(
            cross_backward,
            grid_spec=pltpu.PrefetchScalarGridSpec(
                num_scalar_prefetch=1,
                grid=(2 * pairs, 1),
                in_specs=[row_block, row_block]
                + kv_specs()
                + [row_block, row_block, lse_block],
                out_specs=[row_block, row_block]
                + [near_block(0), near_block(1), far_block(0), far_block(1)],
                scratch_shapes=acc_scratch,
            ),
            out_shape=[jax.ShapeDtypeStruct((t, half), bf16)] * 2
            + [jax.ShapeDtypeStruct((T, hw), bf16)] * 4,
            compiler_params=pltpu.CompilerParams(vmem_limit_bytes=vmem_limit),
            cost_estimate=short,
        )(
            where, cq_keep, cq_other, kv_own, kv_own, kv_far, kv_far, dc_keep, dc_other,
            cross_lse,
        )
        dq_other = core_swap(dq_send)

        def first_back(w, ins, outs, scratch):
            keep_ref, other_ref, d_two_ref, normed_ref, inverse_ref, small_ref = ins[:6]
            rest_refs = ins[6:]
            d_ref, low_ref = outs[0], outs[1]
            sent_refs, sums_ref = outs[2 : 2 + S], outs[2 + S]
            weight, cq, sems = scratch
            copies = Copies(sems)
            for e in range(2):
                copies.add(rest_refs[e].at[:, :, pl.ds(D, half)], cq.at[e])
            load_out(copies, w, rest_refs, 0, weight)
            copies.wait()
            total = alpha_scale * d_two_ref[...]
            for e, ref in enumerate((keep_ref, other_ref)):
                total = total + dot(ref[...], cq[e].reshape(D, half), nt)
            for n, piece in enumerate(halves(keep_ref, other_ref)):
                sums_ref[3:4, span(w[SEQ + n], hw)] = row_sum(piece)
            d, gain, shift = norm_rows_back(
                total, normed_ref[...], inverse_ref[...], small_ref[7:8, :]
            )
            d_ref[...] = d
            low = d.astype(bf16)
            low_ref[...] = low
            sums_ref[0:1, :] = row_sum(low)
            sums_ref[1:2, :] = gain
            sums_ref[2:3, :] = shift
            for n in range(S):
                value = dot(low, group_rows(weight, w[SEQ + n]), nt)
                sent_refs[n][...] = value.astype(bf16)

        d_one, d_branch, *d_attn_sent, sums_one = stage(
            first_back,
            where,
            [dq_keep, dq_other, d_two, normed_one, inverse_one, small] + [hbm(r) for r in rest],
            [((t, D), f32), ((t, D), bf16)] + [((t, hw), bf16)] * S + [((8, D), f32)],
            [out_scratch, cq_scratch, pltpu.SemaphoreType.DMA((4,))],
        )
        d_attn = exchange(d_attn_sent)

        def middle_grads(w, ins, outs, scratch):
            dq_keep_ref, dq_other_ref, low_ref, d_one_ref, co_keep, co_other, d_two_ref = ins[:7]
            attn_refs = ins[7:]
            own, cross = scratch
            core = lax.rem(w[MINE], 2)
            for e, ref in enumerate((dq_keep_ref, dq_other_ref)):
                value = dot(low_ref[...], ref[...], tn)
                outs[e][:, :, D:] = value.astype(bf16).reshape(F, shard, half)
            for n, piece in enumerate(halves(co_keep, co_other)):
                value = dot(piece, d_two_ref[...], tn).astype(bf16)
                cross[pl.ds(w[SEQ + n] * per_group, per_group)] = value.reshape(
                    per_group, 2, deep, D
                )
                value = dot(attn_refs[n][...], d_one_ref[...], tn).astype(bf16)
                own[pl.ds(w[SEQ + n] * per_group, per_group)] = value.reshape(per_group, 2, deep, D)
            for e in range(2):
                at = core if e == 0 else 1 - core
                outs[e][:, 0:deep, 0:D] = own[:, at]
                outs[e][:, deep:, 0:D] = cross[:, at]

        middle_keep, middle_send = stage(
            middle_grads,
            where,
            [dq_keep, dq_other, first_low, after(d_branch, d_attn_sent[1]), cross_keep, cross_other]
            + [d_cross, *attn],
            [((F, shard, rest_cols), bf16)] * 2,
            [out_scratch, out_scratch],
        )
        middle_got = core_swap(middle_send)

        def scatter_terms(parts):
            return [parts[0], core_swap(parts[2]), y_swap(add_pair(parts[1], core_swap(parts[3])))]

        def split_x(w, value, keep_ref, send_ref):
            size = keep_ref.shape[0] // Z
            for n in range(Z):
                rows = slice(n * size, (n + 1) * size)
                keep_ref[rows, :] = value[span(n * X + w[AT_X], size), :]
                send_ref[rows, :] = value[span(n * X + 1 - w[AT_X], size), :]

        def z_sum(sent):
            rows, cols = sent.shape[0] // Z, sent.shape[1]
            terms = z_exchange(sent).reshape(Z, rows, cols)
            return jnp.sum(terms.astype(f32), axis=0).astype(bf16)

        dk_got, dv_got = (y_swap(after(d, d_attn[1])) for d in (dk_far, dv_far))

        def pack_rest(w, ins, outs, _):
            for n in range(Z):
                for out, at in ((outs[0], w[AT_X]), (outs[1], 1 - w[AT_X])):
                    value = ins[0][n * X + at].astype(f32) + ins[1][n * X + at].astype(f32)
                    out[n * shard : (n + 1) * shard, :] = value.astype(bf16)

        rest_keep, rest_send = stage(
            pack_rest,
            where,
            [after(middle_keep, d_attn[1]), middle_got],
            [((Z * shard, rest_cols), bf16)] * 2,
        )
        rest_got = x_shift(rest_send, 1)

        def self_backward(w, q_ref, k_ref, v_ref, *refs):
            grads, lse_ref = refs[:S], refs[S]
            dq_ref, dk_ref, dv_ref, dk_acc, dv_acc, g_rows = refs[S + 1 :]
            i = pl.program_id(1)

            @pl.when(i == 0)
            def _():
                dk_acc[...] = jnp.zeros_like(dk_acc)
                dv_acc[...] = jnp.zeros_like(dv_acc)
                for n in range(S):
                    g_rows[span(w[SEQ + n], t), :] = grads[n][...]

            def visit(key_count):
                dq_ref[...] = backward_pair(
                    q_ref[...], k_ref, v_ref, g_rows[span(i, rows_2), :], lse_ref, key_count,
                    functools.partial(masked, w, i), dk_acc, dv_acc,
                )

            step_cases(i, visit)

            @pl.when(i == T // rows_2 - 1)
            def _():
                sums_out(dk_ref, dk_acc)
                sums_out(dv_ref, dv_acc)

        key_block = pl.BlockSpec((T, pair), lambda g, i, _: (0, g))
        dq_self, dk_self, dv_self = pl.pallas_call(
            self_backward,
            grid_spec=pltpu.PrefetchScalarGridSpec(
                num_scalar_prefetch=1,
                grid=(pairs, T // rows_2),
                in_specs=[q_block, qkv_spec(1), qkv_spec(2)] + [row_block] * S + [lse_block],
                out_specs=[q_block, key_block, key_block],
                scratch_shapes=acc_scratch + [pltpu.VMEM((T, pair), bf16)],
            ),
            out_shape=[jax.ShapeDtypeStruct((T, hw), bf16)] * 3,
            compiler_params=pltpu.CompilerParams(vmem_limit_bytes=vmem_limit),
            cost_estimate=short,
        )(where, qkv, qkv, qkv, *d_attn, after(self_lse, rest_keep))

        tall = shard + 16

        def place_small(small_sums, value):
            for n in range(F):
                lanes = slice(n * shard, (n + 1) * shard)
                at = n * tall + shard
                value[at : at + 16, 0:shard] = small_sums[0:16, lanes].astype(bf16)
                rest_rows = [small_sums[16:, lanes], jnp.zeros((32 - small_rows, shard), f32)]
                value[at : at + 16, shard : 2 * shard] = jnp.concatenate(
                    rest_rows, axis=0
                ).astype(bf16)

        def last_grads(w, ins, outs, scratch):
            dq, dk, dv, one, two, three, ffn = ins[:7]
            mem_refs, weight = ins[7:11], ins[11]
            blocks, mem_blocks = ins[12 : 12 + S], ins[12 + S :]
            keep_ref, send_ref = outs[S], outs[S + 1]
            x_all, m_all, d_all, value, small_sums, sems = scratch
            copies = Copies(sems)
            for n in range(S):
                copies.add(blocks[n], x_all.at[span(w[SEQ + n], t)])
            for n in range(S):
                copies.add(mem_blocks[n], m_all.at[pl.ds(n * t, t)])
            for m in range(2):
                near, far = mem_refs[m], mem_refs[2 + m]
                for n in range(S):
                    rows = slice(n * t, (n + 1) * t)
                    total = near[rows, :].astype(f32) + far[rows, :].astype(f32)
                    d_all[rows, m * hw : (m + 1) * hw] = total.astype(bf16)
            for n in (3, 2, 1, 0):
                total = dot(d_all[n * t : (n + 1) * t, :], weight[...], nt)
                outs[n][...] = total.astype(bf16)
            copies.wait()

            def store(grad, cols):
                for n in range(F):
                    value[n * tall : n * tall + shard, cols] = grad[n * shard : (n + 1) * shard]

            for m, d in enumerate((dq, dk, dv)):
                grad = dot(x_all[...], d[...], tn).astype(bf16)
                store(grad, slice(m * hw, (m + 1) * hw))
            grad = dot(m_all[...], d_all[...], tn).astype(bf16)
            store(grad, slice(3 * hw, 5 * hw))
            small_sums[...] = jnp.zeros_like(small_sums)
            mine = span(w[MINE], hw)
            small_sums[0:1, mine] = row_sum(dq[...])
            small_sums[1:2, mine] = row_sum(dv[...])
            small_sums[4:5, mine] = row_sum(d_all[:, hw:])
            rows = [
                (2, one, 0), (3, one, 3), (5, two, 0), (6, three, 0), (7, one, 1), (8, two, 1),
                (9, three, 1), (10, one, 2), (11, two, 2), (12, three, 2),
            ]
            for at, ref, row in rows:
                small_sums[at : at + 1, :] = ref[row : row + 1, :]
            small_sums[pl.ds(13 + w[MINE], 1), :] = ffn[0:1, :]
            place_small(small_sums, value)
            split_x(w, value, keep_ref, send_ref)

        *mem_parts, last_keep, last_send = stage(
            last_grads,
            where,
            [dq_self, dk_self, dv_self, sums_one, sums_two, sums_three, sums_ffn]
            + [dk_own, dv_own, dk_got, dv_got, w_mem]
            + [hbm(b) for b in x_blocks + m_blocks],
            [((t, D), bf16)] * S + [((Z * tall, 5 * hw), bf16)] * 2,
            [
                pltpu.VMEM((T, D), bf16),
                pltpu.VMEM((T, D), bf16),
                pltpu.VMEM((T, 2 * hw), bf16),
                pltpu.VMEM((F * tall, 5 * hw), bf16),
                pltpu.VMEM((small_rows, D), f32),
                pltpu.SemaphoreType.DMA((2 * S,)),
            ],
        )
        last_got = x_shift(last_send, 1)
        rest_sent = add_pair(rest_keep, after(rest_got, last_keep))

        def input_parts(w, ins, outs, scratch):
            grads, pieces = ins[:3], ins[3:]
            weight, sems = scratch
            copies = Copies(sems)
            for k in range(2):
                at = w[AT_X] if k == 0 else 1 - w[AT_X]
                copies.add(pieces[k].at[:, pl.ds(0, shard)], weight.at[:, at])
            copies.wait()
            for n in (3, 2, 1, 0):
                rows = span(w[SEQ + n], t)
                value = None
                for m in range(3):
                    part_of = weight[..., m * hw : (m + 1) * hw].reshape(D, hw)
                    term = dot(grads[m][rows, :], part_of, nt)
                    value = term if value is None else value + term
                outs[n][...] = value.astype(bf16)

        in_parts = stage(
            input_parts,
            where,
            [after(dq_self, last_got), dk_self, dv_self] + [hbm(p) for p in got_qkv],
            [((t, D), bf16)] * S,
            [pltpu.VMEM((Z, X, shard, 3 * hw), bf16), pltpu.SemaphoreType.DMA((2,))],
        )
        in_terms = scatter_terms(in_parts)
        memory_grad = sum(term.astype(f32) for term in scatter_terms(mem_parts)).astype(bf16)
        input_grad = (
            alpha_scale * d_one + sum(term.astype(f32) for term in in_terms)
        ).astype(bf16)


        def finish_ffn(w, ins, outs, _):
            for n in range(S):
                for m in range(F):
                    lanes = pl.ds(pl.multiple_of(m * S * fw + w[SEQ + n] * fw, fw), fw)
                    outs[0][:, lanes] = ins[n][0:shard, m * fw : (m + 1) * fw].astype(f32)
                outs[1][span(w[SEQ + n], fw), :] = ins[n][shard:, :].astype(f32)

        grad_fin, grad_fout = stage(
            finish_ffn,
            where,
            seq_gather(after(own_ffn, last_keep)),
            [((shard, FF), f32), ((S * fw, D), f32)],
        )

        own_rest = z_sum(rest_sent)
        last_sent = add_pair(
            last_keep, after(last_got, own_rest, grad_fin, memory_grad)
        )
        own_last = z_sum(last_sent)

        def sum_chips(w, ins, outs, _):
            near, away = ins
            out = outs[0]
            out[:, 0:D] = (near[:, 0:D].astype(f32) + away[:, 0:D].astype(f32)).astype(bf16)
            for k in range(2):
                mine = slice(D + k * hw, D + (k + 1) * hw)
                theirs = slice(D + (1 - k) * hw, D + (2 - k) * hw)
                out[:, mine] = (near[:, mine].astype(f32) + away[:, theirs].astype(f32)).astype(bf16)

        (rest_sum,) = stage(
            sum_chips, where, [own_rest, y_swap(own_rest)], [((shard, rest_cols), bf16)]
        )

        def finish_rest(w, ins, outs, _):
            query, own, cross = outs
            core = lax.rem(w[MINE], 2)
            for e in range(2):
                rows = span(core if e == 0 else 1 - core, deep)
                own[rows, :] = ins[e][0:deep, 0:D].astype(f32)
                cross[rows, :] = ins[e][deep:, 0:D].astype(f32)
                for k in range(2):
                    query[:, span(w[SEQ + 2 * e + k], hw)] = ins[e][
                        :, D + k * hw : D + (k + 1) * hw
                    ].astype(f32)

        grad_query, grad_self_out, grad_cross_out = stage(
            finish_rest, where, [rest_sum, core_swap(rest_sum)], [((shard, D), f32)] * 3
        )

        def finish_last(w, ins, outs, _):
            for n in range(S):
                group = w[SEQ + n] * hw
                for m in range(5):
                    target, at = (outs[0], m) if m < 3 else (outs[1], m - 3)
                    lanes = pl.ds(pl.multiple_of(at * D + group, hw), hw)
                    target[:, lanes] = ins[n][0:shard, m * hw : (m + 1) * hw].astype(f32)
            outs[2][0:16, :] = sum(ins[n][shard:, 0:shard].astype(f32) for n in range(S))
            outs[2][16:, :] = sum(
                ins[n][shard : shard + 8, shard : 2 * shard].astype(f32) for n in range(S)
            )

        grad_self_in, grad_memory, small_own = stage(
            finish_last,
            where,
            seq_gather(own_last),
            [((shard, 3 * D), f32), ((shard, 2 * D), f32), ((small_rows, shard), f32)],
        )

        rows = [small_own[n] for n in range(7)]
        return (
            layer_out[None],
            input_grad[None],
            memory_grad[None],
            grad_self_in,
            rows[0],
            rows[1],
            grad_self_out,
            rows[2],
            grad_query,
            rows[3],
            grad_memory,
            rows[4],
            grad_cross_out,
            rows[5],
            grad_fin,
            small_own[13 : 13 + S].reshape(S * fw),
            grad_fout,
            rows[6],
            small_own[7:10],
            small_own[10:13],
        )

    return local


def solution(mesh):
    general, tiled = general_layer(mesh), tiled_layer(mesh)
    S, F = mesh.shape["seq"], mesh.shape["fsdp"]

    def local(*args):
        _, t, D = args[0].shape
        FF = args[15].shape[1]
        blocks = (D // F, D // S, FF // (F * S))
        whole_tiles = all(n % 128 == 0 for n in blocks) and D // F // 2 % 16 == 0
        if whole_tiles and S == 4 and F == 8 and t == BLK:
            return tiled(*args)
        return general(*args)

    by_row, rows_1d = P("fsdp", None), P("fsdp")
    tokens, norms = P("fsdp", "seq", None), P(None, "fsdp")
    in_specs = (
        tokens, tokens, rows_1d, tokens, by_row, rows_1d, rows_1d, by_row, rows_1d, by_row, rows_1d,
        by_row, rows_1d, by_row, rows_1d, by_row, rows_1d, by_row, rows_1d, norms, norms,
    )
    out_specs = (
        tokens, tokens, tokens, by_row, rows_1d, rows_1d, by_row, rows_1d, by_row, rows_1d, by_row,
        rows_1d, by_row, rows_1d, by_row, rows_1d, by_row, rows_1d, norms, norms,
    )
    return jax.shard_map(local, mesh=mesh, in_specs=in_specs, out_specs=out_specs, check_vma=False)
```

```python
import functools

import jax
import jax.numpy as jnp
from jax import lax
from jax.experimental import pallas as pl
from jax.experimental.pallas import tpu as pltpu
from jax.sharding import PartitionSpec as P

HD = 64
BLK = 256
CORES = 2

alpha_scale = 300.0**0.25
layer_eps = 1e-05
score_scale = 0.125
masked_value = -1e30
gelu_coef = 0.7978845608028654
gelu_cube = 0.044715

f32 = jnp.float32
bf16 = jnp.bfloat16
vmem_limit = 56 * 1024 * 1024


def dot(left, right, dims):
    return lax.dot_general(left, right, (dims, ((), ())), preferred_element_type=f32)


nn = ((1,), (0,))
nt = ((1,), (1,))
tn = ((0,), (0,))


def key_cases(total_keys, causal, block_index, visit):
    if not causal:
        visit(total_keys)
        return
    blocks = total_keys // BLK
    cases = min(4, blocks)
    for case in range(cases):
        low, high = case * blocks // cases, (case + 1) * blocks // cases

        @pl.when((block_index >= low) & (block_index < high))
        def _(high=high):
            visit(high * BLK)


def mask_scores(scores, first_key, limit):
    key_pos = first_key + lax.broadcasted_iota(jnp.int32, scores.shape, 0)
    return jnp.where(key_pos < limit, scores, masked_value)


def forward_kernel(causal, heads, chunk, len_ref, q_ref, k_ref, v_ref, o_ref, lse_ref):
    block_index = pl.program_id(1)
    total_keys = k_ref.shape[0]
    limit = jnp.minimum(len_ref[0], (block_index + 1) * BLK) if causal else 0
    rows = q_ref.shape[0]

    if total_keys <= chunk:

        def visit(key_count):
            outs, lses = [], []
            for h in range(heads):
                cols = slice(h * HD, (h + 1) * HD)
                query = q_ref[:, cols] * jnp.asarray(score_scale, bf16)
                scores = dot(k_ref[:key_count, cols], query, nt)
                if causal:
                    scores = mask_scores(scores, 0, limit)
                top = jnp.max(scores, axis=0, keepdims=True)
                weights = jnp.exp(scores - top)
                totals = jnp.sum(weights, axis=0, keepdims=True)
                low = (weights * (1.0 / totals)).astype(bf16)
                outs.append(dot(low, v_ref[:key_count, cols], tn).astype(bf16))
                lses.append(top + jnp.log(totals))
            o_ref[...] = outs[0] if heads == 1 else jnp.concatenate(outs, axis=1)
            lse_ref[0] = lses[0] if heads == 1 else jnp.concatenate(lses, axis=0)

        key_cases(total_keys, causal, block_index, visit)
    else:
        live = ((block_index + 1) * BLK + chunk - 1) // chunk if causal else total_keys // chunk
        outs, lses = [], []
        for h in range(heads):
            cols = slice(h * HD, (h + 1) * HD)
            query = q_ref[:, cols] * jnp.asarray(score_scale, bf16)

            def step(n, carry, cols=cols, query=query):
                top, totals, acc = carry
                span = pl.ds(pl.multiple_of(n * chunk, chunk), chunk)
                scores = dot(k_ref[span, cols], query, nt)
                if causal:
                    scores = mask_scores(scores, n * chunk, limit)
                new_top = jnp.maximum(top, jnp.max(scores, axis=0, keepdims=True))
                decay = jnp.exp(top - new_top)
                weights = jnp.exp(scores - new_top)
                totals = totals * decay + jnp.sum(weights, axis=0, keepdims=True)
                acc = acc * decay + dot(v_ref[span, cols], weights.astype(bf16), tn)
                return new_top, totals, acc

            start = (
                jnp.full((1, rows), masked_value, f32),
                jnp.zeros((1, rows), f32),
                jnp.zeros((HD, rows), f32),
            )
            top, totals, acc = lax.fori_loop(0, live, step, start)
            outs.append((acc / totals).T.astype(bf16))
            lses.append(top + jnp.log(totals))
        o_ref[...] = outs[0] if heads == 1 else jnp.concatenate(outs, axis=1)
        lse_ref[0] = lses[0] if heads == 1 else jnp.concatenate(lses, axis=0)


def backward_kernel(
    causal, heads, chunk, len_ref, q_ref, k_ref, v_ref, g_ref, lse_ref, dq_ref, dk_ref, dv_ref,
    dk_acc, dv_acc
):
    block_index = pl.program_id(1)
    total_keys = k_ref.shape[0]
    limit = jnp.minimum(len_ref[0], (block_index + 1) * BLK) if causal else 0

    @pl.when(block_index == 0)
    def _():
        dk_acc[...] = jnp.zeros_like(dk_acc)
        dv_acc[...] = jnp.zeros_like(dv_acc)

    def probabilities(query, span, cols, first_key, lse):
        scores = dot(k_ref[span, cols], query, nt)
        if causal:
            scores = mask_scores(scores, first_key, limit)
        return jnp.exp(scores - lse)

    if total_keys <= chunk:

        def visit(key_count):
            span = slice(0, key_count)
            dqs = []
            for h in range(heads):
                cols = slice(h * HD, (h + 1) * HD)
                query = q_ref[:, cols] * jnp.asarray(score_scale, bf16)
                grad = g_ref[:, cols]
                weights = probabilities(query, span, cols, 0, lse_ref[0, h : h + 1, :])
                dv_acc[h, span, :] += dot(weights.astype(bf16), grad, nn)
                grad_weights = dot(v_ref[span, cols], grad, nt)
                row_term = jnp.sum(grad_weights * weights, axis=0, keepdims=True)
                low = (weights * (grad_weights - row_term)).astype(bf16)
                dk_acc[h, span, :] += dot(low, query, nn)
                dqs.append((dot(low, k_ref[span, cols], tn) * score_scale).astype(bf16))
            dq_ref[...] = dqs[0] if heads == 1 else jnp.concatenate(dqs, axis=1)

        key_cases(total_keys, causal, block_index, visit)
    else:
        live = ((block_index + 1) * BLK + chunk - 1) // chunk if causal else total_keys // chunk
        rows = q_ref.shape[0]
        dqs = []
        for h in range(heads):
            cols = slice(h * HD, (h + 1) * HD)
            query = q_ref[:, cols] * jnp.asarray(score_scale, bf16)
            grad = g_ref[:, cols]
            lse = lse_ref[0, h : h + 1, :]

            def sums(n, row_term, cols=cols, query=query, grad=grad, lse=lse):
                span = pl.ds(pl.multiple_of(n * chunk, chunk), chunk)
                weights = probabilities(query, span, cols, n * chunk, lse)
                grad_weights = dot(v_ref[span, cols], grad, nt)
                return row_term + jnp.sum(grad_weights * weights, axis=0, keepdims=True)

            row_term = lax.fori_loop(0, live, sums, jnp.zeros((1, rows), f32))

            def step(n, acc, h=h, cols=cols, query=query, grad=grad, lse=lse, row_term=row_term):
                span = pl.ds(pl.multiple_of(n * chunk, chunk), chunk)
                weights = probabilities(query, span, cols, n * chunk, lse)
                dv_acc[h, span, :] += dot(weights.astype(bf16), grad, nn)
                grad_weights = dot(v_ref[span, cols], grad, nt)
                low = (weights * (grad_weights - row_term)).astype(bf16)
                dk_acc[h, span, :] += dot(low, query, nn)
                return acc + dot(low, k_ref[span, cols], tn)

            acc = lax.fori_loop(0, live, step, jnp.zeros((rows, HD), f32))
            dqs.append((acc * score_scale).astype(bf16))
        dq_ref[...] = dqs[0] if heads == 1 else jnp.concatenate(dqs, axis=1)

    @pl.when(block_index == pl.num_programs(1) - 1)
    def _():
        for ref, acc in ((dk_ref, dk_acc), (dv_ref, dv_acc)):
            parts = [acc[h].astype(bf16) for h in range(heads)]
            ref[...] = parts[0] if heads == 1 else jnp.concatenate(parts, axis=1)


def attention_specs(total_q, total_k, width):
    block = min(2 * HD, width)
    heads = block // HD
    groups = width // block
    rows = min(BLK, total_q)
    chunk = min(1024, total_k)
    q_spec = pl.BlockSpec((rows, block), lambda g, i, _: (i, g))
    k_spec = pl.BlockSpec((total_k, block), lambda g, i, _: (0, g))
    l_spec = pl.BlockSpec((1, heads, rows), lambda g, i, _: (g, 0, i))
    return block, heads, groups, rows, chunk, q_spec, k_spec, l_spec


def attend_forward(queries, keys, values, lengths, causal):
    total_q, width = queries.shape
    total_k = keys.shape[0]
    block, heads, groups, rows, chunk, q_spec, k_spec, l_spec = attention_specs(
        total_q, total_k, width
    )
    work = total_q * total_k * width
    return pl.pallas_call(
        functools.partial(forward_kernel, causal, heads, chunk),
        grid_spec=pltpu.PrefetchScalarGridSpec(
            num_scalar_prefetch=1,
            grid=(groups, total_q // rows),
            in_specs=[q_spec, k_spec, k_spec],
            out_specs=[q_spec, l_spec],
        ),
        out_shape=[
            jax.ShapeDtypeStruct((total_q, width), bf16),
            jax.ShapeDtypeStruct((groups, heads, total_q), f32),
        ],
        compiler_params=pltpu.CompilerParams(vmem_limit_bytes=vmem_limit),
        cost_estimate=pl.CostEstimate(
            flops=4 * work, bytes_accessed=8 * total_k * width, transcendentals=work // HD
        ),
    )(lengths, queries, keys, values)


def attend_back(queries, keys, values, grads, lse, lengths, causal):
    total_q, width = queries.shape
    total_k = keys.shape[0]
    block, heads, groups, rows, chunk, q_spec, k_spec, l_spec = attention_specs(
        total_q, total_k, width
    )
    work = total_q * total_k * width
    return pl.pallas_call(
        functools.partial(backward_kernel, causal, heads, chunk),
        grid_spec=pltpu.PrefetchScalarGridSpec(
            num_scalar_prefetch=1,
            grid=(groups, total_q // rows),
            in_specs=[q_spec, k_spec, k_spec, q_spec, l_spec],
            out_specs=[q_spec, k_spec, k_spec],
            scratch_shapes=[
                pltpu.VMEM((heads, total_k, HD), f32),
                pltpu.VMEM((heads, total_k, HD), f32),
            ],
        ),
        out_shape=[
            jax.ShapeDtypeStruct((total_q, width), bf16),
            jax.ShapeDtypeStruct((total_k, width), bf16),
            jax.ShapeDtypeStruct((total_k, width), bf16),
        ],
        compiler_params=pltpu.CompilerParams(vmem_limit_bytes=vmem_limit),
        cost_estimate=pl.CostEstimate(
            flops=10 * work, bytes_accessed=16 * total_k * width, transcendentals=work // HD
        ),
    )(lengths, queries, keys, values, grads, lse)


def assemble(arrays, moves, shape):
    dtype = arrays[0].dtype
    if any(m[2] % 16 or m[4] % 128 or m[1] % 16 or m[3] % 128 for m in moves):
        result = jnp.zeros(shape, dtype)
        for index, row, rows, col, cols, to_row, to_col in moves:
            part = arrays[index][row : row + rows, col : col + cols]
            result = lax.dynamic_update_slice(result, part, (to_row, to_col))
        return result
    count = len(arrays)
    places = jnp.stack([jnp.asarray(p, jnp.int32) for m in moves for p in (m[5], m[6])])

    def kernel(places_ref, *refs):
        sources, target, sems = refs[:count], refs[count], refs[count + 1]
        copies = []
        for n, (index, row, rows, col, cols, _, _) in enumerate(moves):
            to_row = pl.multiple_of(places_ref[2 * n], rows)
            to_col = pl.multiple_of(places_ref[2 * n + 1], cols)
            copies.append(
                pltpu.make_async_copy(
                    sources[index].at[pl.ds(row, rows), pl.ds(col, cols)],
                    target.at[pl.ds(to_row, rows), pl.ds(to_col, cols)],
                    sems.at[n],
                )
            )
        for copy in copies:
            copy.start()
        for copy in copies:
            copy.wait()

    return pl.pallas_call(
        kernel,
        grid_spec=pltpu.PrefetchScalarGridSpec(
            num_scalar_prefetch=1,
            grid=(1,),
            in_specs=[pl.BlockSpec(memory_space=pl.ANY)] * count,
            out_specs=pl.BlockSpec(memory_space=pltpu.VMEM),
            scratch_shapes=[pltpu.SemaphoreType.DMA((len(moves),))],
        ),
        out_shape=jax.ShapeDtypeStruct(shape, dtype),
        compiler_params=pltpu.CompilerParams(vmem_limit_bytes=vmem_limit),
        cost_estimate=pl.CostEstimate(
            flops=0,
            bytes_accessed=2 * sum(a.size * a.dtype.itemsize for a in arrays),
            transcendentals=0,
        ),
    )(places, *arrays)


def gelu_both(values):
    inner = gelu_coef * (values + gelu_cube * values * values * values)
    tangent = jnp.tanh(inner)
    output = 0.5 * values * (1.0 + tangent)
    slope = 0.5 * (1.0 + tangent) + 0.5 * values * (1.0 - tangent * tangent) * gelu_coef * (
        1.0 + 3.0 * gelu_cube * values * values
    )
    return (output, slope)


def layer_norm(values, gain_row, shift_row):
    center = values - jnp.mean(values, axis=-1, keepdims=True)
    inverse = lax.rsqrt(jnp.mean(center * center, axis=-1, keepdims=True) + layer_eps)
    normed = center * inverse
    return (normed * gain_row + shift_row, normed, inverse)


def norm_back(grad_rows, normed, inverse, gain_row):
    scaled = grad_rows * gain_row
    inner_term = scaled - jnp.mean(scaled, axis=-1, keepdims=True)
    inner_term = inner_term - normed * jnp.mean(scaled * normed, axis=-1, keepdims=True)
    return (
        inverse * inner_term,
        jnp.sum(grad_rows * normed, axis=0),
        jnp.sum(grad_rows, axis=0),
    )


def column_sum(array):
    return jnp.sum(array.astype(f32), axis=0)


def after(value, *earlier):
    return lax.optimization_barrier((value, *earlier))[0]


def general_layer(mesh):
    S, F = mesh.shape["seq"], mesh.shape["fsdp"]
    Y = S // CORES
    Z = 4 if F % 4 == 0 else 1
    X = F // Z

    core_perm = [(n, n ^ 1) for n in range(S)]

    def y_perm(k):
        return [(y * CORES + c, (y + k) % Y * CORES + c) for y in range(Y) for c in range(CORES)]

    def z_perm(k):
        return [(z * X + x, (z + k) % Z * X + x) for z in range(Z) for x in range(X)]

    def x_perm(k):
        return [(z * X + x, z * X + (x + k) % X) for z in range(Z) for x in range(X)]

    def core_swap(array):
        return lax.ppermute(array, "seq", core_perm)

    def y_shift(array, k):
        return lax.ppermute(array, "seq", y_perm(k % Y)) if k % Y else array

    def z_shift(array, k):
        return lax.ppermute(array, "fsdp", z_perm(k % Z)) if k % Z else array

    def x_shift(array, k):
        return lax.ppermute(array, "fsdp", x_perm(k % X)) if k % X else array

    def local(
        hidden_in,
        memory,
        lengths,
        out_grad,
        self_in_weight,
        self_query_bias,
        self_value_bias,
        self_out_weight,
        self_out_bias,
        cross_query_weight,
        cross_query_bias,
        memory_weight,
        memory_value_bias,
        cross_out_weight,
        cross_out_bias,
        ffn_in_weight,
        ffn_in_bias,
        ffn_out_weight,
        ffn_out_bias,
        norm_gain,
        norm_bias,
    ):
        s = lax.axis_index("seq")
        y, c = s // CORES, s % CORES
        f = lax.axis_index("fsdp")
        z, x = f // X, f % X
        _, t, D = hidden_in.shape
        T = S * t
        hw = D // S
        FF = ffn_in_weight.shape[1]
        shard = D // F
        part = shard // S
        fw = FF // (F * S)
        hidden_in, memory, out_grad = hidden_in[0], memory[0], out_grad[0]

        relative = [(k, e) for e in range(CORES) for k in range(Y)]

        def seq_of(k, e):
            return lax.rem(y - k + Y, Y) * CORES + (c if e == 0 else 1 - c)

        def seq_gather(array):
            own = [y_shift(array, k) for k in range(Y)]
            return own + [core_swap(a) for a in own]

        def seq_scatter(parts):
            chip = []
            for k in reversed(range(Y)):
                other = core_swap(parts[(k, 1)].astype(bf16))
                chip.append((k, parts[(k, 0)].astype(f32) + other.astype(f32)))
            total = None
            for k, value in chip:
                value = y_shift(value.astype(bf16), -k).astype(f32) if k else value
                total = value if total is None else total + value
            return total

        def fsdp_gather(chunk):
            pieces = []
            for kz in range(Z):
                column = z_shift(chunk, kz)
                for kx in range(X):
                    pieces.append(x_shift(column, kx))
            return pieces

        def fsdp_place(pieces):
            rows, cols = pieces[0].shape
            moves = []
            for n in range(F):
                kz, kx = n // X, n % X
                where = lax.rem(z - kz + Z, Z) * X + lax.rem(x - kx + X, X)
                moves.append((n, 0, rows, 0, cols, where * rows, 0))
            return assemble(pieces, moves, (F * rows, cols))

        def fsdp_scatter(grads):
            rows, cols = grads.shape[0] // F, grads.shape[1]
            view = grads.reshape(Z, X, rows, cols)
            total = lax.dynamic_index_in_dim(view, x, 1, keepdims=False).astype(f32)
            for kx in range(1, X):
                sent = lax.dynamic_index_in_dim(view, lax.rem(x + kx, X), 1, keepdims=False)
                total = total + x_shift(sent.astype(bf16), kx).astype(f32)
            low = total.astype(bf16)
            own = lax.dynamic_index_in_dim(low, z, 0, keepdims=False).astype(f32)
            for kz in range(1, Z):
                sent = lax.dynamic_index_in_dim(low, lax.rem(z + kz, Z), 0, keepdims=False)
                own = own + z_shift(sent, kz).astype(f32)
            return own.astype(bf16)

        def finish(own):
            rows, cols = own.shape
            pieces = seq_gather(own)
            moves = [
                (n, 0, rows, 0, cols, seq_of(k, e) * rows, 0)
                for n, (k, e) in enumerate(relative)
            ]
            return assemble(pieces, moves, (S * rows, cols)).reshape(S, rows, cols).astype(f32)

        def pick(array, start, size):
            return lax.dynamic_slice_in_dim(array, start, size, 1)

        small_list = [
            self_query_bias, self_value_bias, self_out_bias, cross_query_bias, memory_value_bias,
            cross_out_bias, ffn_out_bias, norm_gain.reshape(-1), norm_bias.reshape(-1), ffn_in_bias,
        ]
        small = jnp.concatenate(small_list)
        small = lax.all_to_all(
            jnp.broadcast_to(small[None], (F, small.shape[0])), "fsdp", 0, 0, tiled=True
        ).astype(f32)
        smalls = []
        at = 0
        for _ in range(7):
            smalls.append(small[:, at : at + shard].reshape(D))
            at += shard
        b_query, b_value, b_attn_out, b_cross_q, b_mem_value, b_cross_out, b_ffn_out = smalls
        gains = small[:, at : at + 3 * shard].reshape(F, 3, shard).swapaxes(0, 1).reshape(3, D)
        at += 3 * shard
        shifts = small[:, at : at + 3 * shard].reshape(F, 3, shard).swapaxes(0, 1).reshape(3, D)
        at += 3 * shard
        b_ffn_in = lax.dynamic_index_in_dim(
            small[:, at:].reshape(F, S, fw), s, 1, keepdims=False
        ).reshape(F * fw)

        def group_row(row):
            return lax.dynamic_slice_in_dim(row, s * hw, hw, 0)

        chunk_qkv = jnp.concatenate(
            [pick(self_in_weight, m * D + s * hw, hw) for m in range(3)], axis=1
        )
        chunk_mid = jnp.concatenate(
            [pick(memory_weight, m * D + s * hw, hw) for m in range(2)]
            + [pick(cross_query_weight, s * hw, hw)],
            axis=1,
        )
        chunk_out = jnp.concatenate(
            [
                lax.dynamic_slice_in_dim(w, s * part, part, 0)
                for w in (self_out_weight, cross_out_weight)
            ],
            axis=0,
        )
        chunk_fin = lax.dynamic_index_in_dim(
            ffn_in_weight.reshape(shard, F, S, fw), s, 2, keepdims=False
        ).reshape(shard, F * fw)
        chunk_fout = lax.dynamic_slice_in_dim(ffn_out_weight, s * fw, fw, 0)

        got_qkv = fsdp_gather(chunk_qkv)
        x_blocks = seq_gather(hidden_in)
        got_mid = fsdp_gather(after(chunk_mid, got_qkv[-1]))
        m_blocks = seq_gather(after(memory, x_blocks[-1]))
        got_out = fsdp_gather(after(chunk_out, got_qkv[-1]))
        got_fin = fsdp_gather(after(chunk_fin, got_mid[-1]))
        got_fout = fsdp_gather(after(chunk_fout, got_fin[-1]))

        w_qkv = fsdp_place(got_qkv)
        block_moves = [
            (n, 0, t, 0, D, seq_of(k, e) * t, 0) for n, (k, e) in enumerate(relative)
        ]
        x_all = assemble(x_blocks, block_moves, (T, D))
        qkv_bias = jnp.concatenate([group_row(b_query), jnp.zeros((hw,), f32), group_row(b_value)])
        qkv = (dot(x_all, w_qkv, nn) + qkv_bias).astype(bf16)
        q_self, k_self, v_self = (qkv[:, m * hw : (m + 1) * hw] for m in range(3))
        self_attn, self_lse = attend_forward(q_self, k_self, v_self, lengths, True)

        w_mid = fsdp_place(got_mid)
        w_mem, cq_quarter = w_mid[:, : 2 * hw], w_mid[:, 2 * hw :]
        m_all = jnp.concatenate(m_blocks, axis=0)
        mem_bias = jnp.concatenate([jnp.zeros((hw,), f32), group_row(b_mem_value)])
        kv_mem = (dot(m_all, w_mem, nn) + mem_bias).astype(bf16)

        def all_rows(parts_of):
            return assemble(
                parts_of,
                [(n, 0, t, 0, hw, 0, seq_of(k, e) * hw) for n, (k, e) in enumerate(relative)],
                (t, D),
            )

        def heads_to_rows(array):
            blocks = array.reshape(S, t, hw)
            mine = []
            for k, e in relative:
                target = lax.rem(y + k, Y) * CORES + (c if e == 0 else 1 - c)
                sent = lax.dynamic_index_in_dim(blocks, target, 0, keepdims=False)
                sent = y_shift(sent, k)
                mine.append(core_swap(sent) if e else sent)
            return all_rows(mine)

        def rows_to_heads(array):
            mine = []
            for k, e in relative:
                target = lax.rem(y + k, Y) * CORES + (c if e == 0 else 1 - c)
                sent = y_shift(pick(array, target * hw, hw), k)
                mine.append(core_swap(sent) if e else sent)
            return assemble(
                mine,
                [(n, 0, t, 0, hw, seq_of(k, e) * t, 0) for n, (k, e) in enumerate(relative)],
                (T, hw),
            )

        attn_tok = heads_to_rows(self_attn)
        mem_chips = [y_shift(kv_mem, k) for k in range(Y)]
        mem_key = jnp.concatenate([m[:, :hw] for m in mem_chips], axis=1)
        mem_value = jnp.concatenate([m[:, hw:] for m in mem_chips], axis=1)

        out_quarter = fsdp_place(got_out)
        out_pieces = seq_gather(out_quarter)
        own_moves = [[], []]
        for n, (k, e) in enumerate(relative):
            for which in range(2):
                for shard_index in range(F):
                    own_moves[which].append(
                        (
                            n, shard_index * 2 * part + which * part, part, 0, D,
                            shard_index * shard + seq_of(k, e) * part, 0,
                        )
                    )
        w_attn_out = assemble(out_pieces, own_moves[0], (D, D))
        w_cross_out = assemble(out_pieces, own_moves[1], (D, D))
        cq_pieces = seq_gather(cq_quarter)
        w_cross_q = jnp.concatenate(cq_pieces, axis=1)
        b_cq = jnp.concatenate(
            [lax.dynamic_slice_in_dim(b_cross_q, seq_of(k, e) * hw, hw, 0) for k, e in relative]
        )
        half = Y * hw

        x_float = hidden_in.astype(f32)
        branch = dot(attn_tok, w_attn_out, nn) + b_attn_out
        first, normed_one, inverse_one = layer_norm(
            alpha_scale * x_float + branch, gains[0], shifts[0]
        )
        first_low = first.astype(bf16)
        cq_rows = (dot(first_low, w_cross_q, nn) + b_cq).astype(bf16)

        cross_q = jnp.concatenate([cq_rows[:, :half], core_swap(cq_rows[:, half:])], axis=0)
        cross_attn, cross_lse = attend_forward(cross_q, mem_key, mem_value, lengths, False)
        cross_other = core_swap(cross_attn[t:])
        cross_tok = assemble(
            [cross_attn, cross_other],
            [(e, 0, t, k * hw, hw, 0, seq_of(k, e) * hw) for k, e in relative],
            (t, D),
        )
        cross_branch = dot(cross_tok, w_cross_out, nn) + b_cross_out
        second, normed_two, inverse_two = layer_norm(
            alpha_scale * first + cross_branch, gains[1], shifts[1]
        )
        second_low = second.astype(bf16)

        w_fin = fsdp_place(got_fin)
        w_fout = fsdp_place(got_fout)
        second_all = jnp.concatenate(seq_gather(second_low), axis=0)
        pre_act = dot(second_all, w_fin, nn) + b_ffn_in
        act_value, act_slope = gelu_both(pre_act)
        hidden_low = act_value.astype(bf16)
        ffn_part = dot(hidden_low, w_fout, nn)

        def by_owner(array):
            return {ke: array[n * t : (n + 1) * t] for n, ke in enumerate(relative)}

        ffn_branch = seq_scatter(by_owner(ffn_part)) + b_ffn_out
        result, normed_three, inverse_three = layer_norm(
            alpha_scale * second + ffn_branch, gains[2], shifts[2]
        )
        layer_out = result.astype(bf16)

        d_three, gain_three, shift_three = norm_back(
            out_grad.astype(f32), normed_three, inverse_three, gains[2]
        )
        d_ffn = d_three.astype(bf16)
        d_ffn_all = jnp.concatenate(seq_gather(d_ffn), axis=0)
        d_hidden = dot(d_ffn_all, w_fout, nt)
        d_pre = (act_slope * d_hidden).astype(bf16)
        d_second_part = dot(d_pre, w_fin, nt)
        d_second = alpha_scale * d_three + seq_scatter(by_owner(d_second_part))
        grad_fout = dot(hidden_low, d_ffn_all, tn).astype(bf16)
        own_fout = fsdp_scatter(grad_fout)
        grad_fin = dot(second_all, d_pre, tn).astype(bf16)
        own_fin = fsdp_scatter(grad_fin)

        d_two, gain_two, shift_two = norm_back(d_second, normed_two, inverse_two, gains[1])
        d_cross = d_two.astype(bf16)
        d_cross_tok = dot(d_cross, w_cross_out, nt).astype(bf16)
        keep, send = (
            jnp.concatenate([pick(d_cross_tok, seq_of(k, e) * hw, hw) for k in range(Y)], axis=1)
            for e in range(CORES)
        )
        d_cross_heads = jnp.concatenate([keep, core_swap(send)], axis=0)
        dq_cross, dk_mem, dv_mem = attend_back(
            cross_q, mem_key, mem_value, d_cross_heads, cross_lse, lengths, False
        )
        d_cq_rows = jnp.concatenate([dq_cross[:t], core_swap(dq_cross[t:])], axis=1)
        d_first = alpha_scale * d_two + dot(d_cq_rows, w_cross_q, nt)
        grad_cross_out = dot(cross_tok, d_cross, tn)
        grad_cq = dot(first_low, d_cq_rows, tn)
        d_mem = None
        for k in range(Y):
            sent = jnp.concatenate([d[:, k * hw : (k + 1) * hw] for d in (dk_mem, dv_mem)], axis=1)
            got = y_shift(sent, -k).astype(f32)
            d_mem = got if d_mem is None else d_mem + got
        d_mem = d_mem.astype(bf16)
        grad_mem = dot(m_all, d_mem, tn).astype(bf16)
        memory_grad = seq_scatter(by_owner(dot(d_mem, w_mem, nt))).astype(bf16)

        d_one, gain_one, shift_one = norm_back(d_first, normed_one, inverse_one, gains[0])
        d_branch = d_one.astype(bf16)
        d_attn_heads = rows_to_heads(dot(d_branch, w_attn_out, nt).astype(bf16))
        grad_self_out = dot(attn_tok, d_branch, tn)
        dq_self, dk_self, dv_self = attend_back(
            q_self, k_self, v_self, d_attn_heads, self_lse, lengths, True
        )
        d_qkv = jnp.concatenate([dq_self, dk_self, dv_self], axis=1)
        grad_qkv = dot(x_all, d_qkv, tn).astype(bf16)
        own_qkv = fsdp_scatter(grad_qkv)
        input_part = dot(d_qkv, w_qkv, nt).reshape(S, t, D)
        input_sum = seq_scatter(
            {
                (k, e): lax.dynamic_index_in_dim(input_part, seq_of(k, e), 0, keepdims=False)
                for k, e in relative
            }
        )
        input_grad = (alpha_scale * d_one + input_sum).astype(bf16)

        def out_parts(grad):
            view = grad.astype(bf16).reshape(F, S, part, D)
            return {
                (k, e): lax.dynamic_index_in_dim(view, seq_of(k, e), 1, keepdims=False)
                for k, e in relative
            }

        own_cross_out = seq_scatter(out_parts(grad_cross_out)).astype(bf16)
        own_self_out = seq_scatter(out_parts(grad_self_out)).astype(bf16)
        own_cq = seq_scatter(
            {ke: grad_cq[:, n * hw : (n + 1) * hw] for n, ke in enumerate(relative)}
        ).astype(bf16)
        own_mid = fsdp_scatter(jnp.concatenate([grad_mem, own_cq], axis=1))
        own_out = fsdp_scatter(
            jnp.concatenate([own_self_out, own_cross_out], axis=1).reshape(F * 2 * part, D)
        )

        all_fout = finish(own_fout).reshape(S * fw, D)
        all_fin = (
            finish(own_fin).reshape(S, shard, F, fw).transpose(1, 2, 0, 3).reshape(shard, FF)
        )
        all_mid = finish(own_mid)
        all_mem = (
            all_mid[:, :, : 2 * hw]
            .reshape(S, shard, 2, hw)
            .transpose(1, 2, 0, 3)
            .reshape(shard, 2 * D)
        )
        all_cq = all_mid[:, :, 2 * hw :].transpose(1, 0, 2).reshape(shard, D)
        all_out = finish(own_out).reshape(S, 2, part, D)
        all_self_out = all_out[:, 0].reshape(shard, D)
        all_cross_out = all_out[:, 1].reshape(shard, D)
        all_qkv = (
            finish(own_qkv).reshape(S, shard, 3, hw).transpose(1, 2, 0, 3).reshape(shard, 3 * D)
        )

        def spread(row):
            return lax.dynamic_update_slice_in_dim(jnp.zeros((D,), f32), row, s * hw, 0)

        d_cq_sum = column_sum(d_cq_rows)
        cq_bias = jnp.zeros((D,), f32)
        for n, (k, e) in enumerate(relative):
            cq_bias = lax.dynamic_update_slice_in_dim(
                cq_bias, d_cq_sum[n * hw : (n + 1) * hw], seq_of(k, e) * hw, 0
            )
        fin_bias = lax.dynamic_update_slice_in_dim(
            jnp.zeros((F, S, fw), f32), column_sum(d_pre).reshape(F, 1, fw), s, 1
        ).reshape(F, S * fw)
        small_grads = jnp.concatenate(
            [
                row.reshape(F, shard)
                for row in (
                    spread(column_sum(dq_self)), spread(column_sum(dv_self)), column_sum(d_branch),
                    cq_bias, spread(column_sum(d_mem[:, hw:])), column_sum(d_cross),
                    column_sum(d_ffn), gain_one, gain_two, gain_three, shift_one, shift_two,
                    shift_three,
                )
            ]
            + [fin_bias],
            axis=1,
        )
        small_own = jnp.sum(lax.all_to_all(small_grads, "fsdp", 0, 0, tiled=True), axis=0)
        small_own = lax.psum(small_own, "seq")
        rows = [small_own[n * shard : (n + 1) * shard] for n in range(13)]
        return (
            layer_out[None],
            input_grad[None],
            memory_grad[None],
            all_qkv,
            rows[0],
            rows[1],
            all_self_out,
            rows[2],
            all_cq,
            rows[3],
            all_mem,
            rows[4],
            all_cross_out,
            rows[5],
            all_fin,
            small_own[13 * shard :],
            all_fout,
            rows[6],
            jnp.stack(rows[7:10]),
            jnp.stack(rows[10:13]),
        )

    return local


short = pl.CostEstimate(flops=1024, bytes_accessed=1024, transcendentals=0)

small_rows = 24


def hbm(array):
    return ("hbm", array)


def stage(body, where, ins, outs, scratch=(), time=0):
    specs, arrays = [], []
    for item in ins:
        if isinstance(item, tuple):
            specs.append(pl.BlockSpec(memory_space=pl.ANY))
            arrays.append(item[1])
        else:
            specs.append(pl.BlockSpec(memory_space=pltpu.VMEM))
            arrays.append(item)
    n_in, n_out = len(arrays), len(outs)

    def kernel(w, *refs):
        body(w, refs[:n_in], refs[n_in : n_in + n_out], refs[n_in + n_out :])

    return pl.pallas_call(
        kernel,
        grid_spec=pltpu.PrefetchScalarGridSpec(
            num_scalar_prefetch=1,
            grid=(1,),
            in_specs=specs,
            out_specs=[pl.BlockSpec(memory_space=pltpu.VMEM)] * n_out,
            scratch_shapes=list(scratch),
        ),
        out_shape=[jax.ShapeDtypeStruct(shape, dtype) for shape, dtype in outs],
        compiler_params=pltpu.CompilerParams(vmem_limit_bytes=vmem_limit),
        cost_estimate=pl.CostEstimate(
            flops=1024, bytes_accessed=1024 + int(3.5e6 * time), transcendentals=0
        ),
    )(where, *arrays)


class Copies:
    def __init__(self, sems):
        self.sems, self.count, self.lots = sems, 0, [[]]

    def add(self, source, target):
        copy = pltpu.make_async_copy(source, target, self.sems.at[self.count])
        copy.start()
        self.count += 1
        self.lots[-1].append(copy)

    def split(self):
        self.lots.append([])

    def wait(self):
        for copy in self.lots.pop(0):
            copy.wait()


def span(index, size):
    return pl.ds(pl.multiple_of(index * size, size), size)


def norm_rows(values, gain_row, shift_row):
    center = values - jnp.mean(values, axis=-1, keepdims=True)
    inverse = lax.rsqrt(jnp.mean(center * center, axis=-1, keepdims=True) + layer_eps)
    normed = center * inverse
    return normed * gain_row + shift_row, normed, inverse


def norm_rows_back(grad_rows, normed, inverse, gain_row):
    scaled = grad_rows * gain_row
    inner = scaled - jnp.mean(scaled, axis=-1, keepdims=True)
    inner = inner - normed * jnp.mean(scaled * normed, axis=-1, keepdims=True)
    return (
        inverse * inner,
        jnp.sum(grad_rows * normed, axis=0, keepdims=True),
        jnp.sum(grad_rows, axis=0, keepdims=True),
    )


def row_sum(array):
    return jnp.sum(array.astype(f32), axis=0, keepdims=True)


def tiled_layer(mesh):
    S, F = mesh.shape["seq"], mesh.shape["fsdp"]
    Z = 4 if F % 4 == 0 else 1
    X = F // Z
    SEQ, MINE, AT_X, LENGTH = 0, S, S + 1, S + 2

    core_perm = [(n, n ^ 1) for n in range(S)]
    y_perm = [(n, n ^ 2) for n in range(S)]
    diagonal_perm = [(n, n ^ 3) for n in range(S)]

    def core_swap(array):
        return lax.ppermute(array, "seq", core_perm)

    def y_swap(array):
        return lax.ppermute(array, "seq", y_perm)

    z_groups = [[z * X + x for z in range(Z)] for x in range(X)]

    def z_exchange(array):
        return lax.all_to_all(array, "fsdp", 0, 0, axis_index_groups=z_groups, tiled=True)

    def x_shift(array, k):
        perm = [(z * X + x, z * X + (x + k) % X) for z in range(Z) for x in range(X)]
        return lax.ppermute(array, "fsdp", perm) if k % X else array

    def seq_gather(array):
        far = y_swap(array)
        return [array, far, core_swap(array), core_swap(far)]

    def tied(values):
        return lax.optimization_barrier(list(values))

    def z_gather(copies):
        return z_exchange(copies)

    def x_gather(column):
        rows, cols = column.shape[0] // Z, column.shape[1]
        return [a.reshape(Z, rows, cols) for a in (column, x_shift(column, 1))]

    def exchange(parts):
        got = [y_swap(parts[1]), core_swap(parts[2]), lax.ppermute(parts[3], "seq", diagonal_perm)]
        return [parts[0], *tied(got)]

    def local(
        hidden_in,
        memory,
        lengths,
        out_grad,
        self_in_weight,
        self_query_bias,
        self_value_bias,
        self_out_weight,
        self_out_bias,
        cross_query_weight,
        cross_query_bias,
        memory_weight,
        memory_value_bias,
        cross_out_weight,
        cross_out_bias,
        ffn_in_weight,
        ffn_in_bias,
        ffn_out_weight,
        ffn_out_bias,
        norm_gain,
        norm_bias,
    ):
        s, f = lax.axis_index("seq"), lax.axis_index("fsdp")
        z, x = f // X, f % X
        _, t, D = hidden_in.shape
        T = S * t
        hw = D // S
        FF = ffn_in_weight.shape[1]
        shard = D // F
        fw = FF // (F * S)
        half = 2 * hw
        per_group = hw // shard
        part = shard // S
        deep = shard // 2
        rest_cols = D + half
        hidden_in, memory, out_grad = hidden_in[0], memory[0], out_grad[0]
        where = jnp.stack(
            [s, s ^ 2, s ^ 1, s ^ 3, s, x, lengths[0]]
        ).astype(jnp.int32)

        def prepare_rest(w, ins, outs, _):
            query, own, cross = ins
            out = outs[0]
            me = w[MINE]
            out[:, 0:hw] = query[:, span(me, hw)]
            rows = span(me, part)
            for h in range(2):
                for m, source in enumerate((own, cross)):
                    at = (2 * h + m) * part
                    out[at : at + part, hw:] = source[rows, h * (D // 2) : (h + 1) * (D // 2)]

        (chunk_rest,) = stage(
            prepare_rest,
            where,
            [cross_query_weight, self_out_weight, cross_out_weight],
            [((shard, 3 * hw), bf16)],
        )
        rest_own = lax.all_gather(chunk_rest, "fsdp", axis=0, tiled=True)

        def prepare_qkv(w, ins, outs, _):
            weight, out = ins[0], outs[0]
            me = w[MINE]
            for m in range(3):
                lanes = pl.ds(pl.multiple_of(m * D + me * hw, hw), hw)
                for k in range(Z):
                    out[k, 0:shard, m * hw : (m + 1) * hw] = weight[:, lanes]
            rows = [ins[n][...].reshape(1, shard) for n in range(1, 8)]
            rows += [ins[8][...], ins[9][...]]
            rows += [
                ins[10][n * fw : (n + 1) * fw].reshape(1, fw) for n in range(S)
            ]
            packed = jnp.concatenate([r.astype(f32) for r in rows], axis=0)
            first = packed[0:16].astype(bf16)
            rest = jnp.concatenate(
                [packed[16:], jnp.zeros((32 - packed.shape[0], shard), f32)], axis=0
            ).astype(bf16)
            below = jnp.concatenate(
                [first, rest, jnp.zeros((16, 3 * hw - 2 * shard), bf16)], axis=1
            )
            for k in range(Z):
                out[k, shard : shard + 16, :] = below

        (chunk_qkv,) = stage(
            prepare_qkv,
            where,
            [
                after(self_in_weight, chunk_rest), self_query_bias, self_value_bias, self_out_bias, cross_query_bias,
                memory_value_bias, cross_out_bias, ffn_out_bias, norm_gain, norm_bias, ffn_in_bias,
            ],
            [((Z, shard + 16, 3 * hw), bf16)],
        )

        def prepare_mem(w, ins, outs, _):
            for m in range(2):
                lanes = pl.ds(pl.multiple_of(m * D + w[MINE] * hw, hw), hw)
                for k in range(Z):
                    outs[0][k, :, m * hw : (m + 1) * hw] = ins[0][:, lanes]

        (chunk_mem,) = stage(prepare_mem, where, [memory_weight], [((Z, shard, 2 * hw), bf16)])

        def prepare_ffn(w, ins, outs, _):
            me = w[MINE]
            for n in range(F):
                lanes = pl.ds(pl.multiple_of(n * S * fw + me * fw, fw), fw)
                outs[0][0:shard, n * fw : (n + 1) * fw] = ins[0][:, lanes]
            outs[0][shard:, :] = ins[1][span(me, fw), :]

        (chunk_ffn,) = stage(
            prepare_ffn, where, [ffn_in_weight, ffn_out_weight], [((shard + fw, D), bf16)]
        )

        hidden_far = y_swap(after(hidden_in, chunk_qkv))
        z_qkv = z_gather(chunk_qkv.reshape(Z * (shard + 16), 3 * hw))
        z_qkv, hidden_far, chunk_mem, chunk_ffn = tied([z_qkv, hidden_far, chunk_mem, chunk_ffn])
        x_blocks = [hidden_in, hidden_far, core_swap(hidden_in), core_swap(hidden_far)]
        got_qkv = x_gather(z_qkv)
        memory_far = y_swap(after(memory, hidden_far))
        z_mem = z_gather(after(chunk_mem, z_qkv).reshape(Z * shard, 2 * hw))
        got_qkv[0], z_mem, memory_far = tied([got_qkv[0], z_mem, memory_far])
        m_blocks = [memory, memory_far, core_swap(memory), core_swap(memory_far)]
        got_mem = x_gather(z_mem)

        def project_qkv(w, ins, outs, scratch):
            blocks, pieces = ins[:S], ins[S:]
            qkv, small = outs
            x_all, weight, packed, sems = scratch
            copies = Copies(sems)
            for k in range(2):
                at = w[AT_X] if k == 0 else 1 - w[AT_X]
                copies.add(pieces[k].at[:, pl.ds(0, shard)], weight.at[:, at])
                copies.add(pieces[k].at[:, pl.ds(shard, 16), pl.ds(0, 2 * shard)], packed.at[:, at])
            for n in range(S):
                copies.add(blocks[n], x_all.at[span(w[SEQ + n], t)])
            copies.wait()
            small[...] = jnp.zeros_like(small)
            for n in range(F):
                lanes = slice(n * shard, (n + 1) * shard)
                small[0:16, lanes] = packed[n // X, n % X, :, 0:shard].astype(f32)
                small[16:24, lanes] = packed[n // X, n % X, 0:8, shard : 2 * shard].astype(f32)
            mine = span(w[MINE], hw)
            biases = [small[0:1, mine], jnp.zeros((1, hw), f32), small[1:2, mine]]
            for n in range(S):
                rows = slice(n * t, (n + 1) * t)
                for m in range(3):
                    cols = slice(m * hw, (m + 1) * hw)
                    value = dot(x_all[rows, :], weight[..., cols].reshape(D, hw), nn) + biases[m]
                    qkv[rows, cols] = value.astype(bf16)

        qkv, small = stage(
            project_qkv,
            where,
            [hbm(b) for b in x_blocks] + [hbm(p) for p in got_qkv],
            [((T, 3 * hw), bf16), ((small_rows, D), f32)],
            [
                pltpu.VMEM((T, D), bf16),
                pltpu.VMEM((Z, X, shard, 3 * hw), bf16),
                pltpu.VMEM((Z, X, 16, 2 * shard), bf16),
                pltpu.SemaphoreType.DMA((4 + S,)),
            ],
        )

        pairs = hw // (2 * HD)
        pair = 2 * HD

        def qkv_spec(m):
            return pl.BlockSpec((T, pair), lambda g, i, _: (0, m * pairs + g))

        rows_2 = 2 * t

        def masked(w, i, scores):
            key_pos = lax.broadcasted_iota(jnp.int32, scores.shape, 0)
            query_pos = i * rows_2 + lax.broadcasted_iota(jnp.int32, (1, rows_2), 1)
            limit = jnp.minimum(w[LENGTH], (query_pos // BLK + 1) * BLK)
            return jnp.where(key_pos < limit, scores, masked_value)

        def forward_pair(queries, k_ref, v_ref, key_count, mask, lse_ref):
            parts, lses = [], []
            for h in range(2):
                cols = slice(h * HD, (h + 1) * HD)
                query = queries[:, cols] * jnp.asarray(score_scale, bf16)
                scores = mask(dot(k_ref[:key_count, cols], query, nt))
                top = jnp.max(scores, axis=0, keepdims=True)
                weights = jnp.exp(scores - top)
                totals = jnp.sum(weights, axis=0, keepdims=True)
                value = dot(v_ref[:key_count, cols], weights.astype(bf16), tn)
                parts.append(value * (1.0 / totals))
                lses.append(top + jnp.log(totals))
            lse_ref[0] = jnp.concatenate(lses, axis=0)
            return jnp.concatenate(parts, axis=0).T.astype(bf16)

        def step_cases(i, visit):
            for n in range(T // rows_2):

                @pl.when(i == n)
                def _(n=n):
                    visit((n + 1) * rows_2)

        def self_forward(w, q_ref, k_ref, v_ref, *outs):
            i = pl.program_id(1)

            def visit(key_count):
                mask = functools.partial(masked, w, i)
                out = forward_pair(q_ref[...], k_ref, v_ref, key_count, mask, outs[S])
                for n in range(S):
                    for b in range(2):

                        @pl.when(w[SEQ + n] == 2 * i + b)
                        def _(n=n, b=b):
                            outs[n][...] = out[b * t : (b + 1) * t]

            step_cases(i, visit)

        q_block = pl.BlockSpec((rows_2, pair), lambda g, i, _: (i, g))
        row_block = pl.BlockSpec((t, pair), lambda g, i, _: (0, g))
        lse_block = pl.BlockSpec((1, 2, rows_2), lambda g, i, _: (g, 0, i))
        *attn_sent, self_lse = pl.pallas_call(
            self_forward,
            grid_spec=pltpu.PrefetchScalarGridSpec(
                num_scalar_prefetch=1,
                grid=(pairs, T // rows_2),
                in_specs=[q_block, qkv_spec(1), qkv_spec(2)],
                out_specs=[row_block] * S + [lse_block],
            ),
            out_shape=[jax.ShapeDtypeStruct((t, hw), bf16)] * S
            + [jax.ShapeDtypeStruct((pairs, 2, T), f32)],
            compiler_params=pltpu.CompilerParams(vmem_limit_bytes=vmem_limit),
            cost_estimate=short,
        )(where, after(qkv, m_blocks[2], m_blocks[3]), qkv, qkv)
        attn = exchange(attn_sent)
        rest_own = after(rest_own, qkv)
        rest_far = y_swap(rest_own)

        w_ffn = lax.all_gather(after(chunk_ffn, qkv), "fsdp", axis=0, tiled=True).reshape(
            F, shard + fw, D
        )
        def project_memory(w, ins, outs, scratch):
            blocks, pieces, small_ref = ins[:S], ins[S : S + 2], ins[S + 2]
            kv, weight = outs
            m_all, sems = scratch
            copies = Copies(sems)
            for k in range(2):
                copies.add(pieces[k], weight.at[:, w[AT_X] if k == 0 else 1 - w[AT_X]])
            for n in range(S):
                copies.add(blocks[n], m_all.at[pl.ds(n * t, t)])
            copies.wait()
            bias = jnp.concatenate(
                [jnp.zeros((1, hw), f32), small_ref[4:5, span(w[MINE], hw)]], axis=1
            )
            for n in range(S):
                rows = slice(n * t, (n + 1) * t)
                value = dot(m_all[rows, :], weight[...].reshape(D, 2 * hw), nn) + bias
                kv[rows, :] = value.astype(bf16)

        kv_own, w_mem = stage(
            project_memory,
            where,
            [hbm(b) for b in m_blocks] + [hbm(p) for p in got_mem] + [after(small, attn_sent[1])],
            [((T, 2 * hw), bf16), ((Z, X, shard, 2 * hw), bf16)],
            [pltpu.VMEM((T, D), bf16), pltpu.SemaphoreType.DMA((2 + S,))],
        )
        w_mem = w_mem.reshape(D, 2 * hw)
        kv_far = y_swap(after(kv_own, attn[1]))
        rest_core = [core_swap(after(r, kv_own)) for r in (rest_own, rest_far)]
        rest = [r.reshape(F, shard, 3 * hw) for r in (rest_own, rest_far, *rest_core)]

        def load_out(copies, w, rest_refs, which, target):
            for n in range(S):
                for h in range(2):
                    at = (2 * h + which) * part
                    copies.add(
                        rest_refs[n].at[:, pl.ds(at, part), pl.ds(hw, D // 2)],
                        target.at[:, w[SEQ + n], :, pl.ds(h * (D // 2), D // 2)],
                    )

        def group_rows(weight, group):
            return weight[pl.ds(group * per_group, per_group)].reshape(hw, D)

        out_scratch = pltpu.VMEM((F, S, part, D), bf16)
        half_scratch = pltpu.VMEM((F, 2, deep, D), bf16)
        cq_scratch = pltpu.VMEM((S, F, shard, hw), bf16)

        def first_stage(w, ins, outs, scratch):
            pieces, rest_refs, x_ref, small_ref = ins[:S], ins[S : 2 * S], ins[2 * S], ins[2 * S + 1]
            normed_ref, inverse_ref, low_ref, keep_ref, send_ref = outs
            weight, cq, sems = scratch
            copies = Copies(sems)
            load_out(copies, w, rest_refs, 0, weight)
            copies.split()
            for n in range(S):
                copies.add(rest_refs[n].at[:, :, pl.ds(0, hw)], cq.at[n])
            copies.wait()
            total = alpha_scale * x_ref[...].astype(f32) + small_ref[2:3, :]
            for n in range(S):
                total = total + dot(pieces[n][...], group_rows(weight, w[SEQ + n]), nn)
            value, normed, inverse = norm_rows(total, small_ref[7:8, :], small_ref[10:11, :])
            normed_ref[...] = normed
            inverse_ref[...] = inverse
            low = value.astype(bf16)
            low_ref[...] = low
            copies.wait()
            for n in (2, 3, 0, 1):
                bias = small_ref[3:4, span(w[SEQ + n], hw)]
                query = (dot(low, cq[n].reshape(D, hw), nn) + bias).astype(bf16)
                target = keep_ref if n < 2 else send_ref
                target[:, (n % 2) * hw : (n % 2 + 1) * hw] = query

        normed_one, inverse_one, first_low, cq_keep, cq_send = stage(
            first_stage,
            where,
            attn + [hbm(r) for r in rest] + [hidden_in, small],
            [
                ((t, D), f32), ((t, 1), f32), ((t, D), bf16), ((t, half), bf16), ((t, half), bf16),
            ],
            [out_scratch, cq_scratch, pltpu.SemaphoreType.DMA((3 * S,))],
        )
        cq_other = core_swap(cq_send)

        def kv_specs():
            near = [
                pl.BlockSpec((T, pair), lambda g, i, _, m=m: (0, m * pairs + jnp.minimum(g, pairs - 1)))
                for m in range(2)
            ]
            far = [
                pl.BlockSpec((T, pair), lambda g, i, _, m=m: (0, m * pairs + jnp.maximum(g - pairs, 0)))
                for m in range(2)
            ]
            return near + far

        def cross_forward(w, qa_ref, qb_ref, k0, v0, k1, v1, oa_ref, ob_ref, lse_ref):
            g = pl.program_id(0)
            for gi, (k_ref, v_ref) in enumerate(((k0, v0), (k1, v1))):

                @pl.when(g // pairs == gi)
                def _(k_ref=k_ref, v_ref=v_ref):
                    queries = jnp.concatenate([qa_ref[...], qb_ref[...]], axis=0)
                    out = forward_pair(queries, k_ref, v_ref, T, lambda scores: scores, lse_ref)
                    oa_ref[...] = out[:t]
                    ob_ref[...] = out[t:]

        cross_keep, cross_send, cross_lse = pl.pallas_call(
            cross_forward,
            grid_spec=pltpu.PrefetchScalarGridSpec(
                num_scalar_prefetch=1,
                grid=(2 * pairs, 1),
                in_specs=[row_block, row_block] + kv_specs(),
                out_specs=[row_block, row_block, lse_block],
            ),
            out_shape=[jax.ShapeDtypeStruct((t, half), bf16)] * 2
            + [jax.ShapeDtypeStruct((2 * pairs, 2, 2 * t), f32)],
            compiler_params=pltpu.CompilerParams(vmem_limit_bytes=vmem_limit),
            cost_estimate=short,
        )(where, cq_keep, cq_other, kv_own, kv_own, kv_far, kv_far)
        cross_other = core_swap(cross_send)

        def halves(keep_ref, other_ref):
            return [
                ref[:, h * hw : (h + 1) * hw] for ref in (keep_ref, other_ref) for h in range(2)
            ]

        def second_stage(w, ins, outs, scratch):
            keep_ref, other_ref, normed_one_ref, small_ref = ins[:4]
            rest_refs = ins[4:]
            normed_ref, inverse_ref, low_ref = outs
            weight, sems = scratch
            copies = Copies(sems)
            load_out(copies, w, rest_refs, 1, weight)
            copies.wait()
            first = normed_one_ref[...] * small_ref[7:8, :] + small_ref[10:11, :]
            total = alpha_scale * first + small_ref[5:6, :]
            for n, piece in enumerate(halves(keep_ref, other_ref)):
                total = total + dot(piece, group_rows(weight, w[SEQ + n]), nn)
            value, normed, inverse = norm_rows(total, small_ref[8:9, :], small_ref[11:12, :])
            normed_ref[...] = normed
            inverse_ref[...] = inverse
            low_ref[...] = value.astype(bf16)

        normed_two, inverse_two, second_low = stage(
            second_stage,
            where,
            [cross_keep, cross_other, normed_one, small] + [hbm(r) for r in rest],
            [((t, D), f32), ((t, 1), f32), ((t, D), bf16)],
            [out_scratch, pltpu.SemaphoreType.DMA((2 * S,))],
        )
        second_far = y_swap(second_low)
        second = [second_low, second_far, core_swap(second_low), None]

        ffn_scratch = [
            pltpu.VMEM((F, shard, D), bf16),
            pltpu.VMEM((F, fw, D), bf16),
            pltpu.SemaphoreType.DMA((2,)),
        ]

        def load_ffn(w_ref, scratch, backward):
            copies = Copies(scratch[2])
            order = (1, 0) if backward else (0, 1)
            for m in order:
                at, rows = (0, shard) if m == 0 else (shard, fw)
                copies.add(w_ref.at[:, pl.ds(at, rows)], scratch[m])
                copies.split()
            copies.wait()
            return scratch[0], scratch[1], copies

        def ffn_forward(w, ins, outs, scratch):
            block_refs, small_ref, w_ref = ins[:2], ins[2], ins[3]
            part_refs, hidden_ref, slope_ref = outs[:2], outs[2], outs[3]
            w_in, w_out, copies = load_ffn(w_ref, scratch, False)
            bias = small_ref[pl.ds(13 + w[MINE], 1), :]
            for n in range(2):
                rows = slice(n * t, (n + 1) * t)
                pre = dot(block_refs[n][...], w_in[...].reshape(D, F * fw), nn) + bias
                value, slope = gelu_both(pre)
                low = value.astype(bf16)
                hidden_ref[rows, :] = low
                slope_ref[rows, :] = slope.astype(bf16)
                if n == 0:
                    copies.wait()
                out = dot(low, w_out[...].reshape(F * fw, D), nn)
                part_refs[n][...] = out.astype(part_refs[n].dtype)

        def ffn_call(blocks):
            return stage(
                ffn_forward,
                where,
                blocks + [small, hbm(w_ffn)],
                [((t, D), bf16), ((t, D), bf16), ((2 * t, F * fw), bf16), ((2 * t, F * fw), bf16)],
                ffn_scratch,
            )

        ffn_part_0, ffn_part_2, hidden_a, slope_a = ffn_call([second[0], second[2]])
        ffn_near = core_swap(ffn_part_2)
        second[1] = after(second_far, ffn_part_0)
        second[3] = core_swap(second[1])
        ffn_part_1, ffn_part_3, hidden_b, slope_b = ffn_call([second[1], second[3]])

        def add_pair(left, right):
            return (left.astype(f32) + right.astype(f32)).astype(bf16)

        ffn_far = y_swap(add_pair(ffn_part_1, core_swap(ffn_part_3)))

        def third_stage(w, ins, outs, _):
            a, b, far, normed_two_ref, small_ref, grad_ref = ins
            out_ref, d_ref, low_ref, sums_ref = outs
            second_rows = normed_two_ref[...] * small_ref[8:9, :] + small_ref[11:12, :]
            branch = a[...].astype(f32) + b[...].astype(f32) + far[...].astype(f32)
            total = alpha_scale * second_rows + branch + small_ref[6:7, :]
            value, normed, inverse = norm_rows(total, small_ref[9:10, :], small_ref[12:13, :])
            out_ref[...] = value.astype(bf16)
            d, gain, shift = norm_rows_back(
                grad_ref[...].astype(f32), normed, inverse, small_ref[9:10, :]
            )
            d_ref[...] = d
            low = d.astype(bf16)
            low_ref[...] = low
            sums_ref[0:1, :] = row_sum(low)
            sums_ref[1:2, :] = gain
            sums_ref[2:3, :] = shift

        layer_out, d_three, d_ffn_own, sums_three = stage(
            third_stage,
            where,
            [ffn_part_0, ffn_near, ffn_far, normed_two, small, out_grad],
            [((t, D), bf16), ((t, D), f32), ((t, D), bf16), ((8, D), f32)],
        )
        d_ffn_far = y_swap(d_ffn_own)
        d_ffn = [d_ffn_own, d_ffn_far, core_swap(d_ffn_own), None]

        def ffn_backward(w, ins, outs, scratch):
            block_refs, slope_ref, w_ref = ins[:2], ins[2], ins[3]
            part_refs, d_pre_ref = outs[:2], outs[2]
            w_in, w_out, copies = load_ffn(w_ref, scratch, True)
            for n in range(2):
                rows = slice(n * t, (n + 1) * t)
                d_hidden = dot(block_refs[n][...], w_out[...].reshape(F * fw, D), nt)
                d_pre = (slope_ref[rows, :].astype(f32) * d_hidden).astype(bf16)
                d_pre_ref[rows, :] = d_pre
                if n == 0:
                    copies.wait()
                out = dot(d_pre, w_in[...].reshape(D, F * fw), nt)
                part_refs[n][...] = out.astype(bf16)

        def ffn_back_call(blocks, slope):
            return stage(
                ffn_backward,
                where,
                blocks + [slope, hbm(w_ffn)],
                [((t, D), bf16), ((t, D), bf16), ((2 * t, F * fw), bf16)],
                ffn_scratch,
            )

        d2_part_0, d2_part_2, d_pre_a = ffn_back_call([d_ffn[0], d_ffn[2]], slope_a)
        d2_near = core_swap(d2_part_2)
        d_ffn[1] = after(d_ffn_far, d2_part_0)
        d_ffn[3] = core_swap(d_ffn[1])
        d2_part_1, d2_part_3, d_pre_b = ffn_back_call([d_ffn[1], d_ffn[3]], slope_b)
        d2_sent = add_pair(d2_part_1, core_swap(d2_part_3))
        d2_far = y_swap(d2_sent)

        def ffn_grads(w, ins, outs, scratch):
            x_refs, g_refs, hidden_a_ref, hidden_b_ref, pre_a_ref, pre_b_ref = (
                ins[0:4], ins[4:8], *ins[8:12],
            )
            grads, sums_ref = outs
            x_rows, g_rows = scratch
            for n in range(S):
                at = (0, 2, 1, 3)[n] * t
                x_rows[at : at + t, :] = x_refs[n][...]
                g_rows[at : at + t, :] = g_refs[n][...]
            for n in range(F):
                cols = slice(n * fw, (n + 1) * fw)
                rows = slice(n * shard, (n + 1) * shard)
                value = dot(x_rows[: 2 * t, rows], pre_a_ref[...], tn)
                value = value + dot(x_rows[2 * t :, rows], pre_b_ref[...], tn)
                grads[n, 0:shard, :] = value.astype(bf16)
                value = dot(hidden_a_ref[:, cols], g_rows[: 2 * t, :], tn)
                value = value + dot(hidden_b_ref[:, cols], g_rows[2 * t :, :], tn)
                grads[n, shard:, :] = value.astype(bf16)
            sums_ref[0:1, :] = row_sum(pre_a_ref[...]) + row_sum(pre_b_ref[...])

        grad_ffn, sums_ffn = stage(
            ffn_grads,
            where,
            second + d_ffn + [after(hidden_a, d2_sent), hidden_b, d_pre_a, d_pre_b],
            [((F, shard + fw, D), bf16), ((8, D), f32)],
            [pltpu.VMEM((T, D), bf16), pltpu.VMEM((T, D), bf16)],
            time=12,
        )
        def second_back(w, ins, outs, scratch):
            a, b, far, d_three_ref, normed_ref, inverse_ref, small_ref = ins[:7]
            rest_refs = ins[7:]
            d_ref, low_ref, keep_ref, send_ref, sums_ref = outs
            weight, sems = scratch
            copies = Copies(sems)
            load_out(copies, w, rest_refs, 1, weight)
            total = alpha_scale * d_three_ref[...]
            total = total + a[...].astype(f32) + b[...].astype(f32) + far[...].astype(f32)
            d, gain, shift = norm_rows_back(
                total, normed_ref[...], inverse_ref[...], small_ref[8:9, :]
            )
            d_ref[...] = d
            low = d.astype(bf16)
            low_ref[...] = low
            sums_ref[0:1, :] = row_sum(low)
            sums_ref[1:2, :] = gain
            sums_ref[2:3, :] = shift
            copies.wait()
            for n in range(S):
                target = keep_ref if n < 2 else send_ref
                value = dot(low, group_rows(weight, w[SEQ + n]), nt)
                target[:, (n % 2) * hw : (n % 2 + 1) * hw] = value.astype(bf16)

        d_two, d_cross, dc_keep, dc_send, sums_two = stage(
            second_back,
            where,
            [d2_part_0, d2_near, d2_far, after(d_three, grad_ffn), normed_two, inverse_two, small]
            + [hbm(r) for r in rest],
            [
                ((t, D), f32), ((t, D), bf16), ((t, half), bf16), ((t, half), bf16), ((8, D), f32),
            ],
            [out_scratch, pltpu.SemaphoreType.DMA((2 * S,))],
        )
        dc_other = core_swap(dc_send)
        own_ffn = lax.psum_scatter(
            after(grad_ffn, d_cross).reshape(F * (shard + fw), D),
            "fsdp",
            scatter_dimension=0,
            tiled=True,
        )

        def backward_pair(queries, k_ref, v_ref, grads, lse_ref, key_count, mask, dk_acc, dv_acc):
            dqs = []
            for h in range(2):
                cols = slice(h * HD, (h + 1) * HD)
                query = queries[:, cols] * jnp.asarray(score_scale, bf16)
                grad = grads[:, cols]
                scores = mask(dot(k_ref[:key_count, cols], query, nt))
                weights = jnp.exp(scores - lse_ref[0, h : h + 1, :])
                dv_acc[h, :key_count, :] += dot(weights.astype(bf16), grad, nn)
                grad_weights = dot(v_ref[:key_count, cols], grad, nt)
                row_term = jnp.sum(grad_weights * weights, axis=0, keepdims=True)
                low = (weights * (grad_weights - row_term)).astype(bf16)
                dk_acc[h, :key_count, :] += dot(low, query, nn)
                dqs.append(dot(k_ref[:key_count, cols], low, tn) * score_scale)
            return jnp.concatenate(dqs, axis=0).T.astype(bf16)

        def sums_out(ref, acc):
            ref[...] = jnp.concatenate([acc[h].astype(bf16) for h in range(2)], axis=1)

        def cross_backward(
            w, qa, qb, k0, v0, k1, v1, ga, gb, lse_ref, da, db, dk0, dv0, dk1, dv1, dk_acc, dv_acc
        ):
            g = pl.program_id(0)
            dk_acc[...] = jnp.zeros_like(dk_acc)
            dv_acc[...] = jnp.zeros_like(dv_acc)
            for gi, (k_ref, v_ref, dk_ref, dv_ref) in enumerate(
                ((k0, v0, dk0, dv0), (k1, v1, dk1, dv1))
            ):

                @pl.when(g // pairs == gi)
                def _(k_ref=k_ref, v_ref=v_ref, dk_ref=dk_ref, dv_ref=dv_ref):
                    queries = jnp.concatenate([qa[...], qb[...]], axis=0)
                    grads = jnp.concatenate([ga[...], gb[...]], axis=0)
                    out = backward_pair(
                        queries, k_ref, v_ref, grads, lse_ref, T, lambda scores: scores, dk_acc,
                        dv_acc,
                    )
                    da[...] = out[:t]
                    db[...] = out[t:]
                    sums_out(dk_ref, dk_acc)
                    sums_out(dv_ref, dv_acc)

        def near_block(m):
            return pl.BlockSpec((T, pair), lambda g, i, _: (0, jnp.minimum(g, pairs - 1)))

        def far_block(m):
            return pl.BlockSpec((T, pair), lambda g, i, _: (0, jnp.maximum(g - pairs, 0)))

        acc_scratch = [pltpu.VMEM((2, T, HD), f32), pltpu.VMEM((2, T, HD), f32)]
        dq_keep, dq_send, dk_own, dv_own, dk_far, dv_far = pl.pallas_call(
            cross_backward,
            grid_spec=pltpu.PrefetchScalarGridSpec(
                num_scalar_prefetch=1,
                grid=(2 * pairs, 1),
                in_specs=[row_block, row_block]
                + kv_specs()
                + [row_block, row_block, lse_block],
                out_specs=[row_block, row_block]
                + [near_block(0), near_block(1), far_block(0), far_block(1)],
                scratch_shapes=acc_scratch,
            ),
            out_shape=[jax.ShapeDtypeStruct((t, half), bf16)] * 2
            + [jax.ShapeDtypeStruct((T, hw), bf16)] * 4,
            compiler_params=pltpu.CompilerParams(vmem_limit_bytes=vmem_limit),
            cost_estimate=short,
        )(
            where, cq_keep, cq_other, kv_own, kv_own, kv_far, kv_far, dc_keep, dc_other,
            cross_lse,
        )
        dq_other = core_swap(dq_send)

        def first_back(w, ins, outs, scratch):
            keep_ref, other_ref, d_two_ref, normed_ref, inverse_ref, small_ref = ins[:6]
            rest_refs = ins[6:]
            d_ref, low_ref = outs[0], outs[1]
            sent_refs, sums_ref = outs[2 : 2 + S], outs[2 + S]
            weight, cq, sems = scratch
            copies = Copies(sems)
            for n in range(S):
                copies.add(rest_refs[n].at[:, :, pl.ds(0, hw)], cq.at[n])
            copies.split()
            load_out(copies, w, rest_refs, 0, weight)
            copies.wait()
            total = alpha_scale * d_two_ref[...]
            for n, piece in enumerate(halves(keep_ref, other_ref)):
                total = total + dot(piece, cq[n].reshape(D, hw), nt)
                sums_ref[3:4, span(w[SEQ + n], hw)] = row_sum(piece)
            d, gain, shift = norm_rows_back(
                total, normed_ref[...], inverse_ref[...], small_ref[7:8, :]
            )
            d_ref[...] = d
            low = d.astype(bf16)
            low_ref[...] = low
            sums_ref[0:1, :] = row_sum(low)
            sums_ref[1:2, :] = gain
            sums_ref[2:3, :] = shift
            copies.wait()
            for n in range(S):
                value = dot(low, group_rows(weight, w[SEQ + n]), nt)
                sent_refs[n][...] = value.astype(bf16)

        d_one, d_branch, *d_attn_sent, sums_one = stage(
            first_back,
            where,
            [dq_keep, dq_other, d_two, normed_one, inverse_one, small] + [hbm(r) for r in rest],
            [((t, D), f32), ((t, D), bf16)] + [((t, hw), bf16)] * S + [((8, D), f32)],
            [out_scratch, cq_scratch, pltpu.SemaphoreType.DMA((3 * S,))],
        )
        d_attn = exchange(d_attn_sent)

        def middle_grads(w, ins, outs, scratch):
            dq_keep_ref, dq_other_ref, low_ref, d_one_ref, co_keep, co_other, d_two_ref = ins[:7]
            attn_refs = ins[7:]
            own, cross = scratch
            core = lax.rem(w[MINE], 2)
            for e, ref in enumerate((dq_keep_ref, dq_other_ref)):
                value = dot(low_ref[...], ref[...], tn)
                outs[e][:, :, D:] = value.astype(bf16).reshape(F, shard, half)
            for n, piece in enumerate(halves(co_keep, co_other)):
                value = dot(piece, d_two_ref[...], tn).astype(bf16)
                cross[pl.ds(w[SEQ + n] * per_group, per_group)] = value.reshape(
                    per_group, 2, deep, D
                )
                value = dot(attn_refs[n][...], d_one_ref[...], tn).astype(bf16)
                own[pl.ds(w[SEQ + n] * per_group, per_group)] = value.reshape(per_group, 2, deep, D)
            for e in range(2):
                at = core if e == 0 else 1 - core
                outs[e][:, 0:deep, 0:D] = own[:, at]
                outs[e][:, deep:, 0:D] = cross[:, at]

        middle_keep, middle_send = stage(
            middle_grads,
            where,
            [dq_keep, dq_other, first_low, after(d_branch, d_attn_sent[1]), cross_keep, cross_other]
            + [d_cross, *attn],
            [((F, shard, rest_cols), bf16)] * 2,
            [half_scratch, half_scratch],
        )
        middle_got = core_swap(middle_send)

        def scatter_terms(parts):
            return [parts[0], core_swap(parts[2]), y_swap(add_pair(parts[1], core_swap(parts[3])))]

        def split_x(w, value, keep_ref, send_ref):
            size = keep_ref.shape[0] // Z
            for n in range(Z):
                rows = slice(n * size, (n + 1) * size)
                keep_ref[rows, :] = value[span(n * X + w[AT_X], size), :]
                send_ref[rows, :] = value[span(n * X + 1 - w[AT_X], size), :]

        def z_sum(sent):
            rows, cols = sent.shape[0] // Z, sent.shape[1]
            terms = z_exchange(sent).reshape(Z, rows, cols)
            return jnp.sum(terms.astype(f32), axis=0).astype(bf16)

        dk_got, dv_got = (y_swap(d) for d in (dk_far, dv_far))

        def pack_rest(w, ins, outs, _):
            for n in range(Z):
                for out, at in ((outs[0], w[AT_X]), (outs[1], 1 - w[AT_X])):
                    value = ins[0][n * X + at].astype(f32) + ins[1][n * X + at].astype(f32)
                    out[n * shard : (n + 1) * shard, :] = value.astype(bf16)

        rest_keep, rest_send = stage(
            pack_rest,
            where,
            [after(middle_keep, d_attn[1]), middle_got],
            [((Z * shard, rest_cols), bf16)] * 2,
        )
        rest_got = x_shift(rest_send, 1)

        def self_backward(w, q_ref, k_ref, v_ref, *refs):
            grads, lse_ref = refs[:S], refs[S]
            dq_ref, dk_ref, dv_ref, dk_acc, dv_acc, g_rows = refs[S + 1 :]
            i = pl.program_id(1)

            @pl.when(i == 0)
            def _():
                dk_acc[...] = jnp.zeros_like(dk_acc)
                dv_acc[...] = jnp.zeros_like(dv_acc)
                for n in range(S):
                    g_rows[span(w[SEQ + n], t), :] = grads[n][...]

            def visit(key_count):
                dq_ref[...] = backward_pair(
                    q_ref[...], k_ref, v_ref, g_rows[span(i, rows_2), :], lse_ref, key_count,
                    functools.partial(masked, w, i), dk_acc, dv_acc,
                )

            step_cases(i, visit)

            @pl.when(i == T // rows_2 - 1)
            def _():
                sums_out(dk_ref, dk_acc)
                sums_out(dv_ref, dv_acc)

        key_block = pl.BlockSpec((T, pair), lambda g, i, _: (0, g))
        dq_self, dk_self, dv_self = pl.pallas_call(
            self_backward,
            grid_spec=pltpu.PrefetchScalarGridSpec(
                num_scalar_prefetch=1,
                grid=(pairs, T // rows_2),
                in_specs=[q_block, qkv_spec(1), qkv_spec(2)] + [row_block] * S + [lse_block],
                out_specs=[q_block, key_block, key_block],
                scratch_shapes=acc_scratch + [pltpu.VMEM((T, pair), bf16)],
            ),
            out_shape=[jax.ShapeDtypeStruct((T, hw), bf16)] * 3,
            compiler_params=pltpu.CompilerParams(vmem_limit_bytes=vmem_limit),
            cost_estimate=short,
        )(where, qkv, qkv, qkv, *d_attn, after(self_lse, rest_keep))

        tall = shard + 16

        def place_small(small_sums, value):
            for n in range(F):
                lanes = slice(n * shard, (n + 1) * shard)
                at = n * tall + shard
                value[at : at + 16, 0:shard] = small_sums[0:16, lanes].astype(bf16)
                rest_rows = [small_sums[16:, lanes], jnp.zeros((32 - small_rows, shard), f32)]
                value[at : at + 16, shard : 2 * shard] = jnp.concatenate(
                    rest_rows, axis=0
                ).astype(bf16)

        def last_grads(w, ins, outs, scratch):
            dq, dk, dv, one, two, three, ffn = ins[:7]
            mem_refs = ins[7:11]
            blocks, mem_blocks = ins[11 : 11 + S], ins[11 + S :]
            keep_ref, send_ref, d_all = outs
            x_all, m_all, value, small_sums, sems = scratch
            copies = Copies(sems)
            for n in range(S):
                copies.add(blocks[n], x_all.at[span(w[SEQ + n], t)])
            for n in range(S):
                copies.add(mem_blocks[n], m_all.at[pl.ds(n * t, t)])
            for m in range(2):
                near, far = mem_refs[m], mem_refs[2 + m]
                for n in range(S):
                    rows = slice(n * t, (n + 1) * t)
                    total = near[rows, :].astype(f32) + far[rows, :].astype(f32)
                    d_all[rows, m * hw : (m + 1) * hw] = total.astype(bf16)
            copies.wait()

            def store(grad, cols):
                for n in range(F):
                    value[n * tall : n * tall + shard, cols] = grad[n * shard : (n + 1) * shard]

            for m, d in enumerate((dq, dk, dv)):
                grad = dot(x_all[...], d[...], tn).astype(bf16)
                store(grad, slice(m * hw, (m + 1) * hw))
            grad = dot(m_all[...], d_all[...], tn).astype(bf16)
            store(grad, slice(3 * hw, 5 * hw))
            small_sums[...] = jnp.zeros_like(small_sums)
            mine = span(w[MINE], hw)
            small_sums[0:1, mine] = row_sum(dq[...])
            small_sums[1:2, mine] = row_sum(dv[...])
            small_sums[4:5, mine] = row_sum(d_all[:, hw:])
            rows = [
                (2, one, 0), (3, one, 3), (5, two, 0), (6, three, 0), (7, one, 1), (8, two, 1),
                (9, three, 1), (10, one, 2), (11, two, 2), (12, three, 2),
            ]
            for at, ref, row in rows:
                small_sums[at : at + 1, :] = ref[row : row + 1, :]
            small_sums[pl.ds(13 + w[MINE], 1), :] = ffn[0:1, :]
            place_small(small_sums, value)
            split_x(w, value, keep_ref, send_ref)

        last_keep, last_send, d_mem = stage(
            last_grads,
            where,
            [dq_self, dk_self, dv_self, sums_one, sums_two, sums_three, sums_ffn]
            + [dk_own, dv_own, dk_got, dv_got]
            + [hbm(b) for b in x_blocks + m_blocks],
            [((Z * tall, 5 * hw), bf16)] * 2 + [((T, 2 * hw), bf16)],
            [
                pltpu.VMEM((T, D), bf16),
                pltpu.VMEM((T, D), bf16),
                pltpu.VMEM((F * tall, 5 * hw), bf16),
                pltpu.VMEM((small_rows, D), f32),
                pltpu.SemaphoreType.DMA((2 * S,)),
            ],
        )
        last_got = x_shift(last_send, 1)
        rest_sent = add_pair(rest_keep, after(rest_got, last_keep))

        def memory_parts(w, ins, outs, _):
            d_ref, weight = ins
            for n in (3, 2, 1, 0):
                value = dot(d_ref[n * t : (n + 1) * t, :], weight[...], nt)
                outs[n][...] = value.astype(bf16)

        mem_parts = stage(
            memory_parts, where, [after(d_mem, rest_sent), w_mem], [((t, D), bf16)] * S
        )

        def input_parts(w, ins, outs, scratch):
            grads, pieces = ins[:3], ins[3:]
            weight, sems = scratch
            copies = Copies(sems)
            for k in range(2):
                at = w[AT_X] if k == 0 else 1 - w[AT_X]
                copies.add(pieces[k].at[:, pl.ds(0, shard)], weight.at[:, at])
            copies.wait()
            for n in (3, 2, 1, 0):
                rows = span(w[SEQ + n], t)
                value = None
                for m in range(3):
                    part_of = weight[..., m * hw : (m + 1) * hw].reshape(D, hw)
                    term = dot(grads[m][rows, :], part_of, nt)
                    value = term if value is None else value + term
                outs[n][...] = value.astype(bf16)

        in_parts = stage(
            input_parts,
            where,
            [after(dq_self, last_got), dk_self, dv_self] + [hbm(p) for p in got_qkv],
            [((t, D), bf16)] * S,
            [pltpu.VMEM((Z, X, shard, 3 * hw), bf16), pltpu.SemaphoreType.DMA((2,))],
        )
        in_terms = scatter_terms(in_parts)
        memory_grad = sum(term.astype(f32) for term in scatter_terms(mem_parts)).astype(bf16)
        input_grad = (
            alpha_scale * d_one + sum(term.astype(f32) for term in in_terms)
        ).astype(bf16)


        def finish_ffn(w, ins, outs, _):
            for n in range(S):
                for m in range(F):
                    lanes = pl.ds(pl.multiple_of(m * S * fw + w[SEQ + n] * fw, fw), fw)
                    outs[0][:, lanes] = ins[n][0:shard, m * fw : (m + 1) * fw].astype(f32)
                outs[1][span(w[SEQ + n], fw), :] = ins[n][shard:, :].astype(f32)

        grad_fin, grad_fout = stage(
            finish_ffn,
            where,
            seq_gather(after(own_ffn, last_keep)),
            [((shard, FF), f32), ((S * fw, D), f32)],
        )

        own_rest = z_sum(rest_sent)
        last_sent = add_pair(
            last_keep, after(last_got, own_rest, grad_fin, memory_grad)
        )
        own_last = z_sum(last_sent)

        def sum_chips(w, ins, outs, _):
            near, away = ins
            out = outs[0]
            out[:, 0:D] = (near[:, 0:D].astype(f32) + away[:, 0:D].astype(f32)).astype(bf16)
            for k in range(2):
                mine = slice(D + k * hw, D + (k + 1) * hw)
                theirs = slice(D + (1 - k) * hw, D + (2 - k) * hw)
                out[:, mine] = (near[:, mine].astype(f32) + away[:, theirs].astype(f32)).astype(bf16)

        (rest_sum,) = stage(
            sum_chips, where, [own_rest, y_swap(own_rest)], [((shard, rest_cols), bf16)]
        )

        def finish_rest(w, ins, outs, _):
            query, own, cross = outs
            core = lax.rem(w[MINE], 2)
            for e in range(2):
                rows = span(core if e == 0 else 1 - core, deep)
                own[rows, :] = ins[e][0:deep, 0:D].astype(f32)
                cross[rows, :] = ins[e][deep:, 0:D].astype(f32)
                for k in range(2):
                    query[:, span(w[SEQ + 2 * e + k], hw)] = ins[e][
                        :, D + k * hw : D + (k + 1) * hw
                    ].astype(f32)

        grad_query, grad_self_out, grad_cross_out = stage(
            finish_rest, where, [rest_sum, core_swap(rest_sum)], [((shard, D), f32)] * 3
        )

        def finish_last(w, ins, outs, _):
            for n in range(S):
                group = w[SEQ + n] * hw
                for m in range(5):
                    target, at = (outs[0], m) if m < 3 else (outs[1], m - 3)
                    lanes = pl.ds(pl.multiple_of(at * D + group, hw), hw)
                    target[:, lanes] = ins[n][0:shard, m * hw : (m + 1) * hw].astype(f32)
            total = sum(ins[n][shard:, 0:shard].astype(f32) for n in range(S))
            below = sum(ins[n][shard : shard + 8, shard : 2 * shard].astype(f32) for n in range(S))
            for n in range(7):
                outs[2 + n][...] = total[n : n + 1, :].reshape(shard)
            outs[9][...] = total[7:10, :]
            outs[10][...] = total[10:13, :]
            for n in range(S):
                row = total[13 + n : 14 + n, :] if n < 3 else below[n - 3 : n - 2, :]
                outs[11][n * fw : (n + 1) * fw] = row.reshape(fw)

        grad_self_in, grad_memory, *rows, grad_gain, grad_shift, grad_fin_bias = stage(
            finish_last,
            where,
            seq_gather(own_last),
            [((shard, 3 * D), f32), ((shard, 2 * D), f32)]
            + [((shard,), f32)] * 7
            + [((3, shard), f32)] * 2
            + [((S * fw,), f32)],
        )

        return (
            layer_out[None],
            input_grad[None],
            memory_grad[None],
            grad_self_in,
            rows[0],
            rows[1],
            grad_self_out,
            rows[2],
            grad_query,
            rows[3],
            grad_memory,
            rows[4],
            grad_cross_out,
            rows[5],
            grad_fin,
            grad_fin_bias,
            grad_fout,
            rows[6],
            grad_gain,
            grad_shift,
        )

    return local


def solution(mesh):
    general, tiled = general_layer(mesh), tiled_layer(mesh)
    S, F = mesh.shape["seq"], mesh.shape["fsdp"]

    def local(*args):
        _, t, D = args[0].shape
        FF = args[15].shape[1]
        blocks = (D // F, D // S, FF // (F * S))
        whole_tiles = all(n % 128 == 0 for n in blocks) and D // F // 2 % 16 == 0
        if whole_tiles and S == 4 and F == 8 and t == BLK:
            return tiled(*args)
        return general(*args)

    by_row, rows_1d = P("fsdp", None), P("fsdp")
    tokens, norms = P("fsdp", "seq", None), P(None, "fsdp")
    in_specs = (
        tokens, tokens, rows_1d, tokens, by_row, rows_1d, rows_1d, by_row, rows_1d, by_row, rows_1d,
        by_row, rows_1d, by_row, rows_1d, by_row, rows_1d, by_row, rows_1d, norms, norms,
    )
    out_specs = (
        tokens, tokens, tokens, by_row, rows_1d, rows_1d, by_row, rows_1d, by_row, rows_1d, by_row,
        rows_1d, by_row, rows_1d, by_row, rows_1d, by_row, rows_1d, norms, norms,
    )
    return jax.shard_map(local, mesh=mesh, in_specs=in_specs, out_specs=out_specs, check_vma=False)
```
